32 devices in a mesh: replica: 4 (over y, x), fsdp: 4 (over z), tensor: 2 (over core).
Axes of the slice: x: 2, y: 2, z: 4, core: 2. Of those that a mesh axis runs over, the one named last changes fastest.
Arguments:
- tokens: bfloat16 [4, 16, 4096], P('replica', ('fsdp', 'tensor')), may hold values from -6 to 6
- d_out: bfloat16 [4, 16, 4096], P('replica', ('fsdp', 'tensor')), may hold values from -6 to 6
- w_gate: bfloat16 [4096, 15360], P(None, ('fsdp', 'tensor')), may hold values from -0.09375 to 0.09375
- w_up: bfloat16 [4096, 15360], P(None, ('fsdp', 'tensor')), may hold values from -0.09375 to 0.09375
- w_down: bfloat16 [15360, 4096], P(('fsdp', 'tensor')), may hold values from -0.046875 to 0.046875
- failed: int32 [8], P(('fsdp', 'tensor')), may hold values from 0 to 3
- master: float32 [2, 15360, 4096], P(None, ('fsdp', 'tensor'), 'replica'), may hold values from -6 to 6
- moment1: float32 [2, 15360, 4096], P(None, ('fsdp', 'tensor'), 'replica'), may hold values from -4 to 4
- moment2: float32 [2, 15360, 4096], P(None, ('fsdp', 'tensor'), 'replica'), may hold values from 0.1 to 1
Outputs:
- d_tokens: bfloat16 [4, 16, 4096], P('replica', ('fsdp', 'tensor'))
- master_new: float32 [15360, 4096], P(('fsdp', 'tensor'), 'replica')
- moment1_new: float32 [15360, 4096], P(('fsdp', 'tensor'), 'replica')
- moment2_new: float32 [15360, 4096], P(('fsdp', 'tensor'), 'replica')
The draws below stay inside these ranges and needn't reach their ends.
All inputs are finite; a program needn't handle non-finite values.
Results may differ from the reference program's by a relative error of at most 0.0049.
Values may be sent and summed in bfloat16 or wider, within the bound.
No kernel may reach another device: no remote copies, remote signals or barrier semaphores. Data moves between devices by JAX's collectives and lax.ppermute only.
A program may use at most 256 MiB of HBM per device.

```python
import math
import jax
import jax.numpy as jnp
from jax import lax

D = 4096
FF = 15360
TOK = 16
SHARDS = 8
N_REPLICA = 4
N_FSDP = 4
N_TENSOR = 2


def touch_ends(result, stream_key, low, largest):
    place = [jax.random.randint(jax.random.fold_in(stream_key, axis), (), 0, length) for axis, length in enumerate(result.shape)]
    widest = result.shape.index(max(result.shape))
    next_to = place[:widest] + [(place[widest] + 1) % result.shape[widest]] + place[widest + 1:]
    return result.at[tuple(place)].set(low).at[tuple(next_to)].set(largest)


def levels(rng, dims, split, smallest, largest):
    level = 1.0
    for position, shards_of in split:
        steps = jax.random.uniform(jax.random.fold_in(jax.random.fold_in(rng, 6), position), (shards_of,), jnp.float32, smallest / len(split), largest / len(split))
        level = level * jnp.repeat(jnp.exp(steps), dims[position] // shards_of).reshape((-1,) + (1,) * (len(dims) - 1 - position))
    return level


def bell_draw(key, shape, width, most, shards=(), held_as=jnp.bfloat16):
    drawn = jax.random.normal(key, shape, jnp.float32) * width
    if len(shards) > 0:
        drawn = levels(key, shape, shards, -0.22, 0.18) * drawn
    return jnp.clip(drawn, min=-most, max=most).astype(held_as)


def setup_inputs(seed: int = 0) -> dict:
    key_list = jax.random.split(jax.random.key(seed), 10)
    return {
        "tokens": bell_draw(key_list[0], (N_REPLICA, TOK, D), 1.0, 6.0, ((0, 4), (1, 8))),
        "d_out": bell_draw(key_list[1], (N_REPLICA, TOK, D), 1.0, 6.0, ((0, 4), (1, 8))),
        "w_gate": bell_draw(key_list[2], (D, FF), D ** -0.5, 0.09375, ((1, 8),)),
        "w_up": bell_draw(key_list[3], (D, FF), D ** -0.5, 0.09375, ((1, 8),)),
        "w_down": bell_draw(key_list[4], (FF, D), FF ** -0.5, 0.046875, ((0, 8),)),
        "failed": touch_ends(jax.random.randint(key_list[5], (SHARDS,), 0, N_REPLICA), jax.random.fold_in(key_list[5], 1), 0, N_REPLICA - 1).astype(jnp.int32),
        "master": bell_draw(key_list[6], (2, FF, D), 1.0, 6.0, ((1, 8), (2, 4)), jnp.float32),
        "moment1": bell_draw(key_list[7], (2, FF, D), 0.5, 4.0, ((1, 8), (2, 4)), jnp.float32),
        "moment2": jnp.clip(jnp.exp(math.log(1.0) - 2.3025851 * jax.random.uniform(key_list[8], (2, FF, D), jnp.float32) ** levels(key_list[8], (2, FF, D), ((1, 8), (2, 4)), -0.2, 0.2)), 0.1, 1.0),
    }


def replica_pass(w_gate, w_up, w_down, rows, grads_out):
    gate = jnp.dot(rows, w_gate, preferred_element_type=jnp.float32)
    up = jnp.dot(rows, w_up, preferred_element_type=jnp.float32)
    sig = 1.0 / (1.0 + jnp.exp(-gate))
    hidden = (gate * sig * up).astype(jnp.bfloat16)
    d_hidden = jnp.dot(grads_out, w_down.T, preferred_element_type=jnp.float32)
    d_gate = (d_hidden * up * sig * (1.0 + gate * (1.0 - sig))).astype(jnp.bfloat16)
    d_up = (d_hidden * gate * sig).astype(jnp.bfloat16)
    d_rows = jnp.dot(d_gate, w_gate.T, preferred_element_type=jnp.float32) + jnp.dot(d_up, w_up.T, preferred_element_type=jnp.float32)
    grad_down = jnp.dot(hidden.T, grads_out, preferred_element_type=jnp.float32)
    return (d_rows.astype(jnp.bfloat16), grad_down)

def recover(stack, failed_rows):
    primary = stack[0].reshape(FF, N_REPLICA, D // N_REPLICA)
    backup = stack[1].reshape(FF, N_REPLICA, D // N_REPLICA)
    rolled = jnp.roll(backup, -1, axis=1)
    select = (jnp.arange(N_REPLICA, dtype=jnp.int32)[None, :] == failed_rows[:, None])[:, :, None]
    return jnp.where(select, rolled, primary).reshape(FF, D)

def reference(tokens, d_out, w_gate, w_up, w_down, failed, master, moment1, moment2):
    failed_rows = jnp.repeat(failed, FF // (N_FSDP * N_TENSOR)).astype(jnp.int32)

    def step(total, inputs):
        rows, grads_out, index = inputs
        d_rows, grad_down = replica_pass(w_gate, w_up, w_down, rows, grads_out)
        keep = (failed_rows != index).astype(jnp.float32)[:, None]
        return (total + keep * grad_down, d_rows)
    total, d_tokens = lax.scan(step, jnp.zeros((FF, D), jnp.float32), (tokens, d_out, jnp.arange(N_REPLICA, dtype=jnp.int32)))
    grad = total / (N_REPLICA - 1.0)
    master_old = recover(master, failed_rows)
    first_old = recover(moment1, failed_rows)
    second_old = recover(moment2, failed_rows)
    first_new = 0.9 * first_old + 0.1 * grad
    second_new = 0.95 * second_old + 0.05 * grad * grad
    master_new = master_old - 0.01 * first_new / (jnp.sqrt(second_new) + 1e-08)
    return (d_tokens, master_new, first_new, second_new)
```

```python
import functools

import jax
import jax.numpy as jnp
from jax import lax
from jax.experimental import pallas as pl
from jax.experimental.pallas import tpu as pltpu
from jax.sharding import PartitionSpec as P

BF16, F32 = jnp.bfloat16, jnp.float32
LAG = 2
MOST_CHUNKS = 20
TILE = 16
VMEM = 48 << 20


def ring_order(n):
    return [0, 1, 3, 2] if n == 4 else list(range(n))


def largest(options, default):
    options = list(options)
    return max(options) if options else default


def updated(first_old, second_old, master_old, grad):
    first_new = 0.9 * first_old + 0.1 * grad
    second_new = 0.95 * second_old + 0.05 * grad * grad
    master_new = master_old - 0.01 * first_new / (jnp.sqrt(second_new) + 1e-08)
    return master_new, first_new, second_new


def pack_body(flag, *refs):
    ahead, behind = refs[0:3], refs[3:6]
    sends = refs[-2:]
    got = refs[6:-2]
    for own, send, seen in zip((ahead, behind), sends, got or (None, None)):
        if seen is None:
            for k in range(3):
                send[k] = own[k][0].astype(BF16)
        else:

            @pl.when(flag[0] == 1)
            def _(own=own, send=send):
                for k in range(3):
                    send[k] = own[k][0].astype(BF16)

            @pl.when(flag[0] == 0)
            def _(send=send, seen=seen):
                send[...] = seen[...]


def pack(is_source, state, got, chunk_ahead, chunk_behind, chunk):
    width = state[0].shape[2]
    half = chunk // 2 if chunk % (2 * TILE) == 0 else chunk
    pieces = chunk // half

    def own(index):
        return pl.BlockSpec((1, half, width), lambda i, s: (1, index * pieces + i, 0))

    moved = pl.BlockSpec((3, half, width), lambda i, s: (0, i, 0))
    shape = jax.ShapeDtypeStruct((3, chunk, width), BF16)
    return pl.pallas_call(
        pack_body,
        grid_spec=pltpu.PrefetchScalarGridSpec(
            num_scalar_prefetch=1,
            grid=(pieces,),
            in_specs=[own(chunk_ahead)] * 3 + [own(chunk_behind)] * 3 + [moved] * len(got),
            out_specs=[moved, moved],
        ),
        out_shape=[shape, shape],
        compiler_params=pltpu.CompilerParams(vmem_limit_bytes=VMEM),
        cost_estimate=pl.CostEstimate(
            flops=0, bytes_accessed=2 * 3 * chunk * width * 8, transcendentals=0
        ),
        name="pack",
    )(is_source, *state, *state, *got)


def update_body(hid_ref, out_ref, m_ref, a_ref, b_ref, m_new, a_new, b_new, *, scale):
    grad = jnp.dot(hid_ref[...], out_ref[...], preferred_element_type=F32) * scale
    m_new[...], a_new[...], b_new[...] = updated(a_ref[0], b_ref[0], m_ref[0], grad)


def update(hidden_t, outs, state, scale):
    _, rows, width = state[0].shape
    depth = hidden_t.shape[1]
    block = largest((b for b in range(TILE, 193, TILE) if rows % b == 0), rows)
    spec = pl.BlockSpec((1, block, width), lambda i: (0, i, 0))
    out = pl.BlockSpec((block, width), lambda i: (i, 0))
    shape = jax.ShapeDtypeStruct((rows, width), F32)
    return pl.pallas_call(
        functools.partial(update_body, scale=scale),
        grid=(rows // block,),
        in_specs=[
            pl.BlockSpec((block, depth), lambda i: (i, 0)),
            pl.BlockSpec((depth, width), lambda i: (0, 0)),
            spec,
            spec,
            spec,
        ],
        out_specs=[out] * 3,
        out_shape=[shape] * 3,
        compiler_params=pltpu.CompilerParams(vmem_limit_bytes=VMEM),
        cost_estimate=pl.CostEstimate(
            flops=2 * rows * width * depth,
            bytes_accessed=6 * rows * width * 4,
            transcendentals=2 * rows * width,
        ),
        name="update",
    )(hidden_t, outs, *state)


def patch_body(info, hid_ref, out_ref, *refs, arrivals, chunks, n, scale):
    count = len(arrivals)
    got = refs[:count]
    news = refs[count + 3 : count + 6]
    held, made, in_sem, out_sem = refs[count + 6 :]
    chunk = held.shape[2]
    part = largest((p for p in (16, 32) if chunk % p == 0), chunk)
    ahead = info[1]
    lag_of = {True: LAG * (ahead - 1), False: LAG * (n - ahead - 1)}

    def fetch(j):
        return pltpu.make_async_copy(got[j], held.at[j % 2], in_sem.at[j % 2])

    def first_row(j):
        step, forward = arrivals[j]
        place = step - lag_of[forward]
        if not forward:
            place = chunks - 1 - place
        return pl.multiple_of(jnp.clip(place, 0, chunks - 1) * chunk, TILE)

    def store(j, k):
        return pltpu.make_async_copy(
            made.at[j % 2, k], news[k].at[pl.ds(first_row(j), chunk)], out_sem.at[j % 2, k]
        )

    def valid(j):
        step, forward = arrivals[j]
        return step >= lag_of[forward]

    def finish(j):
        @pl.when(valid(j))
        def _():
            for k in range(3):
                store(j, k).wait()

    @pl.when(info[0] == 1)
    def _():
        fetch(0).start()
        for j in range(count):
            slot = j % 2
            if j + 1 < count:
                fetch(j + 1).start()
            fetch(j).wait()
            if j >= 2:
                finish(j - 2)

            @pl.when(valid(j))
            def _(j=j, slot=slot):
                first = first_row(j)

                @pl.loop(0, chunk // part)
                def _(i):
                    base = pl.multiple_of(i * part, part)
                    here = pl.ds(base, part)
                    units = hid_ref[pl.ds(pl.multiple_of(first + base, TILE), part)]
                    grad = jnp.dot(units, out_ref[...], preferred_element_type=F32) * scale
                    old = [held[slot, k, here].astype(F32) for k in range(3)]
                    new = updated(old[1], old[2], old[0], grad)
                    for k in range(3):
                        made[slot, k, here] = new[k]

                for k in range(3):
                    store(j, k).start()

        for j in range(max(count - 2, 0), count):
            finish(j)


def patch(info, hidden_t, outs, got, arrivals, news, chunks, n, scale):
    rows, width = news[0].shape
    chunk = rows // chunks
    count = len(got)
    any_spec = pl.BlockSpec(memory_space=pl.ANY)
    whole = pl.BlockSpec(memory_space=pltpu.VMEM)
    shape = jax.ShapeDtypeStruct((rows, width), F32)
    return pl.pallas_call(
        functools.partial(patch_body, arrivals=arrivals, chunks=chunks, n=n, scale=scale),
        in_specs=[pl.BlockSpec(memory_space=pltpu.SMEM), whole, whole]
        + [any_spec] * (count + 3),
        out_specs=[any_spec] * 3,
        out_shape=[shape] * 3,
        scratch_shapes=[
            pltpu.VMEM((2, 3, chunk, width), BF16),
            pltpu.VMEM((2, 3, chunk, width), F32),
            pltpu.SemaphoreType.DMA((2,)),
            pltpu.SemaphoreType.DMA((2, 3)),
        ],
        input_output_aliases={3 + count + k: k for k in range(3)},
        compiler_params=pltpu.CompilerParams(vmem_limit_bytes=VMEM),
        cost_estimate=pl.CostEstimate(
            flops=2 * count * chunk * width * hidden_t.shape[1],
            bytes_accessed=count * 3 * chunk * width * 6,
            transcendentals=2 * count * chunk * width,
        ),
        name="patch",
    )(info, hidden_t, outs, *got, *news)


def halved(x, axis, dim):
    size = lax.axis_size(axis)
    me = lax.axis_index(axis)
    if size & (size - 1):
        return lax.psum_scatter(x, axis, scatter_dimension=dim, tiled=True)
    while size > 1:
        half = size // 2
        length = x.shape[dim] // 2
        bit = (me // half) % 2
        kept = lax.dynamic_slice_in_dim(x, bit * length, length, dim)
        sent = lax.dynamic_slice_in_dim(x, (1 - bit) * length, length, dim)
        route = [(i, i ^ half) for i in range(lax.axis_size(axis))]
        x = kept + lax.ppermute(sent, axis, route)
        size = half
    return x


def per_device(tokens, d_out, w_gate, w_up, w_down, failed, master, moment1, moment2):
    n = lax.axis_size("replica")
    me = lax.axis_index("replica")
    fsdp, tensor = lax.axis_size("fsdp"), lax.axis_size("tensor")
    _, rows, width = master.shape
    scale = 1.0 / (n - 1.0)

    failed_id = failed[0]
    source = (failed_id + 1) % n
    order = ring_order(n)
    place = jnp.array([order.index(i) for i in range(n)], jnp.int32)
    ahead = (place[failed_id] - place[source]) % n
    is_source = (me == source).astype(jnp.int32)[None]
    info = jnp.stack([(me == failed_id).astype(jnp.int32), ahead.astype(jnp.int32)])

    state = (master, moment1, moment2)
    chunks = largest(
        (c for c in range(2, MOST_CHUNKS + 1, 2) if rows % (TILE * c) == 0), 2
    )
    chunk = rows // chunks
    steps = (chunks + LAG * (n - 2)) // 2
    forward = [(order[p], order[(p + 1) % n]) for p in range(n)]
    backward = [(b, a) for a, b in forward]
    got = []
    for step in range(steps):
        seen = got[step - LAG] if step >= LAG else ()
        here = min(step, chunks - 1)
        sends = pack(is_source, state, seen, here, chunks - 1 - here, chunk)
        got.append(
            (
                lax.ppermute(sends[0], "replica", forward),
                lax.ppermute(sends[1], "replica", backward),
            )
        )

    both = jnp.concatenate([tokens[0], d_out[0]], axis=1)
    both = lax.all_gather(both, ("fsdp", "tensor"), axis=0, tiled=True)
    features = tokens.shape[2]
    x, dy = both[:, :features], both[:, features:]
    gate = jnp.dot(x, w_gate, preferred_element_type=F32)
    up = jnp.dot(x, w_up, preferred_element_type=F32)
    sig = 1.0 / (1.0 + jnp.exp(-gate))
    hidden = (gate * sig * up).astype(BF16)
    d_hidden = lax.dot_general(dy, w_down, (((1,), (1,)), ((), ())), preferred_element_type=F32)
    d_gate = (d_hidden * up * sig * (1.0 + gate * (1.0 - sig))).astype(BF16)
    d_up = (d_hidden * gate * sig).astype(BF16)
    d_rows = lax.dot_general(
        d_gate, w_gate, (((1,), (1,)), ((), ())), preferred_element_type=F32
    ) + lax.dot_general(d_up, w_up, (((1,), (1,)), ((), ())), preferred_element_type=F32)

    kept = jnp.where(me == failed_id, jnp.zeros_like(hidden), hidden)

    def parcel(to):
        slab = lax.dynamic_slice_in_dim(dy, to * width, width, 1)
        return jnp.concatenate([kept, slab], axis=1)

    parcels = [parcel(me)]
    for far in range(1, n):
        route = [(i, (i + far) % n) for i in range(n)]
        parcels.append(lax.ppermute(parcel((me + far) % n), "replica", route))
    parcels = jnp.concatenate(parcels, axis=0)
    hidden_t = parcels[:, :rows].T
    outs = parcels[:, rows:]

    d_rows = d_rows.reshape(fsdp, tensor, -1, features)
    d_rows = halved(halved(d_rows, "tensor", 1), "fsdp", 0)
    d_tokens = d_rows.reshape(1, -1, features).astype(BF16)

    news = update(hidden_t, outs, state, scale)
    for group in (range(steps - 1), range(steps - 1, steps)):
        arrivals = [(step, way) for step in group for way in (True, False)]
        blocks = [block for step in group for block in got[step]]
        news = patch(info, hidden_t, outs, blocks, arrivals, news, chunks, n, scale)
    return (d_tokens, *news)


def solution(mesh):
    placed = (
        P("replica", ("fsdp", "tensor"), None),
        P("replica", ("fsdp", "tensor"), None),
        P(None, ("fsdp", "tensor")),
        P(None, ("fsdp", "tensor")),
        P(("fsdp", "tensor"), None),
        P(("fsdp", "tensor")),
        P(None, ("fsdp", "tensor"), "replica"),
        P(None, ("fsdp", "tensor"), "replica"),
        P(None, ("fsdp", "tensor"), "replica"),
    )
    return jax.shard_map(
        per_device,
        mesh=mesh,
        in_specs=placed,
        out_specs=(
            P("replica", ("fsdp", "tensor"), None),
            P(("fsdp", "tensor"), "replica"),
            P(("fsdp", "tensor"), "replica"),
            P(("fsdp", "tensor"), "replica"),
        ),
        check_vma=False,
    )
```

```python
import functools

import jax
import jax.numpy as jnp
from jax import lax
from jax.experimental import pallas as pl
from jax.experimental.pallas import tpu as pltpu
from jax.sharding import PartitionSpec as P

BF16, F32 = jnp.bfloat16, jnp.float32
LAG = 2
MOST_CHUNKS = 20
TILE = 16
VMEM = 48 << 20

ANY = pl.BlockSpec(memory_space=pl.ANY)
SMEM = pl.BlockSpec(memory_space=pltpu.SMEM)
WHOLE = pl.BlockSpec(memory_space=pltpu.VMEM)
PARAMS = pltpu.CompilerParams(vmem_limit_bytes=VMEM)


def ring_order(n):
    return [0, 1, 3, 2] if n == 4 else list(range(n))


def largest(options, default):
    options = list(options)
    return max(options) if options else default


def cost(flops, bytes_accessed, transcendentals=0):
    return pl.CostEstimate(
        flops=flops, bytes_accessed=bytes_accessed, transcendentals=transcendentals
    )


def updated(master_old, first_old, second_old, total, healthy):
    first_new = 0.9 * first_old + (0.1 / healthy) * total
    second_new = 0.95 * second_old + (0.05 / healthy**2) * (total * total)
    root = second_new * lax.rsqrt(second_new)
    step = first_new * pl.reciprocal(root + 1e-08)
    return master_old - 0.01 * step, first_new, second_new


def pack_body(flag, *refs, places, chunk, count_seen, count_after):
    state = refs[0:3]
    seen = refs[3 : 3 + count_seen]
    rest = refs[3 + count_seen + count_after :]
    sends = rest[:2]
    held, made, in_sem, out_sem = rest[2:]

    def fetch(j):
        way, k = divmod(j, 3)
        rows = pl.ds(places[way] * chunk, chunk)
        return pltpu.make_async_copy(state[k].at[1, rows], held.at[j], in_sem.at[j])

    def store(j):
        way, k = divmod(j, 3)
        return pltpu.make_async_copy(made.at[j], sends[way].at[k], out_sem.at[j])

    def convert():
        for j in range(6):
            fetch(j).start()
        for j in range(6):
            fetch(j).wait()
            made[j] = held[j].astype(BF16)
            store(j).start()
        for j in range(6):
            store(j).wait()

    def relay(way):
        return pltpu.make_async_copy(seen[way], sends[way], out_sem.at[way])

    if not seen:
        convert()
        return
    pl.when(flag[0] == 1)(convert)

    @pl.when(flag[0] == 0)
    def _():
        for way in range(2):
            relay(way).start()
        for way in range(2):
            relay(way).wait()


def pack(is_source, state, seen, after, places, chunk):
    width = state[0].shape[2]
    shape = jax.ShapeDtypeStruct((3, chunk, width), BF16)
    return pl.pallas_call(
        functools.partial(
            pack_body,
            places=places,
            chunk=chunk,
            count_seen=len(seen),
            count_after=len(after),
        ),
        in_specs=[SMEM] + [ANY] * (3 + len(seen) + len(after)),
        out_specs=[ANY, ANY],
        out_shape=[shape, shape],
        scratch_shapes=[
            pltpu.VMEM((6, chunk, width), F32),
            pltpu.VMEM((6, chunk, width), BF16),
            pltpu.SemaphoreType.DMA((6,)),
            pltpu.SemaphoreType.DMA((6,)),
        ],
        compiler_params=PARAMS,
        cost_estimate=cost(0, 2 * 3 * chunk * width * 6),
        name="pack",
    )(is_source, *state, *seen, *after)


def beside_body(*refs):
    tokens, d_out, out = refs[0], refs[1], refs[-1]
    width = tokens.shape[1]
    out[:, :width] = tokens[...]
    out[:, width:] = d_out[...]


def beside(tokens, d_out, after):
    rows, width = tokens.shape
    return pl.pallas_call(
        beside_body,
        in_specs=[WHOLE, WHOLE] + [ANY] * len(after),
        out_specs=WHOLE,
        out_shape=jax.ShapeDtypeStruct((rows, 2 * width), tokens.dtype),
        compiler_params=PARAMS,
        cost_estimate=cost(0, 4 * rows * width * 2),
        name="beside",
    )(tokens, d_out, *after)


def by_rows(a, b):
    return lax.dot_general(a, b, (((1,), (1,)), ((), ())), preferred_element_type=F32)


def layer_body(both, gate_ref, up_ref, down_ref, *refs, resumed):
    hidden_ref, sum_ref = refs[-2:]
    features = gate_ref.shape[0]
    tile = gate_ref.shape[1]
    x, dy = both[:, :features], both[:, features:]
    w_gate, w_up = gate_ref[...], up_ref[...]
    joined = tile % 128 == 0
    if joined:
        w_both = jnp.concatenate([w_gate, w_up], axis=1)
        gate_up = jnp.dot(x, w_both, preferred_element_type=F32)
        gate, up = gate_up[:, :tile], gate_up[:, tile:]
    else:
        gate = jnp.dot(x, w_gate, preferred_element_type=F32)
        up = jnp.dot(x, w_up, preferred_element_type=F32)
    d_hidden = by_rows(dy, down_ref[...])
    sig = 1.0 / (1.0 + jnp.exp(-gate))
    hidden_ref[...] = (gate * sig * up).astype(BF16)
    d_gate = (d_hidden * up * sig * (1.0 + gate * (1.0 - sig))).astype(BF16)
    d_up = (d_hidden * gate * sig).astype(BF16)
    if joined:
        term = by_rows(jnp.concatenate([d_gate, d_up], axis=1), w_both)
    else:
        term = by_rows(d_gate, w_gate) + by_rows(d_up, w_up)

    @pl.when(pl.program_id(0) == 0)
    def _():
        sum_ref[...] = (refs[0][...] + term) if resumed else term

    @pl.when(pl.program_id(0) > 0)
    def _():
        sum_ref[...] += term


def layer(both, w_gate, w_up, w_down, partial_sum, after, tile, first, count):
    rows = both.shape[0]
    features = w_gate.shape[0]
    across = pl.BlockSpec((features, tile), lambda i: (0, first + i))
    resumed = partial_sum is not None
    fixed = pl.BlockSpec((rows, features), lambda i: (0, 0))
    return pl.pallas_call(
        functools.partial(layer_body, resumed=resumed),
        grid=(count,),
        in_specs=[
            pl.BlockSpec(both.shape, lambda i: (0, 0)),
            across,
            across,
            pl.BlockSpec((tile, features), lambda i: (first + i, 0)),
        ]
        + [fixed] * resumed
        + [ANY] * len(after),
        out_specs=[pl.BlockSpec((rows, tile), lambda i: (0, i)), fixed],
        out_shape=[
            jax.ShapeDtypeStruct((rows, count * tile), BF16),
            jax.ShapeDtypeStruct((rows, features), F32),
        ],
        compiler_params=PARAMS,
        cost_estimate=cost(
            10 * rows * features * count * tile,
            3 * features * count * tile * 2,
            rows * count * tile,
        ),
        name="layer",
    )(both, w_gate, w_up, w_down, *([partial_sum] if resumed else []), *after)


def halve_body(bit, *refs, arrived, final):
    value = refs[0][...]
    if arrived:
        value = value + refs[1][...]
    if final:
        refs[-1][...] = value.astype(BF16)
        return
    kept, sent = refs[-2:]
    half = value.shape[0] // 2
    low, high = value[:half], value[half:]
    upper = bit[0] == 1
    kept[...] = jnp.where(upper, high, low)
    sent[...] = jnp.where(upper, low, high)


def halve(bit, value, arrived, after, final):
    rows, features = value.shape
    if final:
        out_shape = jax.ShapeDtypeStruct((rows, features), BF16)
    else:
        out_shape = [jax.ShapeDtypeStruct((rows // 2, features), F32)] * 2
    return pl.pallas_call(
        functools.partial(halve_body, arrived=bool(arrived), final=final),
        in_specs=[SMEM] + [WHOLE] * (1 + len(arrived)) + [ANY] * len(after),
        out_specs=WHOLE if final else [WHOLE, WHOLE],
        out_shape=out_shape,
        compiler_params=PARAMS,
        cost_estimate=cost(0, 3 * rows * features * 4),
        name="halve",
    )(bit, value, *arrived, *after)


def sum_scattered(value, axes, afters):
    sizes = [lax.axis_size(axis) for axis in axes]
    if any(size & (size - 1) for size in sizes):
        return lax.psum_scatter(value, axes, scatter_dimension=0, tiled=True).astype(BF16)
    arrived = ()
    level = 0
    for axis, size in zip(axes, sizes):
        me = lax.axis_index(axis)
        apart = size // 2
        while apart:
            bit = ((me // apart) % 2).astype(jnp.int32)[None]
            after = afters[min(level, len(afters) - 1)]
            value, sent = halve(bit, value, arrived, after, False)
            route = [(i, i ^ apart) for i in range(size)]
            arrived = (lax.ppermute(sent, axis, route),)
            apart //= 2
            level += 1
    after = afters[min(level, len(afters) - 1)]
    return halve(jnp.zeros((1,), jnp.int32), value, arrived, after, True)


def collect_body(*refs, count, units):
    hidden_t, outs = refs[-2:]
    rows = refs[0].shape[0]
    for j in range(count):
        outs[pl.ds(j * rows, rows)] = refs[j][:, units:]
    hidden = jnp.concatenate([refs[j][:, :units] for j in range(count)], axis=0)
    hidden_t[...] = hidden.astype(F32).T.astype(BF16)


def collect(parcels, units, after):
    rows, length = parcels[0].shape
    depth = rows * len(parcels)
    return pl.pallas_call(
        functools.partial(collect_body, count=len(parcels), units=units),
        in_specs=[WHOLE] * len(parcels) + [ANY] * len(after),
        out_specs=[WHOLE, WHOLE],
        out_shape=[
            jax.ShapeDtypeStruct((units, depth), BF16),
            jax.ShapeDtypeStruct((depth, length - units), BF16),
        ],
        compiler_params=PARAMS,
        cost_estimate=cost(0, 4 * depth * length),
        name="collect",
    )(*parcels, *after)


def update_body(info, hid_ref, out_ref, m_ref, a_ref, b_ref, *refs, healthy):
    m_new, a_new, b_new = refs[-3:]

    @pl.when(info[0] == 0)
    def _():
        total = jnp.dot(hid_ref[...], out_ref[...], preferred_element_type=F32)
        m_new[...], a_new[...], b_new[...] = updated(
            m_ref[0], a_ref[0], b_ref[0], total, healthy
        )


def update(info, hidden_t, outs, state, news, after, healthy, block, first, count):
    _, rows, width = state[0].shape
    depth = hidden_t.shape[1]

    def at(i, info):
        return jnp.where(info[0] == 1, first, first + i)

    spec = pl.BlockSpec((1, block, width), lambda i, info: (0, at(i, info), 0))
    out = pl.BlockSpec((block, width), lambda i, info: (at(i, info), 0))
    shape = jax.ShapeDtypeStruct((rows, width), F32)
    return pl.pallas_call(
        functools.partial(update_body, healthy=healthy),
        grid_spec=pltpu.PrefetchScalarGridSpec(
            num_scalar_prefetch=1,
            grid=(count,),
            in_specs=[
                pl.BlockSpec((block, depth), lambda i, info: (at(i, info), 0)),
                pl.BlockSpec((depth, width), lambda i, info: (0, 0)),
                spec,
                spec,
                spec,
            ]
            + [ANY] * (len(news) + len(after)),
            out_specs=[out] * 3,
        ),
        out_shape=[shape] * 3,
        input_output_aliases={6 + k: k for k in range(len(news))},
        compiler_params=PARAMS,
        cost_estimate=cost(
            2 * count * block * width * depth,
            6 * count * block * width * 4,
            2 * count * block * width,
        ),
        name="update",
    )(info, hidden_t, outs, *state, *news, *after)


def patch_body(info, hid_ref, out_ref, *refs, arrivals, chunks, n, count_after):
    count = len(arrivals)
    got = refs[:count]
    rest = refs[count + 3 + count_after :]
    news = rest[:3]
    held, made, in_sem, out_sem = rest[3:]
    chunk = held.shape[2]
    part = largest((p for p in (16, 32, 48) if chunk % p == 0), chunk)
    ahead = info[1]
    lag_of = {True: LAG * (ahead - 1), False: LAG * (n - ahead - 1)}

    def fetch(j):
        return pltpu.make_async_copy(got[j], held.at[j % 2], in_sem.at[j % 2])

    def first_row(j):
        step, forward = arrivals[j]
        place = step - lag_of[forward]
        if not forward:
            place = chunks - 1 - place
        return pl.multiple_of(jnp.clip(place, 0, chunks - 1) * chunk, TILE)

    def store(j, k):
        return pltpu.make_async_copy(
            made.at[j % 2, k], news[k].at[pl.ds(first_row(j), chunk)], out_sem.at[j % 2, k]
        )

    def valid(j):
        step, forward = arrivals[j]
        return step >= lag_of[forward]

    def finish(j):
        @pl.when(valid(j))
        def _():
            for k in range(3):
                store(j, k).wait()

    @pl.when(info[0] == 1)
    def _():
        fetch(0).start()
        for j in range(count):
            slot = j % 2
            if j + 1 < count:
                fetch(j + 1).start()
            fetch(j).wait()
            if j >= 2:
                finish(j - 2)

            @pl.when(valid(j))
            def _(j=j, slot=slot):
                first = first_row(j)

                @pl.loop(0, chunk // part)
                def _(i):
                    base = pl.multiple_of(i * part, part)
                    here = pl.ds(base, part)
                    units = hid_ref[pl.ds(pl.multiple_of(first + base, TILE), part)]
                    total = jnp.dot(units, out_ref[...], preferred_element_type=F32)
                    old = [held[slot, k, here].astype(F32) for k in range(3)]
                    new = updated(*old, total, n - 1.0)
                    for k in range(3):
                        made[slot, k, here] = new[k]

                for k in range(3):
                    store(j, k).start()

        for j in range(max(count - 2, 0), count):
            finish(j)


def patch(info, hidden_t, outs, got, arrivals, news, after, chunks, n):
    rows, width = news[0].shape
    chunk = rows // chunks
    count = len(got)
    shape = jax.ShapeDtypeStruct((rows, width), F32)
    return pl.pallas_call(
        functools.partial(
            patch_body, arrivals=arrivals, chunks=chunks, n=n, count_after=len(after)
        ),
        in_specs=[SMEM, WHOLE, WHOLE] + [ANY] * (count + 3 + len(after)),
        out_specs=[ANY] * 3,
        out_shape=[shape] * 3,
        scratch_shapes=[
            pltpu.VMEM((2, 3, chunk, width), BF16),
            pltpu.VMEM((2, 3, chunk, width), F32),
            pltpu.SemaphoreType.DMA((2,)),
            pltpu.SemaphoreType.DMA((2, 3)),
        ],
        input_output_aliases={3 + count + k: k for k in range(3)},
        compiler_params=PARAMS,
        cost_estimate=cost(
            2 * count * chunk * width * hidden_t.shape[1],
            count * 3 * chunk * width * 6,
            2 * count * chunk * width,
        ),
        name="patch",
    )(info, hidden_t, outs, *got, *news, *after)


def per_device(tokens, d_out, w_gate, w_up, w_down, failed, master, moment1, moment2):
    n = lax.axis_size("replica")
    me = lax.axis_index("replica")
    _, rows, width = master.shape
    features, units = w_gate.shape

    failed_id = failed[0]
    source = (failed_id + 1) % n
    order = ring_order(n)
    place = jnp.array([order.index(i) for i in range(n)], jnp.int32)
    ahead = (place[failed_id] - place[source]) % n
    is_source = (me == source).astype(jnp.int32)[None]
    info = jnp.stack([(me == failed_id).astype(jnp.int32), ahead.astype(jnp.int32)])

    state = (master, moment1, moment2)
    chunks = largest(
        (c for c in range(2, MOST_CHUNKS + 1, 2) if rows % (TILE * c) == 0), 2
    )
    steps = (chunks + LAG * (n - 2)) // 2
    forward = [(order[p], order[(p + 1) % n]) for p in range(n)]
    backward = [(b, a) for a, b in forward]
    sends, got = [], []

    def send(*after):
        step = len(got)
        seen = got[step - LAG] if step >= LAG else ()
        here = min(step, chunks - 1)
        places = (here, chunks - 1 - here)
        sends.append(pack(is_source, state, seen, after, places, rows // chunks))
        got.append(
            (
                lax.ppermute(sends[-1][0], "replica", forward),
                lax.ppermute(sends[-1][1], "replica", backward),
            )
        )
        return (sends[-1][0],)

    sent = send()
    sent = send(*sent)
    both = beside(tokens[0], d_out[0], sent)
    both = lax.all_gather(both, ("fsdp", "tensor"), axis=0, tiled=True)
    sent = send(both)

    tile = 128 if units % 128 == 0 else units
    tiles = units // tile
    pieces = largest((p for p in (1, 3) if tiles % p == 0), 1)
    hidden, d_rows = [], None
    for piece in range(pieces):
        count = tiles // pieces
        part, d_rows = layer(
            both, w_gate, w_up, w_down, d_rows, sent, tile, piece * count, count
        )
        hidden.append(part)
        sent = send(d_rows)
    hidden = jnp.concatenate(hidden, axis=1)

    kept = jnp.where(me == failed_id, jnp.zeros_like(hidden), hidden)

    def parcel(to):
        slab = lax.dynamic_slice_in_dim(both, features + to * width, width, 1)
        return jnp.concatenate([kept, slab], axis=1)

    parcels = [parcel(me)]
    for far in range(1, n):
        route = [(i, (i + far) % n) for i in range(n)]
        parcels.append(lax.ppermute(parcel((me + far) % n), "replica", route))

    afters = [sent]
    for _ in range(3):
        afters.append(send(*afters[-1]))
    d_tokens = sum_scattered(d_rows, ("fsdp", "tensor"), afters)

    hidden_t, outs = collect(parcels, units, afters[-1])
    block = largest((b for b in range(TILE, 193, TILE) if rows % b == 0), rows)
    blocks = rows // block
    sent = (hidden_t,)
    news = ()
    turns = 2 if blocks % 2 == 0 else 1
    for turn in range(turns):
        count = blocks // turns
        news = update(
            info, hidden_t, outs, state, news, sent, n - 1.0, block, turn * count, count
        )
        sent = send(news[0])

    patched = 0

    def patch_to(step, news, after):
        nonlocal patched
        arrivals = [(s, way) for s in range(patched, step) for way in (True, False)]
        blocks = [b for s in range(patched, step) for b in got[s]]
        patched = step
        return patch(info, hidden_t, outs, blocks, arrivals, news, after, chunks, n)

    news = patch_to(len(got) - 2, news, sent)
    while len(got) < steps:
        sent = send(news[0])
    news = patch_to(steps - 1, news, sent)
    news = patch_to(steps, news, ())
    return (d_tokens[None], *news)


def solution(mesh):
    placed = (
        P("replica", ("fsdp", "tensor"), None),
        P("replica", ("fsdp", "tensor"), None),
        P(None, ("fsdp", "tensor")),
        P(None, ("fsdp", "tensor")),
        P(("fsdp", "tensor"), None),
        P(("fsdp", "tensor")),
        P(None, ("fsdp", "tensor"), "replica"),
        P(None, ("fsdp", "tensor"), "replica"),
        P(None, ("fsdp", "tensor"), "replica"),
    )
    return jax.shard_map(
        per_device,
        mesh=mesh,
        in_specs=placed,
        out_specs=(
            P("replica", ("fsdp", "tensor"), None),
            P(("fsdp", "tensor"), "replica"),
            P(("fsdp", "tensor"), "replica"),
            P(("fsdp", "tensor"), "replica"),
        ),
        check_vma=False,
    )
```

```python
import functools

import jax
import jax.numpy as jnp
from jax import lax
from jax.experimental import pallas as pl
from jax.experimental.pallas import tpu as pltpu
from jax.sharding import PartitionSpec as P

BF16, F32 = jnp.bfloat16, jnp.float32
LAG = 2
MOST_CHUNKS = 20
TILE = 16
GROUP = 8
VMEM = 48 << 20

ANY = pl.BlockSpec(memory_space=pl.ANY)
SMEM = pl.BlockSpec(memory_space=pltpu.SMEM)
WHOLE = pl.BlockSpec(memory_space=pltpu.VMEM)
PARAMS = pltpu.CompilerParams(vmem_limit_bytes=VMEM)


def ring_order(n):
    return [0, 1, 3, 2] if n == 4 else list(range(n))


def largest(options, default):
    options = list(options)
    return max(options) if options else default


def shares(total, parts):
    parts = min(parts, total)
    edges = [total * i // parts for i in range(parts + 1)]
    return [(a, b - a) for a, b in zip(edges, edges[1:])]


def cost(flops, bytes_accessed, transcendentals=0):
    return pl.CostEstimate(
        flops=flops, bytes_accessed=bytes_accessed, transcendentals=transcendentals
    )


def updated(master_old, first_old, second_old, total, healthy):
    first_new = 0.9 * first_old + (0.1 / healthy) * total
    second_new = 0.95 * second_old + (0.05 / healthy**2) * (total * total)
    root = second_new * lax.rsqrt(second_new)
    step = first_new * pl.reciprocal(root + 1e-08)
    return master_old - 0.01 * step, first_new, second_new


def pack_body(flag, *refs, places, chunk, count_seen, count_after):
    state = refs[0:3]
    seen = refs[3 : 3 + count_seen]
    rest = refs[3 + count_seen + count_after :]
    sends = rest[:2]
    held, sem = rest[2:]

    def fetch(j):
        way, k = divmod(j, 3)
        rows = pl.ds(places[way] * chunk, chunk)
        return pltpu.make_async_copy(state[k].at[1, rows], held.at[j], sem.at[j])

    def convert():
        for j in range(6):
            fetch(j).start()
        for j in range(6):
            way, k = divmod(j, 3)
            fetch(j).wait()
            sends[way][k] = held[j].astype(BF16)

    def relay(way):
        return pltpu.make_async_copy(seen[way], sends[way], sem.at[way])

    if not seen:
        convert()
        return
    pl.when(flag[0] == 1)(convert)

    @pl.when(flag[0] == 0)
    def _():
        for way in range(2):
            relay(way).start()
        for way in range(2):
            relay(way).wait()


def pack(is_source, state, seen, after, places, chunk):
    width = state[0].shape[2]
    shape = jax.ShapeDtypeStruct((3, chunk, width), BF16)
    return pl.pallas_call(
        functools.partial(
            pack_body,
            places=places,
            chunk=chunk,
            count_seen=len(seen),
            count_after=len(after),
        ),
        in_specs=[SMEM] + [ANY] * (3 + len(seen) + len(after)),
        out_specs=[WHOLE, WHOLE],
        out_shape=[shape, shape],
        scratch_shapes=[
            pltpu.VMEM((6, chunk, width), F32),
            pltpu.SemaphoreType.DMA((6,)),
        ],
        compiler_params=PARAMS,
        cost_estimate=cost(0, 2 * 3 * chunk * width * 6),
        name="pack",
    )(is_source, *state, *seen, *after)


def beside_body(*refs):
    tokens, d_out, out = refs[0], refs[1], refs[-1]
    width = tokens.shape[1]
    out[:, :width] = tokens[...]
    out[:, width:] = d_out[...]


def beside(tokens, d_out, after):
    rows, width = tokens.shape
    return pl.pallas_call(
        beside_body,
        in_specs=[WHOLE, WHOLE] + [ANY] * len(after),
        out_specs=WHOLE,
        out_shape=jax.ShapeDtypeStruct((rows, 2 * width), tokens.dtype),
        compiler_params=PARAMS,
        cost_estimate=cost(0, 4 * rows * width * 2),
        name="beside",
    )(tokens, d_out, *after)


def by_rows(a, b):
    return lax.dot_general(a, b, (((1,), (1,)), ((), ())), preferred_element_type=F32)


def layer_body(both, gate_ref, up_ref, down_ref, *refs, resumed):
    hidden_ref, sum_ref = refs[-2:]
    features = gate_ref.shape[0]
    tile = gate_ref.shape[1]
    x, dy = both[:, :features], both[:, features:]
    w_gate, w_up = gate_ref[...], up_ref[...]
    joined = tile % 128 == 0
    if joined:
        w_both = jnp.concatenate([w_gate, w_up], axis=1)
        gate_up = jnp.dot(x, w_both, preferred_element_type=F32)
        gate, up = gate_up[:, :tile], gate_up[:, tile:]
    else:
        gate = jnp.dot(x, w_gate, preferred_element_type=F32)
        up = jnp.dot(x, w_up, preferred_element_type=F32)
    d_hidden = by_rows(dy, down_ref[...])
    sig = 1.0 / (1.0 + jnp.exp(-gate))
    hidden_ref[...] = (gate * sig * up).astype(BF16)
    d_gate = (d_hidden * up * sig * (1.0 + gate * (1.0 - sig))).astype(BF16)
    d_up = (d_hidden * gate * sig).astype(BF16)
    if joined:
        term = by_rows(jnp.concatenate([d_gate, d_up], axis=1), w_both)
    else:
        term = by_rows(d_gate, w_gate) + by_rows(d_up, w_up)

    @pl.when(pl.program_id(0) == 0)
    def _():
        sum_ref[...] = (refs[0][...] + term) if resumed else term

    @pl.when(pl.program_id(0) > 0)
    def _():
        sum_ref[...] += term


def layer(both, w_gate, w_up, w_down, partial_sum, after, tile, first, count):
    rows = both.shape[0]
    features = w_gate.shape[0]
    across = pl.BlockSpec((features, tile), lambda i: (0, first + i))
    resumed = partial_sum is not None
    fixed = pl.BlockSpec((rows, features), lambda i: (0, 0))
    return pl.pallas_call(
        functools.partial(layer_body, resumed=resumed),
        grid=(count,),
        in_specs=[
            pl.BlockSpec(both.shape, lambda i: (0, 0)),
            across,
            across,
            pl.BlockSpec((tile, features), lambda i: (first + i, 0)),
        ]
        + [fixed] * resumed
        + [ANY] * len(after),
        out_specs=[pl.BlockSpec((rows, tile), lambda i: (0, i)), fixed],
        out_shape=[
            jax.ShapeDtypeStruct((rows, count * tile), BF16),
            jax.ShapeDtypeStruct((rows, features), F32),
        ],
        compiler_params=PARAMS,
        cost_estimate=cost(
            10 * rows * features * count * tile,
            3 * features * count * tile * 2,
            rows * count * tile,
        ),
        name="layer",
    )(both, w_gate, w_up, w_down, *([partial_sum] if resumed else []), *after)


def halve_body(bit, *refs, arrived, final):
    value = refs[0][...]
    if arrived:
        value = value + refs[1][...]
    if final:
        refs[-1][...] = value.astype(BF16)
        return
    kept, sent = refs[-2:]
    half = value.shape[0] // 2
    low, high = value[:half], value[half:]
    upper = bit[0] == 1
    kept[...] = jnp.where(upper, high, low)
    sent[...] = jnp.where(upper, low, high)


def halve(bit, value, arrived, after, final):
    rows, features = value.shape
    if final:
        out_shape = jax.ShapeDtypeStruct((rows, features), BF16)
    else:
        out_shape = [jax.ShapeDtypeStruct((rows // 2, features), F32)] * 2
    return pl.pallas_call(
        functools.partial(halve_body, arrived=bool(arrived), final=final),
        in_specs=[SMEM] + [WHOLE] * (1 + len(arrived)) + [ANY] * len(after),
        out_specs=WHOLE if final else [WHOLE, WHOLE],
        out_shape=out_shape,
        compiler_params=PARAMS,
        cost_estimate=cost(0, 3 * rows * features * 4),
        name="halve",
    )(bit, value, *arrived, *after)


class ScatteredSum:
    def __init__(self, value, axes):
        sizes = [lax.axis_size(axis) for axis in axes]
        self.value, self.arrived, self.levels = value, (), []
        self.done = any(size & (size - 1) for size in sizes)
        if self.done:
            summed = lax.psum_scatter(value, axes, scatter_dimension=0, tiled=True)
            self.value = summed.astype(BF16)
            return
        for axis, size in zip(axes, sizes):
            apart = size // 2
            while apart:
                self.levels.append((axis, size, apart))
                apart //= 2

    def advance(self, after):
        if self.done:
            return ()
        if self.levels:
            axis, size, apart = self.levels.pop(0)
            bit = ((lax.axis_index(axis) // apart) % 2).astype(jnp.int32)[None]
            self.value, sent = halve(bit, self.value, self.arrived, after, False)
            route = [(i, i ^ apart) for i in range(size)]
            self.arrived = (lax.ppermute(sent, axis, route),)
        else:
            bit = jnp.zeros((1,), jnp.int32)
            self.value = halve(bit, self.value, self.arrived, after, True)
            self.done = True
        return (self.value,)


def parcels_body(where, *refs, count, n, features):
    both, hidden = refs[0], refs[1 : 1 + count]
    parcels = refs[-n:]
    units = sum(part.shape[1] for part in hidden)
    width = parcels[0].shape[1] - units
    keep = where[1] == 0
    for far in range(n):
        to = lax.rem(where[0] + far, n)
        first = 0
        for part in hidden:
            here = pl.ds(first, part.shape[1])
            parcels[far][:, here] = jnp.where(keep, part[...], jnp.zeros_like(part))
            first += part.shape[1]
        slab = pl.ds(pl.multiple_of(features + to * width, 128), width)
        parcels[far][:, pl.ds(units, width)] = both[:, slab]


def make_parcels(where, both, hidden, after, n, width):
    rows = both.shape[0]
    features = both.shape[1] // 2
    length = sum(part.shape[1] for part in hidden) + width
    shape = jax.ShapeDtypeStruct((rows, length), BF16)
    return pl.pallas_call(
        functools.partial(parcels_body, count=len(hidden), n=n, features=features),
        in_specs=[SMEM] + [WHOLE] * (1 + len(hidden)) + [ANY] * len(after),
        out_specs=[WHOLE] * n,
        out_shape=[shape] * n,
        compiler_params=PARAMS,
        cost_estimate=cost(0, 4 * n * rows * length),
        name="parcels",
    )(where, both, *hidden, *after)


def collect_body(*refs, count, units):
    hidden_t, outs = refs[-2:]
    rows = refs[0].shape[0]
    for j in range(count):
        outs[pl.ds(j * rows, rows)] = refs[j][:, units:]
    hidden = jnp.concatenate([refs[j][:, :units] for j in range(count)], axis=0)
    hidden_t[...] = hidden.astype(F32).T.astype(BF16)


def collect(parcels, units, after):
    rows, length = parcels[0].shape
    depth = rows * len(parcels)
    return pl.pallas_call(
        functools.partial(collect_body, count=len(parcels), units=units),
        in_specs=[WHOLE] * len(parcels) + [ANY] * len(after),
        out_specs=[WHOLE, WHOLE],
        out_shape=[
            jax.ShapeDtypeStruct((units, depth), BF16),
            jax.ShapeDtypeStruct((depth, length - units), BF16),
        ],
        compiler_params=PARAMS,
        cost_estimate=cost(0, 4 * depth * length),
        name="collect",
    )(*parcels, *after)


def update_body(info, hid_ref, out_ref, *refs, healthy, block, first, count, unread):
    state, news = refs[:3], refs[3 + unread : 6 + unread]
    total = refs[6 + unread]
    width = out_ref.shape[1]

    def step(hid, m_ref, a_ref, b_ref, m_new, a_new, b_new):
        total[...] = jnp.dot(hid[...], out_ref[...], preferred_element_type=F32)

        @pl.loop(0, block // GROUP)
        def _(i):
            here = pl.ds(pl.multiple_of(i * GROUP, GROUP), GROUP)
            m_new[here], a_new[here], b_new[here] = updated(
                m_ref[0, here], a_ref[0, here], b_ref[0, here], total[here], healthy
            )

    old = pl.BlockSpec((1, block, width), lambda i: (0, first + i, 0))
    new = pl.BlockSpec((block, width), lambda i: (first + i, 0))

    @pl.when(info[0] == 0)
    def _():
        pltpu.emit_pipeline(
            step,
            grid=(count,),
            in_specs=[
                pl.BlockSpec((block, hid_ref.shape[1]), lambda i: (first + i, 0)),
                old,
                old,
                old,
            ],
            out_specs=[new] * 3,
        )(hid_ref, *state, *news)


def update(info, hidden_t, outs, state, news, after, healthy, block, first, count):
    _, rows, width = state[0].shape
    depth = hidden_t.shape[1]
    shape = jax.ShapeDtypeStruct((rows, width), F32)
    unread = len(news) + len(after)
    return pl.pallas_call(
        functools.partial(
            update_body,
            healthy=healthy,
            block=block,
            first=first,
            count=count,
            unread=unread,
        ),
        in_specs=[SMEM, ANY, WHOLE] + [ANY] * (3 + unread),
        out_specs=[ANY] * 3,
        out_shape=[shape] * 3,
        scratch_shapes=[pltpu.VMEM((block, width), F32)],
        input_output_aliases={6 + k: k for k in range(len(news))},
        compiler_params=PARAMS,
        cost_estimate=cost(
            2 * count * block * width * depth,
            6 * count * block * width * 4,
            2 * count * block * width,
        ),
        name="update",
    )(info, hidden_t, outs, *state, *news, *after)


def patch_body(info, hid_ref, out_ref, *refs, arrivals, chunks, n, count_after):
    count = len(arrivals)
    got = refs[:count]
    rest = refs[count + 3 + count_after :]
    news = rest[:3]
    held, made, total, in_sem, out_sem = rest[3:]
    chunk = held.shape[2]
    ahead = info[1]
    lag_of = {True: LAG * (ahead - 1), False: LAG * (n - ahead - 1)}

    def fetch(j):
        return pltpu.make_async_copy(got[j], held.at[j % 2], in_sem.at[j % 2])

    def first_row(j):
        step, forward = arrivals[j]
        place = step - lag_of[forward]
        if not forward:
            place = chunks - 1 - place
        return pl.multiple_of(jnp.clip(place, 0, chunks - 1) * chunk, TILE)

    def store(j, k):
        return pltpu.make_async_copy(
            made.at[j % 2, k], news[k].at[pl.ds(first_row(j), chunk)], out_sem.at[j % 2, k]
        )

    def valid(j):
        step, forward = arrivals[j]
        return step >= lag_of[forward]

    def finish(j):
        @pl.when(valid(j))
        def _():
            for k in range(3):
                store(j, k).wait()

    @pl.when(info[0] == 1)
    def _():
        fetch(0).start()
        for j in range(count):
            slot = j % 2
            if j + 1 < count:
                fetch(j + 1).start()
            fetch(j).wait()
            if j >= 2:
                finish(j - 2)

            @pl.when(valid(j))
            def _(j=j, slot=slot):
                first = first_row(j)

                units = hid_ref[pl.ds(first, chunk)]
                total[...] = jnp.dot(units, out_ref[...], preferred_element_type=F32)

                @pl.loop(0, chunk // TILE)
                def _(i):
                    here = pl.ds(pl.multiple_of(i * TILE, TILE), TILE)
                    old = [held[slot, k, here].astype(F32) for k in range(3)]
                    new = updated(*old, total[here], n - 1.0)
                    for k in range(3):
                        made[slot, k, here] = new[k]

                for k in range(3):
                    store(j, k).start()

        for j in range(max(count - 2, 0), count):
            finish(j)


def patch(info, hidden_t, outs, got, arrivals, news, after, chunks, n):
    rows, width = news[0].shape
    chunk = rows // chunks
    count = len(got)
    shape = jax.ShapeDtypeStruct((rows, width), F32)
    return pl.pallas_call(
        functools.partial(
            patch_body, arrivals=arrivals, chunks=chunks, n=n, count_after=len(after)
        ),
        in_specs=[SMEM, WHOLE, WHOLE] + [ANY] * (count + 3 + len(after)),
        out_specs=[ANY] * 3,
        out_shape=[shape] * 3,
        scratch_shapes=[
            pltpu.VMEM((2, 3, chunk, width), BF16),
            pltpu.VMEM((2, 3, chunk, width), F32),
            pltpu.VMEM((chunk, width), F32),
            pltpu.SemaphoreType.DMA((2,)),
            pltpu.SemaphoreType.DMA((2, 3)),
        ],
        input_output_aliases={3 + count + k: k for k in range(3)},
        compiler_params=PARAMS,
        cost_estimate=cost(
            2 * count * chunk * width * hidden_t.shape[1],
            count * 3 * chunk * width * 6,
            2 * count * chunk * width,
        ),
        name="patch",
    )(info, hidden_t, outs, *got, *news, *after)


def per_device(tokens, d_out, w_gate, w_up, w_down, failed, master, moment1, moment2):
    n = lax.axis_size("replica")
    me = lax.axis_index("replica")
    _, rows, width = master.shape
    features, units = w_gate.shape

    failed_id = failed[0]
    source = (failed_id + 1) % n
    order = ring_order(n)
    place = jnp.array([order.index(i) for i in range(n)], jnp.int32)
    ahead = (place[failed_id] - place[source]) % n
    is_source = (me == source).astype(jnp.int32)[None]
    info = jnp.stack([(me == failed_id).astype(jnp.int32), ahead.astype(jnp.int32)])

    state = (master, moment1, moment2)
    chunks = largest(
        (c for c in range(2, MOST_CHUNKS + 1, 2) if rows % (TILE * c) == 0), 2
    )
    steps = (chunks + LAG * (n - 2)) // 2
    forward = [(order[p], order[(p + 1) % n]) for p in range(n)]
    backward = [(b, a) for a, b in forward]
    sends, got = [], []

    def send(*after):
        step = len(got)
        seen = got[step - LAG] if step >= LAG else ()
        here = min(step, chunks - 1)
        places = (here, chunks - 1 - here)
        sends.append(pack(is_source, state, seen, after, places, rows // chunks))
        got.append(
            (
                lax.ppermute(sends[-1][0], "replica", forward),
                lax.ppermute(sends[-1][1], "replica", backward),
            )
        )
        return (sends[-1][0],)

    sent = send()
    sent = send(*sent)
    both = beside(tokens[0], d_out[0], sent)
    both = lax.all_gather(both, ("fsdp", "tensor"), axis=0, tiled=True)
    sent = send(both)

    tile = 128 if units % 128 == 0 else units
    hidden, d_rows = [], None
    for first, count in shares(units // tile, 4):
        part, d_rows = layer(both, w_gate, w_up, w_down, d_rows, sent, tile, first, count)
        hidden.append(part)
        sent = send(d_rows)

    where = jnp.stack([me, info[0]])
    parcels = make_parcels(where, both, hidden, sent, n, width)
    arrived = [parcels[0]]
    for far in range(1, n):
        route = [(i, (i + far) % n) for i in range(n)]
        arrived.append(lax.ppermute(parcels[far], "replica", route))
    cotangents = ScatteredSum(d_rows, ("fsdp", "tensor"))
    sent = send(parcels[0], *cotangents.advance((parcels[0],)))
    sent = send(*cotangents.advance(sent))

    hidden_t, outs = collect(arrived, units, sent)
    sent = (hidden_t,)
    block = largest((b for b in range(TILE, 193, TILE) if rows % b == 0), rows)
    turns = shares(rows // block, 3)
    news = ()
    patched = 0

    def update_next(after):
        first, count = turns.pop(0)
        return update(
            info, hidden_t, outs, state, news, after, n - 1.0, block, first, count
        )

    def patch_to(step, after):
        nonlocal patched
        arrivals = [(s, way) for s in range(patched, step) for way in (True, False)]
        if not arrivals:
            return news
        blocks = [b for s in range(patched, step) for b in got[s]]
        patched = step
        return patch(info, hidden_t, outs, blocks, arrivals, news, after, chunks, n)

    while len(got) < steps:
        if len(turns) > 1:
            news = update_next(sent)
            news = patch_to(len(got) // 2 if patched == 0 else len(got) - 2, ())
        sent = send(*news[:1], *cotangents.advance(sent))
    while turns:
        news = update_next(sent)
    news = patch_to(steps - 1, sent)
    news = patch_to(steps, ())
    while not cotangents.done:
        cotangents.advance(sent)
    return (cotangents.value[None], *news)


def solution(mesh):
    placed = (
        P("replica", ("fsdp", "tensor"), None),
        P("replica", ("fsdp", "tensor"), None),
        P(None, ("fsdp", "tensor")),
        P(None, ("fsdp", "tensor")),
        P(("fsdp", "tensor"), None),
        P(("fsdp", "tensor")),
        P(None, ("fsdp", "tensor"), "replica"),
        P(None, ("fsdp", "tensor"), "replica"),
        P(None, ("fsdp", "tensor"), "replica"),
    )
    return jax.shard_map(
        per_device,
        mesh=mesh,
        in_specs=placed,
        out_specs=(
            P("replica", ("fsdp", "tensor"), None),
            P(("fsdp", "tensor"), "replica"),
            P(("fsdp", "tensor"), "replica"),
            P(("fsdp", "tensor"), "replica"),
        ),
        check_vma=False,
    )
```

```python
import functools

import jax
import jax.numpy as jnp
from jax import lax
from jax.experimental import pallas as pl
from jax.experimental.pallas import tpu as pltpu
from jax.sharding import PartitionSpec as P

BF16, F32 = jnp.bfloat16, jnp.float32
LAG = 2
MOST_CHUNKS = 20
TILE = 16
VMEM = 48 << 20

ANY = pl.BlockSpec(memory_space=pl.ANY)
SMEM = pl.BlockSpec(memory_space=pltpu.SMEM)
WHOLE = pl.BlockSpec(memory_space=pltpu.VMEM)
PARAMS = pltpu.CompilerParams(vmem_limit_bytes=VMEM)


def ring_order(n):
    return [0, 1, 3, 2] if n == 4 else list(range(n))


def largest(options, default):
    options = list(options)
    return max(options) if options else default


def shares(total, parts):
    parts = min(parts, total)
    edges = [total * i // parts for i in range(parts + 1)]
    return [(a, b - a) for a, b in zip(edges, edges[1:])]


def row_group(rows):
    return largest((g for g in (16, 32) if rows % g == 0), rows)


def cost(flops, bytes_accessed, transcendentals=0):
    return pl.CostEstimate(
        flops=flops, bytes_accessed=bytes_accessed, transcendentals=transcendentals
    )


def updated(master_old, first_old, second_old, total, healthy):
    first_new = 0.9 * first_old + (0.1 / healthy) * total
    second_new = 0.95 * second_old + (0.05 / healthy**2) * (total * total)
    root = second_new * lax.rsqrt(second_new)
    step = first_new * pl.reciprocal(root + 1e-08)
    return master_old - 0.01 * step, first_new, second_new


def column_pieces(lengths, width):
    moves, column = [], 0
    for part, length in enumerate(lengths):
        begin = 0
        while begin < length:
            piece, to = divmod(column, width)
            run = min(length - begin, width - to)
            moves.append((part, begin, piece, to, run))
            begin, column = begin + run, column + run
    return moves


def pack_body(flag, targets, *refs, places, chunk, slabs, passed, counts):
    state = refs[0:3]
    count_seen, count_parts, count_after = counts
    seen = refs[3 : 3 + count_seen]
    both = refs[3 + count_seen]
    parts = refs[4 + count_seen : 4 + count_seen + count_parts]
    rest = refs[3 + count_seen + (count_parts + 1 if count_parts else 0) + count_after :]
    sends = rest[:2]
    held, sem, passed_sem = rest[2:]
    width = sends[0].shape[1]
    size = 3 * chunk

    def fetch(j):
        way, k = divmod(j, 3)
        rows = pl.ds(places[way] * chunk, chunk)
        return pltpu.make_async_copy(state[k].at[1, rows], held.at[j], sem.at[j])

    def convert():
        for j in range(6):
            fetch(j).start()
        for j in range(6):
            way, k = divmod(j, 3)
            fetch(j).wait()
            sends[way][pl.ds(k * chunk, chunk)] = held[j].astype(BF16)

    def relay(way):
        rows = pl.ds(0, size)
        return pltpu.make_async_copy(seen[way].at[rows], sends[way].at[rows], sem.at[way])

    def hand_on(way):
        rows = pl.ds(size, passed[way])
        return pltpu.make_async_copy(
            seen[way].at[rows], sends[way].at[rows], passed_sem.at[way]
        )

    for way in range(2):
        if passed[way]:
            hand_on(way).start()

    if not seen:
        convert()
    else:
        pl.when(flag[0] == 1)(convert)

        @pl.when(flag[0] == 0)
        def _():
            for way in range(2):
                relay(way).start()
            for way in range(2):
                relay(way).wait()

    n = targets.shape[0]
    for way in range(2):
        if slabs[way]:
            tokens, features = both.shape[0], both.shape[1] // 2
            keep = flag[1] == 0
            below = size
            moves = column_pieces([part.shape[1] for part in parts], width)
            for part, begin, piece, to, run in moves:
                units = parts[part][:, begin : begin + run]
                rows = pl.ds(size + piece * tokens, tokens)
                sends[way][rows, pl.ds(to, run)] = jnp.where(
                    keep, units, jnp.zeros_like(units)
                )
            below += (1 + moves[-1][2]) * tokens
            for far in range(slabs[way], 0, -1):
                target = targets[far if way == 0 else n - far]
                slab = pl.ds(pl.multiple_of(features + target * width, 128), width)
                sends[way][pl.ds(below, tokens)] = both[:, slab]
                below += tokens

    for way in range(2):
        if passed[way]:
            hand_on(way).wait()


def pack(flag, targets, state, seen, parcel, after, places, chunk, slabs, passed):
    width = state[0].shape[2]
    extra = list(passed)
    if parcel:
        tokens = parcel[0].shape[0]
        pieces = -(-sum(part.shape[1] for part in parcel[1:]) // width)
        extra = [tokens * (pieces + count) if count else 0 for count in slabs]
    counts = (len(seen), max(len(parcel) - 1, 0), len(after))
    return pl.pallas_call(
        functools.partial(
            pack_body, places=places, chunk=chunk, slabs=slabs, passed=passed, counts=counts
        ),
        in_specs=[SMEM, SMEM]
        + [ANY] * (3 + len(seen))
        + [WHOLE] * len(parcel)
        + [ANY] * len(after),
        out_specs=[WHOLE, WHOLE],
        out_shape=[
            jax.ShapeDtypeStruct((3 * chunk + more, width), BF16) for more in extra
        ],
        scratch_shapes=[
            pltpu.VMEM((6, chunk, width), F32),
            pltpu.SemaphoreType.DMA((6,)),
            pltpu.SemaphoreType.DMA((2,)),
        ],
        compiler_params=PARAMS,
        cost_estimate=cost(0, 2 * 3 * chunk * width * 6),
        name="pack",
    )(flag, targets, *state, *seen, *parcel, *after)


def beside_body(*refs):
    tokens, d_out, out = refs[0], refs[1], refs[-1]
    width = tokens.shape[1]
    out[:, :width] = tokens[...]
    out[:, width:] = d_out[...]


def beside(tokens, d_out, after):
    rows, width = tokens.shape
    return pl.pallas_call(
        beside_body,
        in_specs=[WHOLE, WHOLE] + [ANY] * len(after),
        out_specs=WHOLE,
        out_shape=jax.ShapeDtypeStruct((rows, 2 * width), tokens.dtype),
        compiler_params=PARAMS,
        cost_estimate=cost(0, 4 * rows * width * 2),
        name="beside",
    )(tokens, d_out, *after)


def by_rows(a, b):
    return lax.dot_general(a, b, (((1,), (1,)), ((), ())), preferred_element_type=F32)


def layer_body(both, gate_ref, up_ref, down_ref, *refs, resumed):
    hidden_ref, sum_ref = refs[-2:]
    features = gate_ref.shape[0]
    tile = gate_ref.shape[1]
    x, dy = both[:, :features], both[:, features:]
    w_gate, w_up = gate_ref[...], up_ref[...]
    joined = tile % 128 == 0
    if joined:
        w_both = jnp.concatenate([w_gate, w_up], axis=1)
        gate_up = jnp.dot(x, w_both, preferred_element_type=F32)
        gate, up = gate_up[:, :tile], gate_up[:, tile:]
    else:
        gate = jnp.dot(x, w_gate, preferred_element_type=F32)
        up = jnp.dot(x, w_up, preferred_element_type=F32)
    d_hidden = by_rows(dy, down_ref[...])
    sig = 1.0 / (1.0 + jnp.exp(-gate))
    hidden_ref[...] = (gate * sig * up).astype(BF16)
    d_gate = (d_hidden * up * sig * (1.0 + gate * (1.0 - sig))).astype(BF16)
    d_up = (d_hidden * gate * sig).astype(BF16)
    if joined:
        term = by_rows(jnp.concatenate([d_gate, d_up], axis=1), w_both)
    else:
        term = by_rows(d_gate, w_gate) + by_rows(d_up, w_up)

    @pl.when(pl.program_id(0) == 0)
    def _():
        sum_ref[...] = (refs[0][...] + term) if resumed else term

    @pl.when(pl.program_id(0) > 0)
    def _():
        sum_ref[...] += term


def layer(both, w_gate, w_up, w_down, partial_sum, after, tile, first, count):
    rows = both.shape[0]
    features = w_gate.shape[0]
    across = pl.BlockSpec((features, tile), lambda i: (0, first + i))
    resumed = partial_sum is not None
    fixed = pl.BlockSpec((rows, features), lambda i: (0, 0))
    return pl.pallas_call(
        functools.partial(layer_body, resumed=resumed),
        grid=(count,),
        in_specs=[
            pl.BlockSpec(both.shape, lambda i: (0, 0)),
            across,
            across,
            pl.BlockSpec((tile, features), lambda i: (first + i, 0)),
        ]
        + [fixed] * resumed
        + [ANY] * len(after),
        out_specs=[pl.BlockSpec((rows, tile), lambda i: (0, i)), fixed],
        out_shape=[
            jax.ShapeDtypeStruct((rows, count * tile), BF16),
            jax.ShapeDtypeStruct((rows, features), F32),
        ],
        compiler_params=PARAMS,
        cost_estimate=cost(
            10 * rows * features * count * tile,
            3 * features * count * tile * 2,
            rows * count * tile,
        ),
        name="layer",
    )(both, w_gate, w_up, w_down, *([partial_sum] if resumed else []), *after)


def halve_body(bit, *refs, arrived, final):
    value = refs[0][...]
    if arrived:
        value = value + refs[1][...]
    if final:
        refs[-1][...] = value.astype(BF16)
        return
    kept, sent = refs[-2:]
    half = value.shape[0] // 2
    low, high = value[:half], value[half:]
    upper = bit[0] == 1
    kept[...] = jnp.where(upper, high, low)
    sent[...] = jnp.where(upper, low, high)


def halve(bit, value, arrived, after, final):
    rows, features = value.shape
    if final:
        out_shape = jax.ShapeDtypeStruct((rows, features), BF16)
    else:
        out_shape = [jax.ShapeDtypeStruct((rows // 2, features), F32)] * 2
    return pl.pallas_call(
        functools.partial(halve_body, arrived=bool(arrived), final=final),
        in_specs=[SMEM] + [WHOLE] * (1 + len(arrived)) + [ANY] * len(after),
        out_specs=WHOLE if final else [WHOLE, WHOLE],
        out_shape=out_shape,
        compiler_params=PARAMS,
        cost_estimate=cost(0, 3 * rows * features * 4),
        name="halve",
    )(bit, value, *arrived, *after)


class ScatteredSum:
    def __init__(self, value, axes):
        sizes = [lax.axis_size(axis) for axis in axes]
        self.value, self.arrived, self.levels = value, (), []
        self.done = any(size & (size - 1) for size in sizes)
        if self.done:
            summed = lax.psum_scatter(value, axes, scatter_dimension=0, tiled=True)
            self.value = summed.astype(BF16)
            return
        for axis, size in zip(axes, sizes):
            apart = size // 2
            while apart:
                self.levels.append((axis, size, apart))
                apart //= 2

    def advance(self, after):
        if self.done:
            return ()
        if self.levels:
            axis, size, apart = self.levels.pop(0)
            bit = ((lax.axis_index(axis) // apart) % 2).astype(jnp.int32)[None]
            self.value, sent = halve(bit, self.value, self.arrived, after, False)
            route = [(i, i ^ apart) for i in range(size)]
            self.arrived = (lax.ppermute(sent, axis, route),)
        else:
            bit = jnp.zeros((1,), jnp.int32)
            self.value = halve(bit, self.value, self.arrived, after, True)
            self.done = True
        return (self.value,)


def collect_body(flag, targets, both, *refs, places, parts_count, size, pieces):
    parts = refs[:parts_count]
    blocks = refs[parts_count : parts_count + len(places)]
    hidden_t, outs, held, sem = refs[-4:]
    tokens, features = both.shape[0], both.shape[1] // 2
    width = outs.shape[1]

    def fetch(j, part):
        rows = pl.ds(size, pieces * tokens) if part == 0 else pl.ds(places[j], tokens)
        here = pl.ds(0, pieces * tokens) if part == 0 else pl.ds(pieces * tokens, tokens)
        return pltpu.make_async_copy(
            blocks[j].at[rows], held.at[j + 1, here], sem.at[j, part]
        )

    for j in range(len(places)):
        for part in range(2):
            fetch(j, part).start()
    keep = flag[1] == 0
    for part, begin, piece, to, run in column_pieces([p.shape[1] for p in parts], width):
        units = parts[part][:, begin : begin + run]
        held[0, pl.ds(piece * tokens, tokens), pl.ds(to, run)] = jnp.where(
            keep, units, jnp.zeros_like(units)
        )
    slab = pl.ds(pl.multiple_of(features + targets[0] * width, 128), width)
    held[0, pl.ds(pieces * tokens, tokens)] = both[:, slab]
    for j in range(len(places)):
        for part in range(2):
            fetch(j, part).wait()

    count = len(places) + 1
    for j in range(count):
        outs[pl.ds(j * tokens, tokens)] = held[j, pl.ds(pieces * tokens, tokens)]
    for piece in range(pieces):
        run = min(width, hidden_t.shape[0] - piece * width)
        rows = pl.ds(piece * tokens, tokens)
        hidden = jnp.concatenate([held[j, rows, :run] for j in range(count)], axis=0)
        hidden_t[pl.ds(piece * width, run)] = hidden.astype(F32).T.astype(BF16)


def collect(flag, targets, both, parts, blocks, places, size, width, after):
    tokens = both.shape[0]
    units = sum(part.shape[1] for part in parts)
    pieces = -(-units // width)
    depth = tokens * (len(blocks) + 1)
    return pl.pallas_call(
        functools.partial(
            collect_body,
            places=places,
            parts_count=len(parts),
            size=size,
            pieces=pieces,
        ),
        in_specs=[SMEM, SMEM]
        + [WHOLE] * (1 + len(parts))
        + [ANY] * (len(blocks) + len(after)),
        out_specs=[WHOLE, WHOLE],
        out_shape=[
            jax.ShapeDtypeStruct((units, depth), BF16),
            jax.ShapeDtypeStruct((depth, width), BF16),
        ],
        scratch_shapes=[
            pltpu.VMEM((len(blocks) + 1, (pieces + 1) * tokens, width), BF16),
            pltpu.SemaphoreType.DMA((len(blocks), 2)),
        ],
        compiler_params=PARAMS,
        cost_estimate=cost(0, 4 * depth * (units + width)),
        name="collect",
    )(flag, targets, both, *parts, *blocks, *after)


def update_body(info, hid_ref, out_ref, *refs, healthy, block, first, count, unread):
    state, news = refs[:3], refs[3 + unread : 6 + unread]
    total = refs[6 + unread]
    width = out_ref.shape[1]
    group = row_group(block)

    def step(hid, m_ref, a_ref, b_ref, m_new, a_new, b_new):
        total[...] = jnp.dot(hid[...], out_ref[...], preferred_element_type=F32)

        @pl.loop(0, block // group)
        def _(i):
            here = pl.ds(pl.multiple_of(i * group, group), group)
            m_new[here], a_new[here], b_new[here] = updated(
                m_ref[0, here], a_ref[0, here], b_ref[0, here], total[here], healthy
            )

    old = pl.BlockSpec((1, block, width), lambda i: (0, first + i, 0))
    new = pl.BlockSpec((block, width), lambda i: (first + i, 0))

    @pl.when(info[0] == 0)
    def _():
        pltpu.emit_pipeline(
            step,
            grid=(count,),
            in_specs=[
                pl.BlockSpec((block, hid_ref.shape[1]), lambda i: (first + i, 0)),
                old,
                old,
                old,
            ],
            out_specs=[new] * 3,
        )(hid_ref, *state, *news)


def update(info, hidden_t, outs, state, news, after, healthy, block, first, count):
    _, rows, width = state[0].shape
    depth = hidden_t.shape[1]
    shape = jax.ShapeDtypeStruct((rows, width), F32)
    unread = len(news) + len(after)
    return pl.pallas_call(
        functools.partial(
            update_body,
            healthy=healthy,
            block=block,
            first=first,
            count=count,
            unread=unread,
        ),
        in_specs=[SMEM, ANY, WHOLE] + [ANY] * (3 + unread),
        out_specs=[ANY] * 3,
        out_shape=[shape] * 3,
        scratch_shapes=[pltpu.VMEM((block, width), F32)],
        input_output_aliases={6 + k: k for k in range(len(news))},
        compiler_params=PARAMS,
        cost_estimate=cost(
            2 * count * block * width * depth,
            6 * count * block * width * 4,
            2 * count * block * width,
        ),
        name="update",
    )(info, hidden_t, outs, *state, *news, *after)


def patch_body(info, hid_ref, out_ref, *refs, arrivals, chunks, n, count_after):
    count = len(arrivals)
    got = refs[:count]
    rest = refs[count + 3 + count_after :]
    news = rest[:3]
    held, made, total, in_sem, out_sem = rest[3:]
    chunk = made.shape[2]
    group = row_group(chunk)
    ahead = info[1]
    lag_of = {True: LAG * (ahead - 1), False: LAG * (n - ahead - 1)}

    def fetch(j):
        rows = got[j].at[pl.ds(0, 3 * chunk)]
        return pltpu.make_async_copy(rows, held.at[j % 2], in_sem.at[j % 2])

    def first_row(j):
        step, forward = arrivals[j]
        place = step - lag_of[forward]
        if not forward:
            place = chunks - 1 - place
        return pl.multiple_of(jnp.clip(place, 0, chunks - 1) * chunk, TILE)

    def store(j, k):
        return pltpu.make_async_copy(
            made.at[j % 2, k], news[k].at[pl.ds(first_row(j), chunk)], out_sem.at[j % 2, k]
        )

    def valid(j):
        step, forward = arrivals[j]
        return step >= lag_of[forward]

    def finish(j):
        @pl.when(valid(j))
        def _():
            for k in range(3):
                store(j, k).wait()

    @pl.when(info[0] == 1)
    def _():
        fetch(0).start()
        for j in range(count):
            slot = j % 2
            if j + 1 < count:
                fetch(j + 1).start()
            fetch(j).wait()
            if j >= 2:
                finish(j - 2)

            @pl.when(valid(j))
            def _(j=j, slot=slot):
                first = first_row(j)

                units = hid_ref[pl.ds(first, chunk)]
                total[...] = jnp.dot(units, out_ref[...], preferred_element_type=F32)

                @pl.loop(0, chunk // group)
                def _(i):
                    base = pl.multiple_of(i * group, group)
                    old = [
                        held[slot, pl.ds(k * chunk + base, group)].astype(F32)
                        for k in range(3)
                    ]
                    new = updated(*old, total[pl.ds(base, group)], n - 1.0)
                    for k in range(3):
                        made[slot, k, pl.ds(base, group)] = new[k]

                for k in range(3):
                    store(j, k).start()

        for j in range(max(count - 2, 0), count):
            finish(j)


def patch(info, hidden_t, outs, got, arrivals, news, after, chunks, n):
    rows, width = news[0].shape
    chunk = rows // chunks
    count = len(got)
    shape = jax.ShapeDtypeStruct((rows, width), F32)
    return pl.pallas_call(
        functools.partial(
            patch_body, arrivals=arrivals, chunks=chunks, n=n, count_after=len(after)
        ),
        in_specs=[SMEM, WHOLE, WHOLE] + [ANY] * (count + 3 + len(after)),
        out_specs=[ANY] * 3,
        out_shape=[shape] * 3,
        scratch_shapes=[
            pltpu.VMEM((2, 3 * chunk, width), BF16),
            pltpu.VMEM((2, 3, chunk, width), F32),
            pltpu.VMEM((chunk, width), F32),
            pltpu.SemaphoreType.DMA((2,)),
            pltpu.SemaphoreType.DMA((2, 3)),
        ],
        input_output_aliases={3 + count + k: k for k in range(3)},
        compiler_params=PARAMS,
        cost_estimate=cost(
            2 * count * chunk * width * hidden_t.shape[1],
            count * 3 * chunk * width * 6,
            2 * count * chunk * width,
        ),
        name="patch",
    )(info, hidden_t, outs, *got, *news, *after)


def per_device(tokens, d_out, w_gate, w_up, w_down, failed, master, moment1, moment2):
    n = lax.axis_size("replica")
    me = lax.axis_index("replica")
    _, rows, width = master.shape
    features, units = w_gate.shape

    failed_id = failed[0]
    source = (failed_id + 1) % n
    order = ring_order(n)
    place = jnp.array([order.index(i) for i in range(n)], jnp.int32)
    ahead = (place[failed_id] - place[source]) % n
    lost = (me == failed_id).astype(jnp.int32)
    flag = jnp.stack([(me == source).astype(jnp.int32), lost])
    info = jnp.stack([lost, ahead.astype(jnp.int32)])
    targets = jnp.array(order, jnp.int32)[(place[me] + jnp.arange(n)) % n]

    state = (master, moment1, moment2)
    chunks = largest(
        (c for c in range(2, MOST_CHUNKS + 1, 2) if rows % (TILE * c) == 0), 2
    )
    chunk = rows // chunks
    steps = (chunks + LAG * (n - 2)) // 2
    reach = (n // 2, (n - 1) // 2)
    forward = [(order[p], order[(p + 1) % n]) for p in range(n)]
    backward = [(b, a) for a, b in forward]
    sends, got = [], []
    parcel_from = None

    def send(*after, parcel=()):
        nonlocal parcel_from
        step = len(got)
        seen = got[step - LAG] if step >= LAG else ()
        here = min(step, chunks - 1)
        slabs, passed = (0, 0), (0, 0)
        if parcel:
            parcel_from, slabs = step, reach
        elif parcel_from is not None and (step - parcel_from) % LAG == 0:
            hop = (step - parcel_from) // LAG
            passed = tuple(
                seen[way].shape[0] - 3 * chunk - both.shape[0]
                if hop < reach[way]
                else 0
                for way in range(2)
            )
        sends.append(
            pack(
                flag,
                targets,
                state,
                seen,
                parcel,
                after,
                (here, chunks - 1 - here),
                chunk,
                slabs,
                passed,
            )
        )
        got.append(
            (
                lax.ppermute(sends[-1][0], "replica", forward),
                lax.ppermute(sends[-1][1], "replica", backward),
            )
        )
        return (sends[-1][0],)

    sent = send()
    sent = send(*sent)
    both = beside(tokens[0], d_out[0], sent)
    both = lax.all_gather(both, ("fsdp", "tensor"), axis=0, tiled=True)
    sent = send(both)

    tile = 128 if units % 128 == 0 else units
    hidden, d_rows = [], None
    pieces = shares(units // tile, 4)
    for first, count in pieces:
        part, d_rows = layer(both, w_gate, w_up, w_down, d_rows, sent, tile, first, count)
        hidden.append(part)
        last = len(hidden) == len(pieces)
        sent = send(d_rows, parcel=(both, *hidden) if last else ())
    cotangents = ScatteredSum(d_rows, ("fsdp", "tensor"))

    news = ()
    patched = 0
    hidden_t = outs = None

    def gathered(after):
        blocks, places = [], []
        for way in range(2):
            for hop in range(reach[way]):
                blocks.append(got[parcel_from + LAG * hop][way])
                places.append(blocks[-1].shape[0] - both.shape[0])
        return collect(
            flag, targets, both, hidden, blocks, places, 3 * chunk, width, after
        )

    def update_part(first, count, after):
        return update(
            info, hidden_t, outs, state, news, after, n - 1.0, block, first, count
        )

    def patch_to(step, after):
        nonlocal patched
        arrivals = [(s, way) for s in range(patched, step) for way in (True, False)]
        if not arrivals:
            return news
        blocks = [b for s in range(patched, step) for b in got[s]]
        patched = step
        return patch(info, hidden_t, outs, blocks, arrivals, news, after, chunks, n)

    block = largest((b for b in range(TILE, 193, TILE) if rows % b == 0), rows)
    blocks = rows // block
    early = blocks // 4
    ready = parcel_from + LAG * reach[0] + 1
    while len(got) < steps:
        sent = send(*cotangents.advance(sent), *news[:1])
        if len(got) == ready and early and len(got) < steps:
            hidden_t, outs = gathered(sent)
            news = update_part(0, early, (hidden_t,))
            news = patch_to(4, ())
    if hidden_t is None:
        hidden_t, outs = gathered(sent)
        early = 0
    news = update_part(early, blocks - early, sent)
    news = patch_to(steps - 1, sent)
    news = patch_to(steps, ())
    while not cotangents.done:
        cotangents.advance(sent)
    return (cotangents.value[None], *news)


def solution(mesh):
    placed = (
        P("replica", ("fsdp", "tensor"), None),
        P("replica", ("fsdp", "tensor"), None),
        P(None, ("fsdp", "tensor")),
        P(None, ("fsdp", "tensor")),
        P(("fsdp", "tensor"), None),
        P(("fsdp", "tensor")),
        P(None, ("fsdp", "tensor"), "replica"),
        P(None, ("fsdp", "tensor"), "replica"),
        P(None, ("fsdp", "tensor"), "replica"),
    )
    return jax.shard_map(
        per_device,
        mesh=mesh,
        in_specs=placed,
        out_specs=(
            P("replica", ("fsdp", "tensor"), None),
            P(("fsdp", "tensor"), "replica"),
            P(("fsdp", "tensor"), "replica"),
            P(("fsdp", "tensor"), "replica"),
        ),
        check_vma=False,
    )
```

```python
import functools

import jax
import jax.numpy as jnp
from jax import lax
from jax.experimental import pallas as pl
from jax.experimental.pallas import tpu as pltpu
from jax.sharding import PartitionSpec as P

BF16, F32 = jnp.bfloat16, jnp.float32
LAG = 2
MOST_CHUNKS = 20
TILE = 16
BUFFERS = 3
FETCHED = 4
VMEM = 48 << 20

ANY = pl.BlockSpec(memory_space=pl.ANY)
SMEM = pl.BlockSpec(memory_space=pltpu.SMEM)
WHOLE = pl.BlockSpec(memory_space=pltpu.VMEM)
PARAMS = pltpu.CompilerParams(vmem_limit_bytes=VMEM)


def ring_order(n):
    return [0, 1, 3, 2] if n == 4 else list(range(n))


def largest(options, default):
    options = list(options)
    return max(options) if options else default


def shares(total, parts):
    parts = min(parts, total)
    edges = [total * i // parts for i in range(parts + 1)]
    return [(a, b - a) for a, b in zip(edges, edges[1:])]


def row_group(rows):
    return largest((g for g in (16, 32) if rows % g == 0), rows)


def cost(flops, bytes_accessed, transcendentals=0):
    return pl.CostEstimate(
        flops=flops, bytes_accessed=bytes_accessed, transcendentals=transcendentals
    )


def updated(master_old, first_old, second_old, total, healthy):
    first_new = 0.9 * first_old + (0.1 / healthy) * total
    second_new = 0.95 * second_old + (0.05 / healthy**2) * (total * total)
    root = second_new * lax.rsqrt(second_new)
    step = first_new * pl.reciprocal(root + 1e-08)
    return master_old - 0.01 * step, first_new, second_new


def column_pieces(lengths, width):
    moves, column = [], 0
    for part, length in enumerate(lengths):
        begin = 0
        while begin < length:
            piece, to = divmod(column, width)
            run = min(length - begin, width - to)
            moves.append((part, begin, piece, to, run))
            begin, column = begin + run, column + run
    return moves


def pack_body(*refs, places, chunk, slabs, passed, counts):
    count_flags, count_seen, count_parts, count_after = counts
    flag, targets = refs[:2] if count_flags else (None, None)
    refs = refs[count_flags:]
    state = refs[0:3]
    seen = refs[3 : 3 + count_seen]
    rest = refs[3 + count_seen :]
    if count_parts:
        both, parts, rest = rest[0], rest[1 : 1 + count_parts], rest[1 + count_parts :]
    sends = rest[count_after : count_after + 2]
    held, made, sem, out_sem, below_sem = rest[count_after + 2 :]
    width = held.shape[2]
    size = 3 * chunk

    def fetch(j):
        way, k = divmod(j, 3)
        rows = pl.ds(places[way] * chunk, chunk)
        return pltpu.make_async_copy(state[k].at[1, rows], held.at[j], sem.at[j])

    def store(j):
        way, k = divmod(j, 3)
        rows = pl.ds(k * chunk, chunk)
        return pltpu.make_async_copy(
            made.at[way, rows], sends[way].at[rows], out_sem.at[j]
        )

    def convert():
        for j in range(6):
            fetch(j).start()
        for j in range(6):
            way, k = divmod(j, 3)
            fetch(j).wait()
            made[way, pl.ds(k * chunk, chunk)] = held[j].astype(BF16)
            store(j).start()
        for j in range(6):
            store(j).wait()

    def relay(way):
        rows = pl.ds(0, size)
        return pltpu.make_async_copy(seen[way].at[rows], sends[way].at[rows], sem.at[way])

    def below(way):
        count = passed[way] or sends[way].shape[0] - size
        rows = pl.ds(size, count)
        origin = seen[way].at[rows] if passed[way] else made.at[way, rows]
        return pltpu.make_async_copy(origin, sends[way].at[rows], below_sem.at[way])

    for way in range(2):
        if slabs[way]:
            n = targets.shape[0]
            tokens, features = both.shape[0], both.shape[1] // 2
            keep = flag[1] == 0
            moves = column_pieces([part.shape[1] for part in parts], width)
            for part, begin, piece, to, run in moves:
                units = parts[part][:, begin : begin + run]
                made[way, pl.ds(size + piece * tokens, tokens), pl.ds(to, run)] = (
                    jnp.where(keep, units, jnp.zeros_like(units))
                )
            row = size + (1 + moves[-1][2]) * tokens
            for far in range(slabs[way], 0, -1):
                target = targets[far if way == 0 else n - far]
                slab = pl.ds(pl.multiple_of(features + target * width, 128), width)
                made[way, pl.ds(row, tokens)] = both[:, slab]
                row += tokens
        if slabs[way] or passed[way]:
            below(way).start()

    if not seen:
        convert()
    else:
        pl.when(flag[0] == 1)(convert)

        @pl.when(flag[0] == 0)
        def _():
            for way in range(2):
                relay(way).start()
            for way in range(2):
                relay(way).wait()

    for way in range(2):
        if slabs[way] or passed[way]:
            below(way).wait()


def pack(flags, state, seen, parcel, after, places, chunk, slabs, passed):
    width = state[0].shape[2]
    extra = list(passed)
    if parcel:
        tokens = parcel[0].shape[0]
        pieces = -(-sum(part.shape[1] for part in parcel[1:]) // width)
        extra = [tokens * (pieces + count) if count else 0 for count in slabs]
    counts = (len(flags), len(seen), max(len(parcel) - 1, 0), len(after))
    return pl.pallas_call(
        functools.partial(
            pack_body, places=places, chunk=chunk, slabs=slabs, passed=passed, counts=counts
        ),
        in_specs=[SMEM] * len(flags)
        + [ANY] * (3 + len(seen))
        + [WHOLE] * len(parcel)
        + [ANY] * len(after),
        out_specs=[ANY, ANY],
        out_shape=[
            jax.ShapeDtypeStruct((3 * chunk + more, width), BF16) for more in extra
        ],
        scratch_shapes=[
            pltpu.VMEM((6, chunk, width), F32),
            pltpu.VMEM((2, 3 * chunk + max(extra), width), BF16),
            pltpu.SemaphoreType.DMA((6,)),
            pltpu.SemaphoreType.DMA((6,)),
            pltpu.SemaphoreType.DMA((2,)),
        ],
        compiler_params=PARAMS,
        cost_estimate=cost(0, 2 * 3 * chunk * width * 6),
        name="pack",
    )(*flags, *state, *seen, *parcel, *after)


def beside_body(*refs):
    tokens, d_out, out = refs[0], refs[1], refs[-1]
    width = tokens.shape[1]
    out[:, :width] = tokens[...]
    out[:, width:] = d_out[...]


def beside(tokens, d_out, after):
    rows, width = tokens.shape
    return pl.pallas_call(
        beside_body,
        in_specs=[WHOLE, WHOLE] + [ANY] * len(after),
        out_specs=WHOLE,
        out_shape=jax.ShapeDtypeStruct((rows, 2 * width), tokens.dtype),
        compiler_params=PARAMS,
        cost_estimate=cost(0, 4 * rows * width * 2),
        name="beside",
    )(tokens, d_out, *after)


def by_rows(a, b):
    return lax.dot_general(a, b, (((1,), (1,)), ((), ())), preferred_element_type=F32)


def layer_body(both, *refs, resumed, tile, first, count):
    weights = refs[:3]
    hidden_ref, sum_ref = refs[-2:]
    features = weights[0].shape[0]
    rows = both.shape[0]
    joined = tile % 128 == 0
    sum_ref[...] = refs[3][...] if resumed else jnp.zeros_like(sum_ref)

    def step(gate_ref, up_ref, down_ref, hidden):
        x, dy = both[:, :features], both[:, features:]
        w_gate, w_up = gate_ref[...], up_ref[...]
        if joined:
            w_both = jnp.concatenate([w_gate, w_up], axis=1)
            gate_up = jnp.dot(x, w_both, preferred_element_type=F32)
            gate, up = gate_up[:, :tile], gate_up[:, tile:]
        else:
            gate = jnp.dot(x, w_gate, preferred_element_type=F32)
            up = jnp.dot(x, w_up, preferred_element_type=F32)
        d_hidden = by_rows(dy, down_ref[...])
        sig = 1.0 / (1.0 + jnp.exp(-gate))
        hidden[...] = (gate * sig * up).astype(BF16)
        d_gate = (d_hidden * up * sig * (1.0 + gate * (1.0 - sig))).astype(BF16)
        d_up = (d_hidden * gate * sig).astype(BF16)
        if joined:
            sum_ref[...] += by_rows(jnp.concatenate([d_gate, d_up], axis=1), w_both)
        else:
            sum_ref[...] += by_rows(d_gate, w_gate) + by_rows(d_up, w_up)

    deep = pl.Buffered(min(BUFFERS, count + 1))
    across = pl.BlockSpec((features, tile), lambda i: (0, first + i), pipeline_mode=deep)
    pltpu.emit_pipeline(
        step,
        grid=(count,),
        in_specs=[
            across,
            across,
            pl.BlockSpec((tile, features), lambda i: (first + i, 0), pipeline_mode=deep),
        ],
        out_specs=[pl.BlockSpec((rows, tile), lambda i: (0, i))],
    )(*weights, hidden_ref)


def layer(both, w_gate, w_up, w_down, partial_sum, after, tile, first, count):
    rows = both.shape[0]
    features = w_gate.shape[0]
    resumed = partial_sum is not None
    return pl.pallas_call(
        functools.partial(layer_body, resumed=resumed, tile=tile, first=first, count=count),
        in_specs=[WHOLE] + [ANY] * 3 + [WHOLE] * resumed + [ANY] * len(after),
        out_specs=[ANY, WHOLE],
        out_shape=[
            jax.ShapeDtypeStruct((rows, count * tile), BF16),
            jax.ShapeDtypeStruct((rows, features), F32),
        ],
        compiler_params=PARAMS,
        cost_estimate=cost(
            10 * rows * features * count * tile,
            3 * features * count * tile * 2,
            rows * count * tile,
        ),
        name="layer",
    )(both, w_gate, w_up, w_down, *([partial_sum] if resumed else []), *after)


def halve_body(bit, *refs, arrived, final):
    value = refs[0][...]
    if arrived:
        value = value + refs[1][...]
    if final:
        refs[-1][...] = value.astype(BF16)
        return
    kept, sent = refs[-2:]
    half = value.shape[0] // 2
    low, high = value[:half], value[half:]
    upper = bit[0] == 1
    kept[...] = jnp.where(upper, high, low)
    sent[...] = jnp.where(upper, low, high)


def halve(bit, value, arrived, after, final):
    rows, features = value.shape
    if final:
        out_shape = jax.ShapeDtypeStruct((rows, features), BF16)
    else:
        out_shape = [jax.ShapeDtypeStruct((rows // 2, features), F32)] * 2
    return pl.pallas_call(
        functools.partial(halve_body, arrived=bool(arrived), final=final),
        in_specs=[SMEM] + [WHOLE] * (1 + len(arrived)) + [ANY] * len(after),
        out_specs=WHOLE if final else [WHOLE, WHOLE],
        out_shape=out_shape,
        compiler_params=PARAMS,
        cost_estimate=cost(0, 3 * rows * features * 4),
        name="halve",
    )(bit, value, *arrived, *after)


class ScatteredSum:
    def __init__(self, value, axes):
        sizes = [lax.axis_size(axis) for axis in axes]
        self.value, self.arrived, self.levels = value, (), []
        self.done = any(size & (size - 1) for size in sizes)
        if self.done:
            summed = lax.psum_scatter(value, axes, scatter_dimension=0, tiled=True)
            self.value = summed.astype(BF16)
            return
        for axis, size in zip(axes, sizes):
            apart = size // 2
            while apart:
                self.levels.append((axis, size, apart))
                apart //= 2

    def advance(self, after):
        if self.done:
            return ()
        if self.levels:
            axis, size, apart = self.levels.pop(0)
            bit = ((lax.axis_index(axis) // apart) % 2).astype(jnp.int32)[None]
            self.value, sent = halve(bit, self.value, self.arrived, after, False)
            route = [(i, i ^ apart) for i in range(size)]
            self.arrived = (lax.ppermute(sent, axis, route),)
        else:
            bit = jnp.zeros((1,), jnp.int32)
            self.value = halve(bit, self.value, self.arrived, after, True)
            self.done = True
        return (self.value,)


def collect_body(flag, targets, both, *refs, places, parts_count, size, pieces):
    parts = refs[:parts_count]
    blocks = refs[parts_count : parts_count + len(places)]
    hidden_t, outs, held, sem = refs[-4:]
    tokens, features = both.shape[0], both.shape[1] // 2
    width = outs.shape[1]

    def fetch(j, part):
        rows = pl.ds(size, pieces * tokens) if part == 0 else pl.ds(places[j], tokens)
        here = pl.ds(0, pieces * tokens) if part == 0 else pl.ds(pieces * tokens, tokens)
        return pltpu.make_async_copy(
            blocks[j].at[rows], held.at[j + 1, here], sem.at[j, part]
        )

    for j in range(len(places)):
        for part in range(2):
            fetch(j, part).start()
    keep = flag[1] == 0
    for part, begin, piece, to, run in column_pieces([p.shape[1] for p in parts], width):
        units = parts[part][:, begin : begin + run]
        held[0, pl.ds(piece * tokens, tokens), pl.ds(to, run)] = jnp.where(
            keep, units, jnp.zeros_like(units)
        )
    slab = pl.ds(pl.multiple_of(features + targets[0] * width, 128), width)
    held[0, pl.ds(pieces * tokens, tokens)] = both[:, slab]
    for j in range(len(places)):
        for part in range(2):
            fetch(j, part).wait()

    count = len(places) + 1
    for j in range(count):
        outs[pl.ds(j * tokens, tokens)] = held[j, pl.ds(pieces * tokens, tokens)]
    for piece in range(pieces):
        run = min(width, hidden_t.shape[0] - piece * width)
        rows = pl.ds(piece * tokens, tokens)
        hidden = jnp.concatenate([held[j, rows, :run] for j in range(count)], axis=0)
        hidden_t[pl.ds(piece * width, run)] = hidden.astype(F32).T.astype(BF16)


def collect(flag, targets, both, parts, blocks, places, size, width, after):
    tokens = both.shape[0]
    units = sum(part.shape[1] for part in parts)
    pieces = -(-units // width)
    depth = tokens * (len(blocks) + 1)
    return pl.pallas_call(
        functools.partial(
            collect_body,
            places=places,
            parts_count=len(parts),
            size=size,
            pieces=pieces,
        ),
        in_specs=[SMEM, SMEM]
        + [WHOLE] * (1 + len(parts))
        + [ANY] * (len(blocks) + len(after)),
        out_specs=[WHOLE, WHOLE],
        out_shape=[
            jax.ShapeDtypeStruct((units, depth), BF16),
            jax.ShapeDtypeStruct((depth, width), BF16),
        ],
        scratch_shapes=[
            pltpu.VMEM((len(blocks) + 1, (pieces + 1) * tokens, width), BF16),
            pltpu.SemaphoreType.DMA((len(blocks), 2)),
        ],
        compiler_params=PARAMS,
        cost_estimate=cost(0, 4 * depth * (units + width)),
        name="collect",
    )(flag, targets, both, *parts, *blocks, *after)


def update_body(info, hid_ref, out_ref, *refs, healthy, block, first, count, unread):
    state, news = refs[:3], refs[3 + unread : 6 + unread]
    total = refs[6 + unread]
    width = out_ref.shape[1]
    group = row_group(block)

    def step(hid, m_ref, a_ref, b_ref, m_new, a_new, b_new):
        total[...] = jnp.dot(hid[...], out_ref[...], preferred_element_type=F32)

        @pl.loop(0, block // group)
        def _(i):
            here = pl.ds(pl.multiple_of(i * group, group), group)
            m_new[here], a_new[here], b_new[here] = updated(
                m_ref[0, here], a_ref[0, here], b_ref[0, here], total[here], healthy
            )

    deep = pl.Buffered(min(BUFFERS, count + 1))
    old = pl.BlockSpec(
        (1, block, width), lambda i: (0, first + i, 0), pipeline_mode=deep
    )
    new = pl.BlockSpec((block, width), lambda i: (first + i, 0))

    @pl.when(info[0] == 0)
    def _():
        pltpu.emit_pipeline(
            step,
            grid=(count,),
            in_specs=[
                pl.BlockSpec((block, hid_ref.shape[1]), lambda i: (first + i, 0)),
                old,
                old,
                old,
            ],
            out_specs=[new] * 3,
        )(hid_ref, *state, *news)


def update(info, hidden_t, outs, state, news, after, healthy, block, first, count):
    _, rows, width = state[0].shape
    depth = hidden_t.shape[1]
    shape = jax.ShapeDtypeStruct((rows, width), F32)
    unread = len(news) + len(after)
    return pl.pallas_call(
        functools.partial(
            update_body,
            healthy=healthy,
            block=block,
            first=first,
            count=count,
            unread=unread,
        ),
        in_specs=[SMEM, ANY, WHOLE] + [ANY] * (3 + unread),
        out_specs=[ANY] * 3,
        out_shape=[shape] * 3,
        scratch_shapes=[pltpu.VMEM((block, width), F32)],
        input_output_aliases={6 + k: k for k in range(len(news))},
        compiler_params=PARAMS,
        cost_estimate=cost(
            2 * count * block * width * depth,
            6 * count * block * width * 4,
            2 * count * block * width,
        ),
        name="update",
    )(info, hidden_t, outs, *state, *news, *after)


def patch_body(info, hid_ref, out_ref, *refs, arrivals, chunks, n, count_after):
    count = len(arrivals)
    got = refs[:count]
    rest = refs[count + 3 + count_after :]
    news = rest[:3]
    held, made, total, in_sem, out_sem = rest[3:]
    chunk = made.shape[2]
    group = row_group(chunk)
    ahead = info[1]
    lag_of = {True: LAG * (ahead - 1), False: LAG * (n - ahead - 1)}

    def fetch(j):
        rows = got[j].at[pl.ds(0, 3 * chunk)]
        return pltpu.make_async_copy(rows, held.at[j % FETCHED], in_sem.at[j % FETCHED])

    def first_row(j):
        step, forward = arrivals[j]
        place = step - lag_of[forward]
        if not forward:
            place = chunks - 1 - place
        return pl.multiple_of(jnp.clip(place, 0, chunks - 1) * chunk, TILE)

    def store(j, k):
        return pltpu.make_async_copy(
            made.at[j % BUFFERS, k],
            news[k].at[pl.ds(first_row(j), chunk)],
            out_sem.at[j % BUFFERS, k],
        )

    def valid(j):
        step, forward = arrivals[j]
        return step >= lag_of[forward]

    def finish(j):
        @pl.when(valid(j))
        def _():
            for k in range(3):
                store(j, k).wait()

    @pl.when(info[0] == 1)
    def _():
        for j in range(min(FETCHED - 1, count)):
            fetch(j).start()
        for j in range(count):
            if j + FETCHED - 1 < count:
                fetch(j + FETCHED - 1).start()
            fetch(j).wait()
            if j >= BUFFERS:
                finish(j - BUFFERS)

            @pl.when(valid(j))
            def _(j=j, slot=j % FETCHED, out_slot=j % BUFFERS):
                first = first_row(j)

                units = hid_ref[pl.ds(first, chunk)]
                total[...] = jnp.dot(units, out_ref[...], preferred_element_type=F32)

                @pl.loop(0, chunk // group)
                def _(i):
                    base = pl.multiple_of(i * group, group)
                    old = [
                        held[slot, pl.ds(k * chunk + base, group)].astype(F32)
                        for k in range(3)
                    ]
                    new = updated(*old, total[pl.ds(base, group)], n - 1.0)
                    for k in range(3):
                        made[out_slot, k, pl.ds(base, group)] = new[k]

                for k in range(3):
                    store(j, k).start()

        for j in range(max(count - BUFFERS, 0), count):
            finish(j)


def patch(info, hidden_t, outs, got, arrivals, news, after, chunks, n):
    rows, width = news[0].shape
    chunk = rows // chunks
    count = len(got)
    shape = jax.ShapeDtypeStruct((rows, width), F32)
    return pl.pallas_call(
        functools.partial(
            patch_body, arrivals=arrivals, chunks=chunks, n=n, count_after=len(after)
        ),
        in_specs=[SMEM, WHOLE, WHOLE] + [ANY] * (count + 3 + len(after)),
        out_specs=[ANY] * 3,
        out_shape=[shape] * 3,
        scratch_shapes=[
            pltpu.VMEM((FETCHED, 3 * chunk, width), BF16),
            pltpu.VMEM((BUFFERS, 3, chunk, width), F32),
            pltpu.VMEM((chunk, width), F32),
            pltpu.SemaphoreType.DMA((FETCHED,)),
            pltpu.SemaphoreType.DMA((BUFFERS, 3)),
        ],
        input_output_aliases={3 + count + k: k for k in range(3)},
        compiler_params=PARAMS,
        cost_estimate=cost(
            2 * count * chunk * width * hidden_t.shape[1],
            count * 3 * chunk * width * 6,
            2 * count * chunk * width,
        ),
        name="patch",
    )(info, hidden_t, outs, *got, *news, *after)


def per_device(tokens, d_out, w_gate, w_up, w_down, failed, master, moment1, moment2):
    n = lax.axis_size("replica")
    me = lax.axis_index("replica")
    _, rows, width = master.shape
    features, units = w_gate.shape

    failed_id = failed[0]
    source = (failed_id + 1) % n
    order = ring_order(n)
    place = jnp.array([order.index(i) for i in range(n)], jnp.int32)
    ahead = (place[failed_id] - place[source]) % n
    lost = (me == failed_id).astype(jnp.int32)
    flag = jnp.stack([(me == source).astype(jnp.int32), lost])
    info = jnp.stack([lost, ahead.astype(jnp.int32)])
    targets = jnp.array(order, jnp.int32)[(place[me] + jnp.arange(n)) % n]

    state = (master, moment1, moment2)
    chunks = largest(
        (c for c in range(2, MOST_CHUNKS + 1, 2) if rows % (TILE * c) == 0), 2
    )
    chunk = rows // chunks
    steps = (chunks + LAG * (n - 2)) // 2
    reach = (n // 2, (n - 1) // 2)
    forward = [(order[p], order[(p + 1) % n]) for p in range(n)]
    backward = [(b, a) for a, b in forward]
    sends, got = [], []
    parcel_from = None

    def send(*after, parcel=()):
        nonlocal parcel_from
        step = len(got)
        seen = got[step - LAG] if step >= LAG else ()
        here = min(step, chunks - 1)
        slabs, passed = (0, 0), (0, 0)
        if parcel:
            parcel_from, slabs = step, reach
        elif parcel_from is not None and (step - parcel_from) % LAG == 0:
            hop = (step - parcel_from) // LAG
            passed = tuple(
                seen[way].shape[0] - 3 * chunk - both.shape[0]
                if hop < reach[way]
                else 0
                for way in range(2)
            )
        sends.append(
            pack(
                (flag, targets) if seen else (),
                state,
                seen,
                parcel,
                after,
                (here, chunks - 1 - here),
                chunk,
                slabs,
                passed,
            )
        )
        got.append(
            (
                lax.ppermute(sends[-1][0], "replica", forward),
                lax.ppermute(sends[-1][1], "replica", backward),
            )
        )
        return (sends[-1][0],)

    sent = send()
    sent = send(*sent)
    both = beside(tokens[0], d_out[0], sent)
    both = lax.all_gather(both, ("fsdp", "tensor"), axis=0, tiled=True)
    sent = send(both)

    tile = 128 if units % 128 == 0 else units
    hidden, d_rows = [], None
    pieces = shares(units // tile, 4)
    for first, count in pieces:
        part, d_rows = layer(both, w_gate, w_up, w_down, d_rows, sent, tile, first, count)
        hidden.append(part)
        last = len(hidden) == len(pieces)
        sent = send(d_rows, parcel=(both, *hidden) if last else ())
    cotangents = ScatteredSum(d_rows, ("fsdp", "tensor"))

    news = ()
    patched = 0
    hidden_t = outs = None

    def gathered(after):
        blocks, places = [], []
        for way in range(2):
            for hop in range(reach[way]):
                blocks.append(got[parcel_from + LAG * hop][way])
                places.append(blocks[-1].shape[0] - both.shape[0])
        return collect(
            flag, targets, both, hidden, blocks, places, 3 * chunk, width, after
        )

    def update_part(first, count, after):
        return update(
            info, hidden_t, outs, state, news, after, n - 1.0, block, first, count
        )

    def patch_to(step, after):
        nonlocal patched
        arrivals = [(s, way) for s in range(patched, step) for way in (True, False)]
        if not arrivals:
            return news
        blocks = [b for s in range(patched, step) for b in got[s]]
        patched = step
        return patch(info, hidden_t, outs, blocks, arrivals, news, after, chunks, n)

    block = largest((b for b in range(TILE, 193, TILE) if rows % b == 0), rows)
    blocks = rows // block
    early = blocks // 4
    ready = parcel_from + LAG * reach[0] + 1
    while len(got) < steps:
        sent = send(*cotangents.advance(sent), *news[:1])
        if len(got) == ready and early and len(got) < steps:
            hidden_t, outs = gathered(sent)
            news = update_part(0, early, (hidden_t,))
            news = patch_to(len(got) // 2, ())
    if hidden_t is None:
        hidden_t, outs = gathered(sent)
        early = 0
    news = update_part(early, blocks - early, sent)
    for step in (steps - 2, steps - 1, steps):
        news = patch_to(step, ())
    while not cotangents.done:
        cotangents.advance(sent)
    return (cotangents.value[None], *news)


def solution(mesh):
    placed = (
        P("replica", ("fsdp", "tensor"), None),
        P("replica", ("fsdp", "tensor"), None),
        P(None, ("fsdp", "tensor")),
        P(None, ("fsdp", "tensor")),
        P(("fsdp", "tensor"), None),
        P(("fsdp", "tensor")),
        P(None, ("fsdp", "tensor"), "replica"),
        P(None, ("fsdp", "tensor"), "replica"),
        P(None, ("fsdp", "tensor"), "replica"),
    )
    return jax.shard_map(
        per_device,
        mesh=mesh,
        in_specs=placed,
        out_specs=(
            P("replica", ("fsdp", "tensor"), None),
            P(("fsdp", "tensor"), "replica"),
            P(("fsdp", "tensor"), "replica"),
            P(("fsdp", "tensor"), "replica"),
        ),
        check_vma=False,
    )
```

```python
import functools

import jax
import jax.numpy as jnp
from jax import lax
from jax.experimental import pallas as pl
from jax.experimental.pallas import tpu as pltpu
from jax.sharding import PartitionSpec as P

BF16, F32 = jnp.bfloat16, jnp.float32
LAG = 2
MOST_CHUNKS = 20
TILE = 16
BUFFERS = 3
FETCHED = 4
VMEM = 48 << 20

ANY = pl.BlockSpec(memory_space=pl.ANY)
SMEM = pl.BlockSpec(memory_space=pltpu.SMEM)
WHOLE = pl.BlockSpec(memory_space=pltpu.VMEM)
PARAMS = pltpu.CompilerParams(vmem_limit_bytes=VMEM)


def ring_order(n):
    return [0, 1, 3, 2] if n == 4 else list(range(n))


def entry(table, index):
    found = jnp.int32(0)
    for at, value in enumerate(table):
        found = jnp.where(index == at, jnp.int32(value), found)
    return found


class Roles:
    def __init__(self, failed, n):
        self.n = n
        self.order = ring_order(n)
        self.spots = [self.order.index(i) for i in range(n)]
        self.me = lax.axis_index("replica").astype(jnp.int32)
        self.failed = failed[0]
        self.source = lax.rem(self.failed + 1, n)
        self.lost = self.me == self.failed

    def ahead(self):
        apart = entry(self.spots, self.failed) - entry(self.spots, self.source)
        return lax.rem(apart + self.n, self.n)

    def neighbour(self, hops):
        spot = lax.rem(entry(self.spots, self.me) + hops, self.n)
        return entry(self.order, spot)


def largest(options, default):
    options = list(options)
    return max(options) if options else default


def shares(total, parts):
    parts = min(parts, total)
    edges = [total * i // parts for i in range(parts + 1)]
    return [(a, b - a) for a, b in zip(edges, edges[1:])]


def row_group(rows):
    return largest((g for g in (16, 32) if rows % g == 0), rows)


def cost(flops, bytes_accessed, transcendentals=0):
    return pl.CostEstimate(
        flops=flops, bytes_accessed=bytes_accessed, transcendentals=transcendentals
    )


def updated(master_old, first_old, second_old, total, healthy):
    first_new = 0.9 * first_old + (0.1 / healthy) * total
    second_new = 0.95 * second_old + (0.05 / healthy**2) * (total * total)
    root = second_new * lax.rsqrt(second_new)
    step = first_new * pl.reciprocal(root + 1e-08)
    return master_old - 0.01 * step, first_new, second_new


def column_pieces(lengths, width):
    moves, column = [], 0
    for part, length in enumerate(lengths):
        begin = 0
        while begin < length:
            piece, to = divmod(column, width)
            run = min(length - begin, width - to)
            moves.append((part, begin, piece, to, run))
            begin, column = begin + run, column + run
    return moves


def pack_body(*refs, n, places, chunk, slabs, passed, counts):
    count_seen, count_parts, count_after = counts
    if count_seen:
        roles, refs = Roles(refs[0], n), refs[1:]
    state = refs[0:3]
    seen = refs[3 : 3 + count_seen]
    rest = refs[3 + count_seen :]
    if count_parts:
        both, parts, rest = rest[0], rest[1 : 1 + count_parts], rest[1 + count_parts :]
    sends = rest[count_after : count_after + 2]
    held, made, sem, out_sem, below_sem = rest[count_after + 2 :]
    width = held.shape[2]
    size = 3 * chunk

    def rows_of(j):
        way, k = divmod(j, 3)
        return way, pl.ds(k * chunk, chunk)

    def fetch(j):
        way, k = divmod(j, 3)
        rows = pl.ds(places[way] * chunk, chunk)
        return pltpu.make_async_copy(state[k].at[1, rows], held.at[j], sem.at[j])

    def take(j):
        way, rows = rows_of(j)
        return pltpu.make_async_copy(seen[way].at[rows], made.at[way, rows], sem.at[j])

    def store(j):
        way, rows = rows_of(j)
        return pltpu.make_async_copy(
            made.at[way, rows], sends[way].at[rows], out_sem.at[j]
        )

    def convert():
        for j in range(6):
            fetch(j).start()
        for j in range(6):
            way, rows = rows_of(j)
            fetch(j).wait()
            made[way, rows] = held[j].astype(BF16)
            store(j).start()
        for j in range(6):
            store(j).wait()

    def relay():
        for j in range(6):
            take(j).start()
        for j in range(6):
            take(j).wait()
            store(j).start()
        for j in range(6):
            store(j).wait()

    def below(way, inward):
        rows = pl.ds(size, passed[way] or sends[way].shape[0] - size)
        here = made.at[way, rows]
        if inward:
            return pltpu.make_async_copy(seen[way].at[rows], here, below_sem.at[way])
        return pltpu.make_async_copy(here, sends[way].at[rows], below_sem.at[way])

    for way in range(2):
        if passed[way]:
            below(way, True).start()
        if slabs[way]:
            tokens, features = both.shape[0], both.shape[1] // 2
            moves = column_pieces([part.shape[1] for part in parts], width)
            for part, begin, piece, to, run in moves:
                units = parts[part][:, begin : begin + run]
                made[way, pl.ds(size + piece * tokens, tokens), pl.ds(to, run)] = (
                    jnp.where(roles.lost, jnp.zeros_like(units), units)
                )
            row = size + (1 + moves[-1][2]) * tokens
            for far in range(slabs[way], 0, -1):
                target = roles.neighbour(far if way == 0 else n - far)
                slab = pl.ds(pl.multiple_of(features + target * width, 128), width)
                made[way, pl.ds(row, tokens)] = both[:, slab]
                row += tokens
            below(way, False).start()

    for way in range(2):
        if passed[way]:
            below(way, True).wait()
            below(way, False).start()

    if seen:
        pl.when(roles.me == roles.source)(convert)
        pl.when(roles.me != roles.source)(relay)
    else:
        convert()

    for way in range(2):
        if slabs[way] or passed[way]:
            below(way, False).wait()


def pack(failed, n, state, seen, parcel, after, places, chunk, slabs, passed):
    width = state[0].shape[2]
    extra = list(passed)
    if parcel:
        tokens = parcel[0].shape[0]
        pieces = -(-sum(part.shape[1] for part in parcel[1:]) // width)
        extra = [tokens * (pieces + count) if count else 0 for count in slabs]
    counts = (len(seen), max(len(parcel) - 1, 0), len(after))
    return pl.pallas_call(
        functools.partial(
            pack_body,
            n=n,
            places=places,
            chunk=chunk,
            slabs=slabs,
            passed=passed,
            counts=counts,
        ),
        in_specs=[SMEM] * bool(seen)
        + [ANY] * (3 + len(seen))
        + [WHOLE] * len(parcel)
        + [ANY] * len(after),
        out_specs=[ANY, ANY],
        out_shape=[
            jax.ShapeDtypeStruct((3 * chunk + more, width), BF16) for more in extra
        ],
        scratch_shapes=[
            pltpu.VMEM((6, chunk, width), F32),
            pltpu.VMEM((2, 3 * chunk + max(extra), width), BF16),
            pltpu.SemaphoreType.DMA((6,)),
            pltpu.SemaphoreType.DMA((6,)),
            pltpu.SemaphoreType.DMA((2,)),
        ],
        compiler_params=PARAMS,
        cost_estimate=cost(0, 2 * 3 * chunk * width * 6),
        name="pack",
    )(*([failed] if seen else []), *state, *seen, *parcel, *after)


def beside_body(*refs):
    tokens, d_out, out = refs[0], refs[1], refs[-1]
    width = tokens.shape[1]
    out[:, :width] = tokens[...]
    out[:, width:] = d_out[...]


def beside(tokens, d_out, after):
    rows, width = tokens.shape
    return pl.pallas_call(
        beside_body,
        in_specs=[WHOLE, WHOLE] + [ANY] * len(after),
        out_specs=WHOLE,
        out_shape=jax.ShapeDtypeStruct((rows, 2 * width), tokens.dtype),
        compiler_params=PARAMS,
        cost_estimate=cost(0, 4 * rows * width * 2),
        name="beside",
    )(tokens, d_out, *after)


def by_rows(a, b):
    return lax.dot_general(a, b, (((1,), (1,)), ((), ())), preferred_element_type=F32)


def layer_body(both, *refs, resumed, tile, first, count):
    weights = refs[:3]
    hidden_ref, sum_ref = refs[-2:]
    features = weights[0].shape[0]
    rows = both.shape[0]
    joined = tile % 128 == 0
    sum_ref[...] = refs[3][...] if resumed else jnp.zeros_like(sum_ref)

    def step(gate_ref, up_ref, down_ref, hidden):
        x, dy = both[:, :features], both[:, features:]
        w_gate, w_up = gate_ref[...], up_ref[...]
        if joined:
            w_both = jnp.concatenate([w_gate, w_up], axis=1)
            gate_up = jnp.dot(x, w_both, preferred_element_type=F32)
            gate, up = gate_up[:, :tile], gate_up[:, tile:]
        else:
            gate = jnp.dot(x, w_gate, preferred_element_type=F32)
            up = jnp.dot(x, w_up, preferred_element_type=F32)
        d_hidden = by_rows(dy, down_ref[...])
        sig = 1.0 / (1.0 + jnp.exp(-gate))
        hidden[...] = (gate * sig * up).astype(BF16)
        d_gate = (d_hidden * up * sig * (1.0 + gate * (1.0 - sig))).astype(BF16)
        d_up = (d_hidden * gate * sig).astype(BF16)
        if joined:
            sum_ref[...] += by_rows(jnp.concatenate([d_gate, d_up], axis=1), w_both)
        else:
            sum_ref[...] += by_rows(d_gate, w_gate) + by_rows(d_up, w_up)

    deep = pl.Buffered(min(BUFFERS, count + 1))
    across = pl.BlockSpec((features, tile), lambda i: (0, first + i), pipeline_mode=deep)
    pltpu.emit_pipeline(
        step,
        grid=(count,),
        in_specs=[
            across,
            across,
            pl.BlockSpec((tile, features), lambda i: (first + i, 0), pipeline_mode=deep),
        ],
        out_specs=[pl.BlockSpec((rows, tile), lambda i: (0, i))],
    )(*weights, hidden_ref)


def layer(both, w_gate, w_up, w_down, partial_sum, after, tile, first, count):
    rows = both.shape[0]
    features = w_gate.shape[0]
    resumed = partial_sum is not None
    return pl.pallas_call(
        functools.partial(layer_body, resumed=resumed, tile=tile, first=first, count=count),
        in_specs=[WHOLE] + [ANY] * 3 + [WHOLE] * resumed + [ANY] * len(after),
        out_specs=[ANY, WHOLE],
        out_shape=[
            jax.ShapeDtypeStruct((rows, count * tile), BF16),
            jax.ShapeDtypeStruct((rows, features), F32),
        ],
        compiler_params=PARAMS,
        cost_estimate=cost(
            10 * rows * features * count * tile,
            3 * features * count * tile * 2,
            rows * count * tile,
        ),
        name="layer",
    )(both, w_gate, w_up, w_down, *([partial_sum] if resumed else []), *after)


def halve_body(bit, *refs, arrived, final):
    value = refs[0][...]
    if arrived:
        value = value + refs[1][...]
    if final:
        refs[-1][...] = value.astype(BF16)
        return
    kept, sent = refs[-2:]
    half = value.shape[0] // 2
    low, high = value[:half], value[half:]
    upper = bit[0] == 1
    kept[...] = jnp.where(upper, high, low)
    sent[...] = jnp.where(upper, low, high)


def halve(bit, value, arrived, after, final):
    rows, features = value.shape
    if final:
        out_shape = jax.ShapeDtypeStruct((rows, features), BF16)
    else:
        out_shape = [jax.ShapeDtypeStruct((rows // 2, features), F32)] * 2
    return pl.pallas_call(
        functools.partial(halve_body, arrived=bool(arrived), final=final),
        in_specs=[SMEM] + [WHOLE] * (1 + len(arrived)) + [ANY] * len(after),
        out_specs=WHOLE if final else [WHOLE, WHOLE],
        out_shape=out_shape,
        compiler_params=PARAMS,
        cost_estimate=cost(0, 3 * rows * features * 4),
        name="halve",
    )(bit, value, *arrived, *after)


class ScatteredSum:
    def __init__(self, value, axes):
        sizes = [lax.axis_size(axis) for axis in axes]
        self.value, self.arrived, self.levels = value, (), []
        self.done = any(size & (size - 1) for size in sizes)
        if self.done:
            summed = lax.psum_scatter(value, axes, scatter_dimension=0, tiled=True)
            self.value = summed.astype(BF16)
            return
        for axis, size in zip(axes, sizes):
            apart = size // 2
            while apart:
                self.levels.append((axis, size, apart))
                apart //= 2

    def advance(self, after):
        if self.done:
            return ()
        if self.levels:
            axis, size, apart = self.levels.pop(0)
            bit = ((lax.axis_index(axis) // apart) % 2).astype(jnp.int32)[None]
            self.value, sent = halve(bit, self.value, self.arrived, after, False)
            route = [(i, i ^ apart) for i in range(size)]
            self.arrived = (lax.ppermute(sent, axis, route),)
        else:
            bit = jnp.zeros((1,), jnp.int32)
            self.value = halve(bit, self.value, self.arrived, after, True)
            self.done = True
        return (self.value,)


def collect_body(failed, both, *refs, n, places, parts_count, size, pieces):
    roles = Roles(failed, n)
    parts = refs[:parts_count]
    blocks = refs[parts_count : parts_count + len(places)]
    hidden_t, outs, held, sem = refs[-4:]
    tokens, features = both.shape[0], both.shape[1] // 2
    width = outs.shape[1]

    def fetch(j, part):
        rows = pl.ds(size, pieces * tokens) if part == 0 else pl.ds(places[j], tokens)
        here = pl.ds(0, pieces * tokens) if part == 0 else pl.ds(pieces * tokens, tokens)
        return pltpu.make_async_copy(
            blocks[j].at[rows], held.at[j + 1, here], sem.at[j, part]
        )

    for j in range(len(places)):
        for part in range(2):
            fetch(j, part).start()
    for part, begin, piece, to, run in column_pieces([p.shape[1] for p in parts], width):
        units = parts[part][:, begin : begin + run]
        held[0, pl.ds(piece * tokens, tokens), pl.ds(to, run)] = jnp.where(
            roles.lost, jnp.zeros_like(units), units
        )
    slab = pl.ds(pl.multiple_of(features + roles.me * width, 128), width)
    held[0, pl.ds(pieces * tokens, tokens)] = both[:, slab]
    for j in range(len(places)):
        for part in range(2):
            fetch(j, part).wait()

    count = len(places) + 1
    for j in range(count):
        outs[pl.ds(j * tokens, tokens)] = held[j, pl.ds(pieces * tokens, tokens)]
    for piece in range(pieces):
        run = min(width, hidden_t.shape[0] - piece * width)
        rows = pl.ds(piece * tokens, tokens)
        hidden = jnp.concatenate([held[j, rows, :run] for j in range(count)], axis=0)
        hidden_t[pl.ds(piece * width, run)] = hidden.astype(F32).T.astype(BF16)


def collect(failed, n, both, parts, blocks, places, size, width, after):
    tokens = both.shape[0]
    units = sum(part.shape[1] for part in parts)
    pieces = -(-units // width)
    depth = tokens * (len(blocks) + 1)
    return pl.pallas_call(
        functools.partial(
            collect_body,
            n=n,
            places=places,
            parts_count=len(parts),
            size=size,
            pieces=pieces,
        ),
        in_specs=[SMEM]
        + [WHOLE] * (1 + len(parts))
        + [ANY] * (len(blocks) + len(after)),
        out_specs=[WHOLE, WHOLE],
        out_shape=[
            jax.ShapeDtypeStruct((units, depth), BF16),
            jax.ShapeDtypeStruct((depth, width), BF16),
        ],
        scratch_shapes=[
            pltpu.VMEM((len(blocks) + 1, (pieces + 1) * tokens, width), BF16),
            pltpu.SemaphoreType.DMA((len(blocks), 2)),
        ],
        compiler_params=PARAMS,
        cost_estimate=cost(0, 4 * depth * (units + width)),
        name="collect",
    )(failed, both, *parts, *blocks, *after)


def update_body(failed, hid_ref, out_ref, *refs, n, block, first, count, unread):
    state, news = refs[:3], refs[3 + unread : 6 + unread]
    total = refs[6 + unread]
    width = out_ref.shape[1]
    group = row_group(block)

    def step(hid, m_ref, a_ref, b_ref, m_new, a_new, b_new):
        total[...] = jnp.dot(hid[...], out_ref[...], preferred_element_type=F32)

        @pl.loop(0, block // group)
        def _(i):
            here = pl.ds(pl.multiple_of(i * group, group), group)
            m_new[here], a_new[here], b_new[here] = updated(
                m_ref[0, here], a_ref[0, here], b_ref[0, here], total[here], n - 1.0
            )

    deep = pl.Buffered(min(BUFFERS, count + 1))
    old = pl.BlockSpec(
        (1, block, width), lambda i: (0, first + i, 0), pipeline_mode=deep
    )
    new = pl.BlockSpec((block, width), lambda i: (first + i, 0))

    @pl.when(jnp.logical_not(Roles(failed, n).lost))
    def _():
        pltpu.emit_pipeline(
            step,
            grid=(count,),
            in_specs=[
                pl.BlockSpec((block, hid_ref.shape[1]), lambda i: (first + i, 0)),
                old,
                old,
                old,
            ],
            out_specs=[new] * 3,
        )(hid_ref, *state, *news)


def update(failed, n, hidden_t, outs, state, news, after, block, first, count):
    _, rows, width = state[0].shape
    depth = hidden_t.shape[1]
    shape = jax.ShapeDtypeStruct((rows, width), F32)
    unread = len(news) + len(after)
    return pl.pallas_call(
        functools.partial(
            update_body,
            n=n,
            block=block,
            first=first,
            count=count,
            unread=unread,
        ),
        in_specs=[SMEM, ANY, WHOLE] + [ANY] * (3 + unread),
        out_specs=[ANY] * 3,
        out_shape=[shape] * 3,
        scratch_shapes=[pltpu.VMEM((block, width), F32)],
        input_output_aliases={6 + k: k for k in range(len(news))},
        compiler_params=PARAMS,
        cost_estimate=cost(
            2 * count * block * width * depth,
            6 * count * block * width * 4,
            2 * count * block * width,
        ),
        name="update",
    )(failed, hidden_t, outs, *state, *news, *after)


def patch_body(failed, hid_ref, out_ref, *refs, arrivals, chunks, n, count_after):
    count = len(arrivals)
    got = refs[:count]
    rest = refs[count + 3 + count_after :]
    news = rest[:3]
    held, made, total, in_sem, out_sem = rest[3:]
    chunk = made.shape[2]
    group = row_group(chunk)
    roles = Roles(failed, n)
    ahead = roles.ahead()
    lag_of = {True: LAG * (ahead - 1), False: LAG * (n - ahead - 1)}

    def fetch(j):
        rows = got[j].at[pl.ds(0, 3 * chunk)]
        return pltpu.make_async_copy(rows, held.at[j % FETCHED], in_sem.at[j % FETCHED])

    def first_row(j):
        step, forward = arrivals[j]
        place = step - lag_of[forward]
        if not forward:
            place = chunks - 1 - place
        return pl.multiple_of(jnp.clip(place, 0, chunks - 1) * chunk, TILE)

    def store(j, k):
        return pltpu.make_async_copy(
            made.at[j % BUFFERS, k],
            news[k].at[pl.ds(first_row(j), chunk)],
            out_sem.at[j % BUFFERS, k],
        )

    def valid(j):
        step, forward = arrivals[j]
        return step >= lag_of[forward]

    def finish(j):
        @pl.when(valid(j))
        def _():
            for k in range(3):
                store(j, k).wait()

    @pl.when(roles.lost)
    def _():
        for j in range(min(FETCHED - 1, count)):
            fetch(j).start()
        for j in range(count):
            if j + FETCHED - 1 < count:
                fetch(j + FETCHED - 1).start()
            fetch(j).wait()
            if j >= BUFFERS:
                finish(j - BUFFERS)

            @pl.when(valid(j))
            def _(j=j, slot=j % FETCHED, out_slot=j % BUFFERS):
                first = first_row(j)

                units = hid_ref[pl.ds(first, chunk)]
                total[...] = jnp.dot(units, out_ref[...], preferred_element_type=F32)

                @pl.loop(0, chunk // group)
                def _(i):
                    base = pl.multiple_of(i * group, group)
                    old = [
                        held[slot, pl.ds(k * chunk + base, group)].astype(F32)
                        for k in range(3)
                    ]
                    new = updated(*old, total[pl.ds(base, group)], n - 1.0)
                    for k in range(3):
                        made[out_slot, k, pl.ds(base, group)] = new[k]

                for k in range(3):
                    store(j, k).start()

        for j in range(max(count - BUFFERS, 0), count):
            finish(j)


def patch(failed, n, hidden_t, outs, got, arrivals, news, after, chunks):
    rows, width = news[0].shape
    chunk = rows // chunks
    count = len(got)
    shape = jax.ShapeDtypeStruct((rows, width), F32)
    return pl.pallas_call(
        functools.partial(
            patch_body, arrivals=arrivals, chunks=chunks, n=n, count_after=len(after)
        ),
        in_specs=[SMEM, WHOLE, WHOLE] + [ANY] * (count + 3 + len(after)),
        out_specs=[ANY] * 3,
        out_shape=[shape] * 3,
        scratch_shapes=[
            pltpu.VMEM((FETCHED, 3 * chunk, width), BF16),
            pltpu.VMEM((BUFFERS, 3, chunk, width), F32),
            pltpu.VMEM((chunk, width), F32),
            pltpu.SemaphoreType.DMA((FETCHED,)),
            pltpu.SemaphoreType.DMA((BUFFERS, 3)),
        ],
        input_output_aliases={3 + count + k: k for k in range(3)},
        compiler_params=PARAMS,
        cost_estimate=cost(
            2 * count * chunk * width * hidden_t.shape[1],
            count * 3 * chunk * width * 6,
            2 * count * chunk * width,
        ),
        name="patch",
    )(failed, hidden_t, outs, *got, *news, *after)


def per_device(tokens, d_out, w_gate, w_up, w_down, failed, master, moment1, moment2):
    n = lax.axis_size("replica")
    _, rows, width = master.shape
    features, units = w_gate.shape

    order = ring_order(n)

    state = (master, moment1, moment2)
    chunks = largest(
        (c for c in range(2, MOST_CHUNKS + 1, 2) if rows % (TILE * c) == 0), 2
    )
    chunk = rows // chunks
    steps = (chunks + LAG * (n - 2)) // 2
    reach = (n // 2, (n - 1) // 2)
    forward = [(order[p], order[(p + 1) % n]) for p in range(n)]
    backward = [(b, a) for a, b in forward]
    sends, got = [], []
    parcel_from = None

    def send(*after, parcel=()):
        nonlocal parcel_from
        step = len(got)
        seen = got[step - LAG] if step >= LAG else ()
        here = min(step, chunks - 1)
        slabs, passed = (0, 0), (0, 0)
        if parcel:
            parcel_from, slabs = step, reach
        elif parcel_from is not None and (step - parcel_from) % LAG == 0:
            hop = (step - parcel_from) // LAG
            passed = tuple(
                seen[way].shape[0] - 3 * chunk - both.shape[0]
                if hop < reach[way]
                else 0
                for way in range(2)
            )
        sends.append(
            pack(
                failed,
                n,
                state,
                seen,
                parcel,
                after,
                (here, chunks - 1 - here),
                chunk,
                slabs,
                passed,
            )
        )
        got.append(
            (
                lax.ppermute(sends[-1][0], "replica", forward),
                lax.ppermute(sends[-1][1], "replica", backward),
            )
        )
        return (sends[-1][0],)

    sent = send()
    sent = send(*sent)
    both = beside(tokens[0], d_out[0], sent)
    both = lax.all_gather(both, ("fsdp", "tensor"), axis=0, tiled=True)
    sent = send(both)

    tile = 128 if units % 128 == 0 else units
    hidden, d_rows = [], None
    pieces = shares(units // tile, 4)
    for first, count in pieces:
        part, d_rows = layer(both, w_gate, w_up, w_down, d_rows, sent, tile, first, count)
        hidden.append(part)
        last = len(hidden) == len(pieces)
        sent = send(d_rows, parcel=(both, *hidden) if last else ())
    cotangents = ScatteredSum(d_rows, ("fsdp", "tensor"))

    news = ()
    patched = 0
    hidden_t = outs = None

    def gathered(after):
        blocks, places = [], []
        for way in range(2):
            for hop in range(reach[way]):
                blocks.append(got[parcel_from + LAG * hop][way])
                places.append(blocks[-1].shape[0] - both.shape[0])
        return collect(
            failed, n, both, hidden, blocks, places, 3 * chunk, width, after
        )

    def update_part(first, count, after):
        return update(
            failed, n, hidden_t, outs, state, news, after, block, first, count
        )

    def patch_to(step, after):
        nonlocal patched
        arrivals = [(s, way) for s in range(patched, step) for way in (True, False)]
        if not arrivals:
            return news
        blocks = [b for s in range(patched, step) for b in got[s]]
        patched = step
        return patch(failed, n, hidden_t, outs, blocks, arrivals, news, after, chunks)

    block = largest((b for b in range(TILE, 193, TILE) if rows % b == 0), rows)
    blocks = rows // block
    early = blocks // 4
    ready = parcel_from + LAG * reach[0] + 1
    while len(got) < steps:
        sent = send(*cotangents.advance(sent), *news[:1])
        if len(got) == ready and early and len(got) < steps:
            hidden_t, outs = gathered(sent)
            news = update_part(0, early, (hidden_t,))
            news = patch_to(len(got) // 2, ())
    if hidden_t is None:
        hidden_t, outs = gathered(sent)
        early = 0
    news = update_part(early, blocks - early, sent)
    for step in (steps - 2, steps - 1, steps):
        news = patch_to(step, ())
    while not cotangents.done:
        cotangents.advance(sent)
    return (cotangents.value[None], *news)


def solution(mesh):
    placed = (
        P("replica", ("fsdp", "tensor"), None),
        P("replica", ("fsdp", "tensor"), None),
        P(None, ("fsdp", "tensor")),
        P(None, ("fsdp", "tensor")),
        P(("fsdp", "tensor"), None),
        P(("fsdp", "tensor")),
        P(None, ("fsdp", "tensor"), "replica"),
        P(None, ("fsdp", "tensor"), "replica"),
        P(None, ("fsdp", "tensor"), "replica"),
    )
    return jax.shard_map(
        per_device,
        mesh=mesh,
        in_specs=placed,
        out_specs=(
            P("replica", ("fsdp", "tensor"), None),
            P(("fsdp", "tensor"), "replica"),
            P(("fsdp", "tensor"), "replica"),
            P(("fsdp", "tensor"), "replica"),
        ),
        check_vma=False,
    )
```

```python
import functools

import jax
import jax.numpy as jnp
from jax import lax
from jax.experimental import pallas as pl
from jax.experimental.pallas import tpu as pltpu
from jax.sharding import PartitionSpec as P

BF16, F32 = jnp.bfloat16, jnp.float32
LAG = 2
MOST_CHUNKS = 24
TILE = 16
BUFFERS = 3
FETCHED = 4
VMEM = 20 << 20

ANY = pl.BlockSpec(memory_space=pl.ANY)
SMEM = pl.BlockSpec(memory_space=pltpu.SMEM)
WHOLE = pl.BlockSpec(memory_space=pltpu.VMEM)
PARAMS = pltpu.CompilerParams(vmem_limit_bytes=VMEM)


def ring_order(n):
    return [0, 1, 3, 2] if n == 4 else list(range(n))


def entry(table, index):
    found = jnp.int32(0)
    for at, value in enumerate(table):
        found = jnp.where(index == at, jnp.int32(value), found)
    return found


class Roles:
    def __init__(self, failed, n):
        self.n = n
        self.order = ring_order(n)
        self.spots = [self.order.index(i) for i in range(n)]
        self.me = lax.axis_index("replica").astype(jnp.int32)
        self.failed = failed[0]
        self.source = lax.rem(self.failed + 1, n)
        self.lost = self.me == self.failed

    def ahead(self):
        apart = entry(self.spots, self.failed) - entry(self.spots, self.source)
        return lax.rem(apart + self.n, self.n)

    def neighbour(self, hops):
        spot = lax.rem(entry(self.spots, self.me) + hops, self.n)
        return entry(self.order, spot)


def largest(options, default):
    options = list(options)
    return max(options) if options else default


def shares(total, parts):
    parts = min(parts, total)
    edges = [total * i // parts for i in range(parts + 1)]
    return [(a, b - a) for a, b in zip(edges, edges[1:])]


def row_group(rows):
    return largest((g for g in (16, 32) if rows % g == 0), rows)


def cost(flops, bytes_accessed, transcendentals=0):
    return pl.CostEstimate(
        flops=flops, bytes_accessed=bytes_accessed, transcendentals=transcendentals
    )


def updated(master_old, first_old, second_old, total, healthy):
    first_new = 0.9 * first_old + (0.1 / healthy) * total
    second_new = 0.95 * second_old + (0.05 / healthy**2) * (total * total)
    root = second_new * lax.rsqrt(second_new)
    step = first_new * pl.reciprocal(root + 1e-08)
    return master_old - 0.01 * step, first_new, second_new


def column_pieces(lengths, width):
    moves, column = [], 0
    for part, length in enumerate(lengths):
        begin = 0
        while begin < length:
            piece, to = divmod(column, width)
            run = min(length - begin, width - to)
            moves.append((part, begin, piece, to, run))
            begin, column = begin + run, column + run
    return moves


def pack_body(*refs, n, places, chunk, slabs, passed, counts):
    count_seen, count_parts, count_after = counts
    if count_seen:
        roles, refs = Roles(refs[0], n), refs[1:]
    state = refs[0:3]
    seen = refs[3 : 3 + count_seen]
    rest = refs[3 + count_seen :]
    if count_parts:
        both, parts, rest = rest[0], rest[1 : 1 + count_parts], rest[1 + count_parts :]
    sends = rest[count_after : count_after + 2]
    held, made, sem, out_sem, below_sem = rest[count_after + 2 :]
    width = held.shape[2]
    size = 3 * chunk

    def rows_of(j):
        way, k = divmod(j, 3)
        return way, pl.ds(k * chunk, chunk)

    def fetch(j):
        way, k = divmod(j, 3)
        rows = pl.ds(places[way] * chunk, chunk)
        return pltpu.make_async_copy(state[k].at[1, rows], held.at[j], sem.at[j])

    def take(j):
        way, rows = rows_of(j)
        return pltpu.make_async_copy(seen[way].at[rows], made.at[way, rows], sem.at[j])

    def store(j):
        way, rows = rows_of(j)
        return pltpu.make_async_copy(
            made.at[way, rows], sends[way].at[rows], out_sem.at[j]
        )

    def convert():
        for j in range(6):
            fetch(j).start()
        for j in range(6):
            way, rows = rows_of(j)
            fetch(j).wait()
            made[way, rows] = held[j].astype(BF16)
            store(j).start()
        for j in range(6):
            store(j).wait()

    def relay():
        for j in range(6):
            take(j).start()
        for j in range(6):
            take(j).wait()
            store(j).start()
        for j in range(6):
            store(j).wait()

    def below(way, inward):
        rows = pl.ds(size, passed[way] or sends[way].shape[0] - size)
        here = made.at[way, rows]
        if inward:
            return pltpu.make_async_copy(seen[way].at[rows], here, below_sem.at[way])
        return pltpu.make_async_copy(here, sends[way].at[rows], below_sem.at[way])

    for way in range(2):
        if passed[way]:
            below(way, True).start()
        if slabs[way]:
            tokens, features = both.shape[0], both.shape[1] // 2
            moves = column_pieces([part.shape[1] for part in parts], width)
            for part, begin, piece, to, run in moves:
                units = parts[part][:, begin : begin + run]
                made[way, pl.ds(size + piece * tokens, tokens), pl.ds(to, run)] = (
                    jnp.where(roles.lost, jnp.zeros_like(units), units)
                )
            row = size + (1 + moves[-1][2]) * tokens
            for far in range(slabs[way], 0, -1):
                target = roles.neighbour(far if way == 0 else n - far)
                slab = pl.ds(pl.multiple_of(features + target * width, 128), width)
                made[way, pl.ds(row, tokens)] = both[:, slab]
                row += tokens
            below(way, False).start()

    for way in range(2):
        if passed[way]:
            below(way, True).wait()
            below(way, False).start()

    if seen:
        pl.when(roles.me == roles.source)(convert)
        pl.when(roles.me != roles.source)(relay)
    else:
        convert()

    for way in range(2):
        if slabs[way] or passed[way]:
            below(way, False).wait()


def pack(failed, n, state, seen, parcel, after, places, chunk, slabs, passed):
    width = state[0].shape[2]
    extra = list(passed)
    if parcel:
        tokens = parcel[0].shape[0]
        pieces = -(-sum(part.shape[1] for part in parcel[1:]) // width)
        extra = [tokens * (pieces + count) if count else 0 for count in slabs]
    counts = (len(seen), max(len(parcel) - 1, 0), len(after))
    return pl.pallas_call(
        functools.partial(
            pack_body,
            n=n,
            places=places,
            chunk=chunk,
            slabs=slabs,
            passed=passed,
            counts=counts,
        ),
        in_specs=[SMEM] * bool(seen)
        + [ANY] * (3 + len(seen))
        + [WHOLE] * len(parcel)
        + [ANY] * len(after),
        out_specs=[ANY, ANY],
        out_shape=[
            jax.ShapeDtypeStruct((3 * chunk + more, width), BF16) for more in extra
        ],
        scratch_shapes=[
            pltpu.VMEM((6, chunk, width), F32),
            pltpu.VMEM((2, 3 * chunk + max(extra), width), BF16),
            pltpu.SemaphoreType.DMA((6,)),
            pltpu.SemaphoreType.DMA((6,)),
            pltpu.SemaphoreType.DMA((2,)),
        ],
        compiler_params=PARAMS,
        cost_estimate=cost(0, 2 * 3 * chunk * width * 6),
        name="pack",
    )(*([failed] if seen else []), *state, *seen, *parcel, *after)


def beside_body(*refs):
    tokens, d_out, out = refs[0], refs[1], refs[-1]
    width = tokens.shape[1]
    out[:, :width] = tokens[...]
    out[:, width:] = d_out[...]


def beside(tokens, d_out, after):
    rows, width = tokens.shape
    return pl.pallas_call(
        beside_body,
        in_specs=[WHOLE, WHOLE] + [ANY] * len(after),
        out_specs=WHOLE,
        out_shape=jax.ShapeDtypeStruct((rows, 2 * width), tokens.dtype),
        compiler_params=PARAMS,
        cost_estimate=cost(0, 4 * rows * width * 2),
        name="beside",
    )(tokens, d_out, *after)


def by_rows(a, b):
    return lax.dot_general(a, b, (((1,), (1,)), ((), ())), preferred_element_type=F32)


def layer_body(both, *refs, resumed, tile, first, count):
    weights = refs[:3]
    hidden_ref, sum_ref = refs[-2:]
    features = weights[0].shape[0]
    rows = both.shape[0]
    joined = tile % 128 == 0
    sum_ref[...] = refs[3][...] if resumed else jnp.zeros_like(sum_ref)

    def step(gate_ref, up_ref, down_ref, hidden):
        x, dy = both[:, :features], both[:, features:]
        w_gate, w_up = gate_ref[...], up_ref[...]
        if joined:
            w_both = jnp.concatenate([w_gate, w_up], axis=1)
            gate_up = jnp.dot(x, w_both, preferred_element_type=F32)
            gate, up = gate_up[:, :tile], gate_up[:, tile:]
        else:
            gate = jnp.dot(x, w_gate, preferred_element_type=F32)
            up = jnp.dot(x, w_up, preferred_element_type=F32)
        d_hidden = by_rows(dy, down_ref[...])
        sig = 1.0 / (1.0 + jnp.exp(-gate))
        hidden[...] = (gate * sig * up).astype(BF16)
        d_gate = (d_hidden * up * sig * (1.0 + gate * (1.0 - sig))).astype(BF16)
        d_up = (d_hidden * gate * sig).astype(BF16)
        if joined:
            sum_ref[...] += by_rows(jnp.concatenate([d_gate, d_up], axis=1), w_both)
        else:
            sum_ref[...] += by_rows(d_gate, w_gate) + by_rows(d_up, w_up)

    deep = pl.Buffered(min(BUFFERS, count + 1))
    across = pl.BlockSpec((features, tile), lambda i: (0, first + i), pipeline_mode=deep)
    pltpu.emit_pipeline(
        step,
        grid=(count,),
        in_specs=[
            across,
            across,
            pl.BlockSpec((tile, features), lambda i: (first + i, 0), pipeline_mode=deep),
        ],
        out_specs=[pl.BlockSpec((rows, tile), lambda i: (0, i))],
    )(*weights, hidden_ref)


def layer(both, w_gate, w_up, w_down, partial_sum, after, tile, first, count):
    rows = both.shape[0]
    features = w_gate.shape[0]
    resumed = partial_sum is not None
    return pl.pallas_call(
        functools.partial(layer_body, resumed=resumed, tile=tile, first=first, count=count),
        in_specs=[WHOLE] + [ANY] * 3 + [WHOLE] * resumed + [ANY] * len(after),
        out_specs=[ANY, WHOLE],
        out_shape=[
            jax.ShapeDtypeStruct((rows, count * tile), BF16),
            jax.ShapeDtypeStruct((rows, features), F32),
        ],
        compiler_params=PARAMS,
        cost_estimate=cost(
            10 * rows * features * count * tile,
            3 * features * count * tile * 2,
            rows * count * tile,
        ),
        name="layer",
    )(both, w_gate, w_up, w_down, *([partial_sum] if resumed else []), *after)


def halve_body(bit, *refs, arrived, final):
    value = refs[0][...]
    if arrived:
        value = value + refs[1][...]
    if final:
        refs[-1][...] = value.astype(BF16)
        return
    kept, sent = refs[-2:]
    half = value.shape[0] // 2
    low, high = value[:half], value[half:]
    upper = bit[0] == 1
    kept[...] = jnp.where(upper, high, low)
    sent[...] = jnp.where(upper, low, high)


def halve(bit, value, arrived, after, final):
    rows, features = value.shape
    if final:
        out_shape = jax.ShapeDtypeStruct((rows, features), BF16)
    else:
        out_shape = [jax.ShapeDtypeStruct((rows // 2, features), F32)] * 2
    return pl.pallas_call(
        functools.partial(halve_body, arrived=bool(arrived), final=final),
        in_specs=[SMEM] + [WHOLE] * (1 + len(arrived)) + [ANY] * len(after),
        out_specs=WHOLE if final else [WHOLE, WHOLE],
        out_shape=out_shape,
        compiler_params=PARAMS,
        cost_estimate=cost(0, 3 * rows * features * 4),
        name="halve",
    )(bit, value, *arrived, *after)


class ScatteredSum:
    def __init__(self, value, axes):
        sizes = [lax.axis_size(axis) for axis in axes]
        self.value, self.arrived, self.levels = value, (), []
        self.done = any(size & (size - 1) for size in sizes)
        if self.done:
            summed = lax.psum_scatter(value, axes, scatter_dimension=0, tiled=True)
            self.value = summed.astype(BF16)
            return
        for axis, size in zip(axes, sizes):
            apart = size // 2
            while apart:
                self.levels.append((axis, size, apart))
                apart //= 2

    def advance(self, after):
        if self.done:
            return ()
        if self.levels:
            axis, size, apart = self.levels.pop(0)
            bit = ((lax.axis_index(axis) // apart) % 2).astype(jnp.int32)[None]
            self.value, sent = halve(bit, self.value, self.arrived, after, False)
            route = [(i, i ^ apart) for i in range(size)]
            self.arrived = (lax.ppermute(sent, axis, route),)
        else:
            bit = jnp.zeros((1,), jnp.int32)
            self.value = halve(bit, self.value, self.arrived, after, True)
            self.done = True
        return (self.value,)


def collect_body(failed, both, *refs, n, places, parts_count, size, pieces):
    roles = Roles(failed, n)
    parts = refs[:parts_count]
    blocks = refs[parts_count : parts_count + len(places)]
    hidden_t, outs, held, sem = refs[-4:]
    tokens, features = both.shape[0], both.shape[1] // 2
    width = outs.shape[1]

    def fetch(j, part):
        rows = pl.ds(size, pieces * tokens) if part == 0 else pl.ds(places[j], tokens)
        here = pl.ds(0, pieces * tokens) if part == 0 else pl.ds(pieces * tokens, tokens)
        return pltpu.make_async_copy(
            blocks[j].at[rows], held.at[j + 1, here], sem.at[j, part]
        )

    for j in range(len(places)):
        for part in range(2):
            fetch(j, part).start()
    for part, begin, piece, to, run in column_pieces([p.shape[1] for p in parts], width):
        units = parts[part][:, begin : begin + run]
        held[0, pl.ds(piece * tokens, tokens), pl.ds(to, run)] = jnp.where(
            roles.lost, jnp.zeros_like(units), units
        )
    slab = pl.ds(pl.multiple_of(features + roles.me * width, 128), width)
    held[0, pl.ds(pieces * tokens, tokens)] = both[:, slab]
    for j in range(len(places)):
        for part in range(2):
            fetch(j, part).wait()

    count = len(places) + 1
    for j in range(count):
        outs[pl.ds(j * tokens, tokens)] = held[j, pl.ds(pieces * tokens, tokens)]
    for piece in range(pieces):
        run = min(width, hidden_t.shape[0] - piece * width)
        rows = pl.ds(piece * tokens, tokens)
        hidden = jnp.concatenate([held[j, rows, :run] for j in range(count)], axis=0)
        hidden_t[pl.ds(piece * width, run)] = hidden.astype(F32).T.astype(BF16)


def collect(failed, n, both, parts, blocks, places, size, width, after):
    tokens = both.shape[0]
    units = sum(part.shape[1] for part in parts)
    pieces = -(-units // width)
    depth = tokens * (len(blocks) + 1)
    return pl.pallas_call(
        functools.partial(
            collect_body,
            n=n,
            places=places,
            parts_count=len(parts),
            size=size,
            pieces=pieces,
        ),
        in_specs=[SMEM]
        + [WHOLE] * (1 + len(parts))
        + [ANY] * (len(blocks) + len(after)),
        out_specs=[WHOLE, WHOLE],
        out_shape=[
            jax.ShapeDtypeStruct((units, depth), BF16),
            jax.ShapeDtypeStruct((depth, width), BF16),
        ],
        scratch_shapes=[
            pltpu.VMEM((len(blocks) + 1, (pieces + 1) * tokens, width), BF16),
            pltpu.SemaphoreType.DMA((len(blocks), 2)),
        ],
        compiler_params=PARAMS,
        cost_estimate=cost(0, 4 * depth * (units + width)),
        name="collect",
    )(failed, both, *parts, *blocks, *after)


def update_body(failed, hid_ref, out_ref, *refs, n, block, first, count, unread):
    state, news = refs[:3], refs[3 + unread : 6 + unread]
    total = refs[6 + unread]
    width = out_ref.shape[1]
    group = row_group(block)

    def step(hid, m_ref, a_ref, b_ref, m_new, a_new, b_new):
        total[...] = jnp.dot(hid[...], out_ref[...], preferred_element_type=F32)

        @pl.loop(0, block // group)
        def _(i):
            here = pl.ds(pl.multiple_of(i * group, group), group)
            m_new[here], a_new[here], b_new[here] = updated(
                m_ref[0, here], a_ref[0, here], b_ref[0, here], total[here], n - 1.0
            )

    deep = pl.Buffered(min(BUFFERS, count + 1))
    old = pl.BlockSpec(
        (1, block, width), lambda i: (0, first + i, 0), pipeline_mode=deep
    )
    new = pl.BlockSpec((block, width), lambda i: (first + i, 0))

    @pl.when(jnp.logical_not(Roles(failed, n).lost))
    def _():
        pltpu.emit_pipeline(
            step,
            grid=(count,),
            in_specs=[
                pl.BlockSpec((block, hid_ref.shape[1]), lambda i: (first + i, 0)),
                old,
                old,
                old,
            ],
            out_specs=[new] * 3,
        )(hid_ref, *state, *news)


def update(failed, n, hidden_t, outs, state, news, after, block, first, count):
    _, rows, width = state[0].shape
    depth = hidden_t.shape[1]
    shape = jax.ShapeDtypeStruct((rows, width), F32)
    unread = len(news) + len(after)
    return pl.pallas_call(
        functools.partial(
            update_body,
            n=n,
            block=block,
            first=first,
            count=count,
            unread=unread,
        ),
        in_specs=[SMEM, ANY, WHOLE] + [ANY] * (3 + unread),
        out_specs=[ANY] * 3,
        out_shape=[shape] * 3,
        scratch_shapes=[pltpu.VMEM((block, width), F32)],
        input_output_aliases={6 + k: k for k in range(len(news))},
        compiler_params=PARAMS,
        cost_estimate=cost(
            2 * count * block * width * depth,
            6 * count * block * width * 4,
            2 * count * block * width,
        ),
        name="update",
    )(failed, hidden_t, outs, *state, *news, *after)


def patch_body(failed, hid_ref, out_ref, *refs, arrivals, chunks, n, count_after):
    count = len(arrivals)
    got = refs[:count]
    rest = refs[count + 3 + count_after :]
    news = rest[:3]
    held, made, total, in_sem, out_sem = rest[3:]
    chunk = made.shape[2]
    group = row_group(chunk)
    roles = Roles(failed, n)
    ahead = roles.ahead()
    lag_of = {True: LAG * (ahead - 1), False: LAG * (n - ahead - 1)}

    def fetch(j):
        rows = got[j].at[pl.ds(0, 3 * chunk)]
        return pltpu.make_async_copy(rows, held.at[j % FETCHED], in_sem.at[j % FETCHED])

    def first_row(j):
        step, forward = arrivals[j]
        place = step - lag_of[forward]
        if not forward:
            place = chunks - 1 - place
        return pl.multiple_of(jnp.clip(place, 0, chunks - 1) * chunk, TILE)

    def store(j, k):
        return pltpu.make_async_copy(
            made.at[j % BUFFERS, k],
            news[k].at[pl.ds(first_row(j), chunk)],
            out_sem.at[j % BUFFERS, k],
        )

    def valid(j):
        step, forward = arrivals[j]
        return step >= lag_of[forward]

    def finish(j):
        @pl.when(valid(j))
        def _():
            for k in range(3):
                store(j, k).wait()

    @pl.when(roles.lost)
    def _():
        for j in range(min(FETCHED - 1, count)):
            fetch(j).start()
        for j in range(count):
            if j + FETCHED - 1 < count:
                fetch(j + FETCHED - 1).start()
            fetch(j).wait()
            if j >= BUFFERS:
                finish(j - BUFFERS)

            @pl.when(valid(j))
            def _(j=j, slot=j % FETCHED, out_slot=j % BUFFERS):
                first = first_row(j)

                units = hid_ref[pl.ds(first, chunk)]
                total[...] = jnp.dot(units, out_ref[...], preferred_element_type=F32)

                @pl.loop(0, chunk // group)
                def _(i):
                    base = pl.multiple_of(i * group, group)
                    old = [
                        held[slot, pl.ds(k * chunk + base, group)].astype(F32)
                        for k in range(3)
                    ]
                    new = updated(*old, total[pl.ds(base, group)], n - 1.0)
                    for k in range(3):
                        made[out_slot, k, pl.ds(base, group)] = new[k]

                for k in range(3):
                    store(j, k).start()

        for j in range(max(count - BUFFERS, 0), count):
            finish(j)


def patch(failed, n, hidden_t, outs, got, arrivals, news, after, chunks):
    rows, width = news[0].shape
    chunk = rows // chunks
    count = len(got)
    shape = jax.ShapeDtypeStruct((rows, width), F32)
    return pl.pallas_call(
        functools.partial(
            patch_body, arrivals=arrivals, chunks=chunks, n=n, count_after=len(after)
        ),
        in_specs=[SMEM, WHOLE, WHOLE] + [ANY] * (count + 3 + len(after)),
        out_specs=[ANY] * 3,
        out_shape=[shape] * 3,
        scratch_shapes=[
            pltpu.VMEM((FETCHED, 3 * chunk, width), BF16),
            pltpu.VMEM((BUFFERS, 3, chunk, width), F32),
            pltpu.VMEM((chunk, width), F32),
            pltpu.SemaphoreType.DMA((FETCHED,)),
            pltpu.SemaphoreType.DMA((BUFFERS, 3)),
        ],
        input_output_aliases={3 + count + k: k for k in range(3)},
        compiler_params=PARAMS,
        cost_estimate=cost(
            2 * count * chunk * width * hidden_t.shape[1],
            count * 3 * chunk * width * 6,
            2 * count * chunk * width,
        ),
        name="patch",
    )(failed, hidden_t, outs, *got, *news, *after)


def per_device(tokens, d_out, w_gate, w_up, w_down, failed, master, moment1, moment2):
    n = lax.axis_size("replica")
    _, rows, width = master.shape
    features, units = w_gate.shape

    order = ring_order(n)

    state = (master, moment1, moment2)
    chunks = largest(
        (c for c in range(2, MOST_CHUNKS + 1, 2) if rows % (TILE * c) == 0), 2
    )
    chunk = rows // chunks
    steps = (chunks + LAG * (n - 2)) // 2
    reach = (n // 2, (n - 1) // 2)
    forward = [(order[p], order[(p + 1) % n]) for p in range(n)]
    backward = [(b, a) for a, b in forward]
    sends, got = [], []
    parcel_from = None

    def send(*after, parcel=()):
        nonlocal parcel_from
        step = len(got)
        seen = got[step - LAG] if step >= LAG else ()
        here = min(step, chunks - 1)
        slabs, passed = (0, 0), (0, 0)
        if parcel:
            parcel_from, slabs = step, reach
        elif parcel_from is not None and (step - parcel_from) % LAG == 0:
            hop = (step - parcel_from) // LAG
            passed = tuple(
                seen[way].shape[0] - 3 * chunk - both.shape[0]
                if hop < reach[way]
                else 0
                for way in range(2)
            )
        sends.append(
            pack(
                failed,
                n,
                state,
                seen,
                parcel,
                after,
                (here, chunks - 1 - here),
                chunk,
                slabs,
                passed,
            )
        )
        got.append(
            (
                lax.ppermute(sends[-1][0], "replica", forward),
                lax.ppermute(sends[-1][1], "replica", backward),
            )
        )
        return (sends[-1][0],)

    sent = send()
    sent = send(*sent)
    both = beside(tokens[0], d_out[0], sent)
    both = lax.all_gather(both, ("fsdp", "tensor"), axis=0, tiled=True)
    sent = send(both)

    tile = 128 if units % 128 == 0 else units
    hidden, d_rows = [], None
    pieces = shares(units // tile, 5)
    for first, count in pieces:
        part, d_rows = layer(both, w_gate, w_up, w_down, d_rows, sent, tile, first, count)
        hidden.append(part)
        last = len(hidden) == len(pieces)
        sent = send(d_rows, parcel=(both, *hidden) if last else ())
    cotangents = ScatteredSum(d_rows, ("fsdp", "tensor"))

    news = ()
    patched = 0
    hidden_t = outs = None

    def gathered(after):
        blocks, places = [], []
        for way in range(2):
            for hop in range(reach[way]):
                blocks.append(got[parcel_from + LAG * hop][way])
                places.append(blocks[-1].shape[0] - both.shape[0])
        return collect(
            failed, n, both, hidden, blocks, places, 3 * chunk, width, after
        )

    def update_part(first, count, after):
        return update(
            failed, n, hidden_t, outs, state, news, after, block, first, count
        )

    def patch_to(step, after):
        nonlocal patched
        arrivals = [(s, way) for s in range(patched, step) for way in (True, False)]
        if not arrivals:
            return news
        blocks = [b for s in range(patched, step) for b in got[s]]
        patched = step
        return patch(failed, n, hidden_t, outs, blocks, arrivals, news, after, chunks)

    block = largest((b for b in range(TILE, 193, TILE) if rows % b == 0), rows)
    blocks = rows // block
    early = blocks // 4
    ready = parcel_from + LAG * reach[0] + 1
    while len(got) < steps:
        sent = send(*cotangents.advance(sent), *news[:1])
        if len(got) == ready and early and len(got) < steps:
            hidden_t, outs = gathered(sent)
            news = update_part(0, early, (hidden_t,))
            news = patch_to(len(got) // 2, ())
    if hidden_t is None:
        hidden_t, outs = gathered(sent)
        early = 0
    news = update_part(early, blocks - early, sent)
    for step in (steps - 2, steps - 1, steps):
        news = patch_to(step, ())
    while not cotangents.done:
        cotangents.advance(sent)
    return (cotangents.value[None], *news)


def solution(mesh):
    placed = (
        P("replica", ("fsdp", "tensor"), None),
        P("replica", ("fsdp", "tensor"), None),
        P(None, ("fsdp", "tensor")),
        P(None, ("fsdp", "tensor")),
        P(("fsdp", "tensor"), None),
        P(("fsdp", "tensor")),
        P(None, ("fsdp", "tensor"), "replica"),
        P(None, ("fsdp", "tensor"), "replica"),
        P(None, ("fsdp", "tensor"), "replica"),
    )
    return jax.shard_map(
        per_device,
        mesh=mesh,
        in_specs=placed,
        out_specs=(
            P("replica", ("fsdp", "tensor"), None),
            P(("fsdp", "tensor"), "replica"),
            P(("fsdp", "tensor"), "replica"),
            P(("fsdp", "tensor"), "replica"),
        ),
        check_vma=False,
    )
```

```python
import functools

import jax
import jax.numpy as jnp
from jax import lax
from jax.experimental import pallas as pl
from jax.experimental.pallas import tpu as pltpu
from jax.sharding import PartitionSpec as P

BF16, F32 = jnp.bfloat16, jnp.float32
LAG = 2
MOST_CHUNKS = 24
TILE = 16
BUFFERS = 3
FETCHED = 4
VMEM = 50 << 20

ANY = pl.BlockSpec(memory_space=pl.ANY)
SMEM = pl.BlockSpec(memory_space=pltpu.SMEM)
WHOLE = pl.BlockSpec(memory_space=pltpu.VMEM)
PARAMS = pltpu.CompilerParams(vmem_limit_bytes=VMEM)


def ring_order(n):
    return [0, 1, 3, 2] if n == 4 else list(range(n))


def entry(table, index):
    found = jnp.int32(0)
    for at, value in enumerate(table):
        found = jnp.where(index == at, jnp.int32(value), found)
    return found


class Roles:
    def __init__(self, failed, n):
        self.n = n
        self.order = ring_order(n)
        self.spots = [self.order.index(i) for i in range(n)]
        self.me = lax.axis_index("replica").astype(jnp.int32)
        self.failed = failed[0]
        self.source = lax.rem(self.failed + 1, n)
        self.lost = self.me == self.failed

    def ahead(self):
        apart = entry(self.spots, self.failed) - entry(self.spots, self.source)
        return lax.rem(apart + self.n, self.n)

    def neighbour(self, hops):
        spot = lax.rem(entry(self.spots, self.me) + hops, self.n)
        return entry(self.order, spot)


def largest(options, default):
    options = list(options)
    return max(options) if options else default


def shares(total, parts):
    parts = min(parts, total)
    edges = [total * i // parts for i in range(parts + 1)]
    return [(a, b - a) for a, b in zip(edges, edges[1:])]


def row_group(rows):
    return largest((g for g in (16, 32) if rows % g == 0), rows)


def cost(flops, bytes_accessed, transcendentals=0):
    return pl.CostEstimate(
        flops=flops, bytes_accessed=bytes_accessed, transcendentals=transcendentals
    )


def updated(master_old, first_old, second_old, total, healthy):
    first_new = 0.9 * first_old + (0.1 / healthy) * total
    second_new = 0.95 * second_old + (0.05 / healthy**2) * (total * total)
    root = second_new * lax.rsqrt(second_new)
    step = first_new * pl.reciprocal(root + 1e-08)
    return master_old - 0.01 * step, first_new, second_new


def column_pieces(lengths, width):
    moves, column = [], 0
    for part, length in enumerate(lengths):
        begin = 0
        while begin < length:
            piece, to = divmod(column, width)
            run = min(length - begin, width - to)
            moves.append((part, begin, piece, to, run))
            begin, column = begin + run, column + run
    return moves


def pack_body(*refs, n, places, chunk, slabs, passed, counts):
    count_seen, count_parts, count_after = counts
    if count_seen:
        roles, refs = Roles(refs[0], n), refs[1:]
    state = refs[0:3]
    seen = refs[3 : 3 + count_seen]
    rest = refs[3 + count_seen :]
    if count_parts:
        both, parts, rest = rest[0], rest[1 : 1 + count_parts], rest[1 + count_parts :]
    sends = rest[count_after : count_after + 2]
    held, made, sem, out_sem, below_sem = rest[count_after + 2 :]
    width = held.shape[2]
    size = 3 * chunk

    def rows_of(j):
        way, k = divmod(j, 3)
        return way, pl.ds(k * chunk, chunk)

    def fetch(j):
        way, k = divmod(j, 3)
        rows = pl.ds(places[way] * chunk, chunk)
        return pltpu.make_async_copy(state[k].at[1, rows], held.at[j], sem.at[j])

    def take(j):
        way, rows = rows_of(j)
        return pltpu.make_async_copy(seen[way].at[rows], made.at[way, rows], sem.at[j])

    def store(j):
        way, rows = rows_of(j)
        return pltpu.make_async_copy(
            made.at[way, rows], sends[way].at[rows], out_sem.at[j]
        )

    def convert():
        for j in range(6):
            fetch(j).start()
        for j in range(6):
            way, rows = rows_of(j)
            fetch(j).wait()
            made[way, rows] = held[j].astype(BF16)
            store(j).start()
        for j in range(6):
            store(j).wait()

    def relay():
        for j in range(6):
            take(j).start()
        for j in range(6):
            take(j).wait()
            store(j).start()
        for j in range(6):
            store(j).wait()

    def below(way, inward):
        rows = pl.ds(size, passed[way] or sends[way].shape[0] - size)
        here = made.at[way, rows]
        if inward:
            return pltpu.make_async_copy(seen[way].at[rows], here, below_sem.at[way])
        return pltpu.make_async_copy(here, sends[way].at[rows], below_sem.at[way])

    for way in range(2):
        if passed[way]:
            below(way, True).start()
        if slabs[way]:
            tokens, features = both.shape[0], both.shape[1] // 2
            moves = column_pieces([part.shape[1] for part in parts], width)
            for part, begin, piece, to, run in moves:
                units = parts[part][:, begin : begin + run]
                made[way, pl.ds(size + piece * tokens, tokens), pl.ds(to, run)] = (
                    jnp.where(roles.lost, jnp.zeros_like(units), units)
                )
            row = size + (1 + moves[-1][2]) * tokens
            for far in range(slabs[way], 0, -1):
                target = roles.neighbour(far if way == 0 else n - far)
                slab = pl.ds(pl.multiple_of(features + target * width, 128), width)
                made[way, pl.ds(row, tokens)] = both[:, slab]
                row += tokens
            below(way, False).start()

    for way in range(2):
        if passed[way]:
            below(way, True).wait()
            below(way, False).start()

    if seen:
        pl.when(roles.me == roles.source)(convert)
        pl.when(roles.me != roles.source)(relay)
    else:
        convert()

    for way in range(2):
        if slabs[way] or passed[way]:
            below(way, False).wait()


def pack(failed, n, state, seen, parcel, after, places, chunk, slabs, passed):
    width = state[0].shape[2]
    extra = list(passed)
    if parcel:
        tokens = parcel[0].shape[0]
        pieces = -(-sum(part.shape[1] for part in parcel[1:]) // width)
        extra = [tokens * (pieces + count) if count else 0 for count in slabs]
    counts = (len(seen), max(len(parcel) - 1, 0), len(after))
    return pl.pallas_call(
        functools.partial(
            pack_body,
            n=n,
            places=places,
            chunk=chunk,
            slabs=slabs,
            passed=passed,
            counts=counts,
        ),
        in_specs=[SMEM] * bool(seen)
        + [ANY] * (3 + len(seen))
        + [WHOLE] * len(parcel)
        + [ANY] * len(after),
        out_specs=[ANY, ANY],
        out_shape=[
            jax.ShapeDtypeStruct((3 * chunk + more, width), BF16) for more in extra
        ],
        scratch_shapes=[
            pltpu.VMEM((6, chunk, width), F32),
            pltpu.VMEM((2, 3 * chunk + max(extra), width), BF16),
            pltpu.SemaphoreType.DMA((6,)),
            pltpu.SemaphoreType.DMA((6,)),
            pltpu.SemaphoreType.DMA((2,)),
        ],
        compiler_params=PARAMS,
        cost_estimate=cost(0, 2 * 3 * chunk * width * 6),
        name="pack",
    )(*([failed] if seen else []), *state, *seen, *parcel, *after)


def beside_body(*refs):
    tokens, d_out, out = refs[0], refs[1], refs[-1]
    width = tokens.shape[1]
    out[0, :, :width] = tokens[...]
    out[0, :, width:] = d_out[...]


def beside(tokens, d_out, after):
    rows, width = tokens.shape
    return pl.pallas_call(
        beside_body,
        in_specs=[WHOLE, WHOLE] + [ANY] * len(after),
        out_specs=WHOLE,
        out_shape=jax.ShapeDtypeStruct((1, rows, 2 * width), tokens.dtype),
        compiler_params=PARAMS,
        cost_estimate=cost(0, 4 * rows * width * 2),
        name="beside",
    )(tokens, d_out, *after)


def join_body(own, other, *refs, axis, apart, last):
    out = refs[-1]
    count, rows = own.shape[:2]
    second = lax.rem(lax.div(lax.axis_index(axis).astype(jnp.int32), apart), 2)
    if not last:
        out[pl.ds(second * count, count)] = own[...]
        out[pl.ds((1 - second) * count, count)] = other[...]
        return
    for i in range(2 * count):
        here, there = (own, other) if i < count else (other, own)
        value = jnp.where(second == 1, there[i % count], here[i % count])
        out[pl.ds(i * rows, rows)] = value


def join(own, other, after, axis, apart, last):
    count, rows, width = own.shape
    shape = (2 * count * rows, width) if last else (2 * count, rows, width)
    return pl.pallas_call(
        functools.partial(join_body, axis=axis, apart=apart, last=last),
        in_specs=[WHOLE, WHOLE] + [ANY] * len(after),
        out_specs=WHOLE,
        out_shape=jax.ShapeDtypeStruct(shape, own.dtype),
        compiler_params=PARAMS,
        cost_estimate=cost(0, 8 * count * rows * width),
        name="join",
    )(own, other, *after)


def by_rows(a, b):
    return lax.dot_general(a, b, (((1,), (1,)), ((), ())), preferred_element_type=F32)


def layer_body(both, *refs, resumed, tile, first, count):
    weights = refs[:3]
    hidden_ref, sum_ref = refs[-2:]
    features = weights[0].shape[0]
    rows = both.shape[0]
    joined = tile % 128 == 0
    sum_ref[...] = refs[3][...] if resumed else jnp.zeros_like(sum_ref)

    def step(gate_ref, up_ref, down_ref, hidden):
        x, dy = both[:, :features], both[:, features:]
        w_gate, w_up = gate_ref[...], up_ref[...]
        if joined:
            w_both = jnp.concatenate([w_gate, w_up], axis=1)
            gate_up = jnp.dot(x, w_both, preferred_element_type=F32)
            gate, up = gate_up[:, :tile], gate_up[:, tile:]
        else:
            gate = jnp.dot(x, w_gate, preferred_element_type=F32)
            up = jnp.dot(x, w_up, preferred_element_type=F32)
        d_hidden = by_rows(dy, down_ref[...])
        sig = 1.0 / (1.0 + jnp.exp(-gate))
        hidden[...] = (gate * sig * up).astype(BF16)
        d_gate = (d_hidden * up * sig * (1.0 + gate * (1.0 - sig))).astype(BF16)
        d_up = (d_hidden * gate * sig).astype(BF16)
        if joined:
            sum_ref[...] += by_rows(jnp.concatenate([d_gate, d_up], axis=1), w_both)
        else:
            sum_ref[...] += by_rows(d_gate, w_gate) + by_rows(d_up, w_up)

    deep = pl.Buffered(min(BUFFERS, count + 1))
    across = pl.BlockSpec((features, tile), lambda i: (0, first + i), pipeline_mode=deep)
    pltpu.emit_pipeline(
        step,
        grid=(count,),
        in_specs=[
            across,
            across,
            pl.BlockSpec((tile, features), lambda i: (first + i, 0), pipeline_mode=deep),
        ],
        out_specs=[pl.BlockSpec((rows, tile), lambda i: (0, i))],
    )(*weights, hidden_ref)


def layer(both, w_gate, w_up, w_down, partial_sum, after, tile, first, count):
    rows = both.shape[0]
    features = w_gate.shape[0]
    resumed = partial_sum is not None
    return pl.pallas_call(
        functools.partial(layer_body, resumed=resumed, tile=tile, first=first, count=count),
        in_specs=[WHOLE] + [ANY] * 3 + [WHOLE] * resumed + [ANY] * len(after),
        out_specs=[ANY, WHOLE],
        out_shape=[
            jax.ShapeDtypeStruct((rows, count * tile), BF16),
            jax.ShapeDtypeStruct((rows, features), F32),
        ],
        compiler_params=PARAMS,
        cost_estimate=cost(
            10 * rows * features * count * tile,
            3 * features * count * tile * 2,
            rows * count * tile,
        ),
        name="layer",
    )(both, w_gate, w_up, w_down, *([partial_sum] if resumed else []), *after)


def halve_body(bit, *refs, arrived, final):
    value = refs[0][...]
    if arrived:
        value = value + refs[1][...]
    if final:
        refs[-1][...] = value.astype(BF16)
        return
    kept, sent = refs[-2:]
    half = value.shape[0] // 2
    low, high = value[:half], value[half:]
    upper = bit[0] == 1
    kept[...] = jnp.where(upper, high, low)
    sent[...] = jnp.where(upper, low, high)


def halve(bit, value, arrived, after, final):
    rows, features = value.shape
    if final:
        out_shape = jax.ShapeDtypeStruct((rows, features), BF16)
    else:
        out_shape = [jax.ShapeDtypeStruct((rows // 2, features), F32)] * 2
    return pl.pallas_call(
        functools.partial(halve_body, arrived=bool(arrived), final=final),
        in_specs=[SMEM] + [WHOLE] * (1 + len(arrived)) + [ANY] * len(after),
        out_specs=WHOLE if final else [WHOLE, WHOLE],
        out_shape=out_shape,
        compiler_params=PARAMS,
        cost_estimate=cost(0, 3 * rows * features * 4),
        name="halve",
    )(bit, value, *arrived, *after)


class ScatteredSum:
    def __init__(self, value, axes):
        sizes = [lax.axis_size(axis) for axis in axes]
        self.value, self.arrived, self.levels = value, (), []
        self.done = any(size & (size - 1) for size in sizes)
        if self.done:
            summed = lax.psum_scatter(value, axes, scatter_dimension=0, tiled=True)
            self.value = summed.astype(BF16)
            return
        for axis, size in zip(axes, sizes):
            apart = size // 2
            while apart:
                self.levels.append((axis, size, apart))
                apart //= 2

    def advance(self, after):
        if self.done:
            return ()
        if self.levels:
            axis, size, apart = self.levels.pop(0)
            bit = ((lax.axis_index(axis) // apart) % 2).astype(jnp.int32)[None]
            self.value, sent = halve(bit, self.value, self.arrived, after, False)
            route = [(i, i ^ apart) for i in range(size)]
            self.arrived = (lax.ppermute(sent, axis, route),)
        else:
            bit = jnp.zeros((1,), jnp.int32)
            self.value = halve(bit, self.value, self.arrived, after, True)
            self.done = True
        return (self.value,)


def collect_body(failed, both, *refs, n, places, parts_count, size, pieces):
    roles = Roles(failed, n)
    parts = refs[:parts_count]
    blocks = refs[parts_count : parts_count + len(places)]
    hidden_t, outs, held, sem = refs[-4:]
    tokens, features = both.shape[0], both.shape[1] // 2
    width = outs.shape[1]

    def fetch(j, part):
        rows = pl.ds(size, pieces * tokens) if part == 0 else pl.ds(places[j], tokens)
        here = pl.ds(0, pieces * tokens) if part == 0 else pl.ds(pieces * tokens, tokens)
        return pltpu.make_async_copy(
            blocks[j].at[rows], held.at[j + 1, here], sem.at[j, part]
        )

    for j in range(len(places)):
        for part in range(2):
            fetch(j, part).start()
    for part, begin, piece, to, run in column_pieces([p.shape[1] for p in parts], width):
        units = parts[part][:, begin : begin + run]
        held[0, pl.ds(piece * tokens, tokens), pl.ds(to, run)] = jnp.where(
            roles.lost, jnp.zeros_like(units), units
        )
    slab = pl.ds(pl.multiple_of(features + roles.me * width, 128), width)
    held[0, pl.ds(pieces * tokens, tokens)] = both[:, slab]
    for j in range(len(places)):
        for part in range(2):
            fetch(j, part).wait()

    count = len(places) + 1
    for j in range(count):
        outs[pl.ds(j * tokens, tokens)] = held[j, pl.ds(pieces * tokens, tokens)]
    for piece in range(pieces):
        run = min(width, hidden_t.shape[0] - piece * width)
        rows = pl.ds(piece * tokens, tokens)
        hidden = jnp.concatenate([held[j, rows, :run] for j in range(count)], axis=0)
        hidden_t[pl.ds(piece * width, run)] = hidden.astype(F32).T.astype(BF16)


def collect(failed, n, both, parts, blocks, places, size, width, after):
    tokens = both.shape[0]
    units = sum(part.shape[1] for part in parts)
    pieces = -(-units // width)
    depth = tokens * (len(blocks) + 1)
    return pl.pallas_call(
        functools.partial(
            collect_body,
            n=n,
            places=places,
            parts_count=len(parts),
            size=size,
            pieces=pieces,
        ),
        in_specs=[SMEM]
        + [WHOLE] * (1 + len(parts))
        + [ANY] * (len(blocks) + len(after)),
        out_specs=[WHOLE, WHOLE],
        out_shape=[
            jax.ShapeDtypeStruct((units, depth), BF16),
            jax.ShapeDtypeStruct((depth, width), BF16),
        ],
        scratch_shapes=[
            pltpu.VMEM((len(blocks) + 1, (pieces + 1) * tokens, width), BF16),
            pltpu.SemaphoreType.DMA((len(blocks), 2)),
        ],
        compiler_params=PARAMS,
        cost_estimate=cost(0, 4 * depth * (units + width)),
        name="collect",
    )(failed, both, *parts, *blocks, *after)


def update_body(failed, hid_ref, out_ref, *refs, n, block, first, count, unread):
    state, news = refs[:3], refs[3 + unread : 6 + unread]
    total = refs[6 + unread]
    width = out_ref.shape[1]
    group = row_group(block)

    def step(hid, m_ref, a_ref, b_ref, m_new, a_new, b_new):
        total[...] = jnp.dot(hid[...], out_ref[...], preferred_element_type=F32)

        @pl.loop(0, block // group)
        def _(i):
            here = pl.ds(pl.multiple_of(i * group, group), group)
            m_new[here], a_new[here], b_new[here] = updated(
                m_ref[0, here], a_ref[0, here], b_ref[0, here], total[here], n - 1.0
            )

    deep = pl.Buffered(min(BUFFERS, count + 1))
    old = pl.BlockSpec(
        (1, block, width), lambda i: (0, first + i, 0), pipeline_mode=deep
    )
    new = pl.BlockSpec((block, width), lambda i: (first + i, 0))

    @pl.when(jnp.logical_not(Roles(failed, n).lost))
    def _():
        pltpu.emit_pipeline(
            step,
            grid=(count,),
            in_specs=[
                pl.BlockSpec((block, hid_ref.shape[1]), lambda i: (first + i, 0)),
                old,
                old,
                old,
            ],
            out_specs=[new] * 3,
        )(hid_ref, *state, *news)


def update(failed, n, hidden_t, outs, state, news, after, block, first, count):
    _, rows, width = state[0].shape
    depth = hidden_t.shape[1]
    shape = jax.ShapeDtypeStruct((rows, width), F32)
    unread = len(news) + len(after)
    return pl.pallas_call(
        functools.partial(
            update_body,
            n=n,
            block=block,
            first=first,
            count=count,
            unread=unread,
        ),
        in_specs=[SMEM, ANY, WHOLE] + [ANY] * (3 + unread),
        out_specs=[ANY] * 3,
        out_shape=[shape] * 3,
        scratch_shapes=[pltpu.VMEM((block, width), F32)],
        input_output_aliases={6 + k: k for k in range(len(news))},
        compiler_params=PARAMS,
        cost_estimate=cost(
            2 * count * block * width * depth,
            6 * count * block * width * 4,
            2 * count * block * width,
        ),
        name="update",
    )(failed, hidden_t, outs, *state, *news, *after)


def patch_body(failed, hid_ref, out_ref, *refs, arrivals, chunks, n, count_after):
    count = len(arrivals)
    got = refs[:count]
    rest = refs[count + 3 + count_after :]
    news = rest[:3]
    held, made, total, in_sem, out_sem = rest[3:]
    chunk = made.shape[2]
    group = row_group(chunk)
    roles = Roles(failed, n)
    ahead = roles.ahead()
    lag_of = {True: LAG * (ahead - 1), False: LAG * (n - ahead - 1)}

    def fetch(j):
        rows = got[j].at[pl.ds(0, 3 * chunk)]
        return pltpu.make_async_copy(rows, held.at[j % FETCHED], in_sem.at[j % FETCHED])

    def first_row(j):
        step, forward = arrivals[j]
        place = step - lag_of[forward]
        if not forward:
            place = chunks - 1 - place
        return pl.multiple_of(jnp.clip(place, 0, chunks - 1) * chunk, TILE)

    def store(j, k):
        return pltpu.make_async_copy(
            made.at[j % BUFFERS, k],
            news[k].at[pl.ds(first_row(j), chunk)],
            out_sem.at[j % BUFFERS, k],
        )

    def valid(j):
        step, forward = arrivals[j]
        return step >= lag_of[forward]

    def finish(j):
        @pl.when(valid(j))
        def _():
            for k in range(3):
                store(j, k).wait()

    @pl.when(roles.lost)
    def _():
        for j in range(min(FETCHED - 1, count)):
            fetch(j).start()
        for j in range(count):
            if j + FETCHED - 1 < count:
                fetch(j + FETCHED - 1).start()
            fetch(j).wait()
            if j >= BUFFERS:
                finish(j - BUFFERS)

            @pl.when(valid(j))
            def _(j=j, slot=j % FETCHED, out_slot=j % BUFFERS):
                first = first_row(j)

                units = hid_ref[pl.ds(first, chunk)]
                total[...] = jnp.dot(units, out_ref[...], preferred_element_type=F32)

                @pl.loop(0, chunk // group)
                def _(i):
                    base = pl.multiple_of(i * group, group)
                    old = [
                        held[slot, pl.ds(k * chunk + base, group)].astype(F32)
                        for k in range(3)
                    ]
                    new = updated(*old, total[pl.ds(base, group)], n - 1.0)
                    for k in range(3):
                        made[out_slot, k, pl.ds(base, group)] = new[k]

                for k in range(3):
                    store(j, k).start()

        for j in range(max(count - BUFFERS, 0), count):
            finish(j)


def patch(failed, n, hidden_t, outs, got, arrivals, news, after, chunks):
    rows, width = news[0].shape
    chunk = rows // chunks
    count = len(got)
    shape = jax.ShapeDtypeStruct((rows, width), F32)
    return pl.pallas_call(
        functools.partial(
            patch_body, arrivals=arrivals, chunks=chunks, n=n, count_after=len(after)
        ),
        in_specs=[SMEM, WHOLE, WHOLE] + [ANY] * (count + 3 + len(after)),
        out_specs=[ANY] * 3,
        out_shape=[shape] * 3,
        scratch_shapes=[
            pltpu.VMEM((FETCHED, 3 * chunk, width), BF16),
            pltpu.VMEM((BUFFERS, 3, chunk, width), F32),
            pltpu.VMEM((chunk, width), F32),
            pltpu.SemaphoreType.DMA((FETCHED,)),
            pltpu.SemaphoreType.DMA((BUFFERS, 3)),
        ],
        input_output_aliases={3 + count + k: k for k in range(3)},
        compiler_params=PARAMS,
        cost_estimate=cost(
            2 * count * chunk * width * hidden_t.shape[1],
            count * 3 * chunk * width * 6,
            2 * count * chunk * width,
        ),
        name="patch",
    )(failed, hidden_t, outs, *got, *news, *after)


def per_device(tokens, d_out, w_gate, w_up, w_down, failed, master, moment1, moment2):
    n = lax.axis_size("replica")
    _, rows, width = master.shape
    features, units = w_gate.shape

    order = ring_order(n)

    state = (master, moment1, moment2)
    chunks = largest(
        (c for c in range(2, MOST_CHUNKS + 1, 2) if rows % (TILE * c) == 0), 2
    )
    chunk = rows // chunks
    steps = (chunks + LAG * (n - 2)) // 2
    reach = (n // 2, (n - 1) // 2)
    forward = [(order[p], order[(p + 1) % n]) for p in range(n)]
    backward = [(b, a) for a, b in forward]
    sends, got = [], []
    parcel_from = None

    def send(*after, parcel=()):
        nonlocal parcel_from
        step = len(got)
        seen = got[step - LAG] if step >= LAG else ()
        here = min(step, chunks - 1)
        slabs, passed = (0, 0), (0, 0)
        if parcel:
            parcel_from, slabs = step, reach
        elif parcel_from is not None and (step - parcel_from) % LAG == 0:
            hop = (step - parcel_from) // LAG
            passed = tuple(
                seen[way].shape[0] - 3 * chunk - both.shape[0]
                if hop < reach[way]
                else 0
                for way in range(2)
            )
        sends.append(
            pack(
                failed,
                n,
                state,
                seen,
                parcel,
                after,
                (here, chunks - 1 - here),
                chunk,
                slabs,
                passed,
            )
        )
        got.append(
            (
                lax.ppermute(sends[-1][0], "replica", forward),
                lax.ppermute(sends[-1][1], "replica", backward),
            )
        )
        return (sends[-1][0],)

    sent = send()
    both = beside(tokens[0], d_out[0], sent)
    exchanges = []
    for axis in ("tensor", "fsdp"):
        size = lax.axis_size(axis)
        exchanges += [(axis, size, 1 << k) for k in range((size - 1).bit_length())]
    if all(size & (size - 1) == 0 for _, size, _ in exchanges):
        for level, (axis, size, apart) in enumerate(exchanges):
            last = level == len(exchanges) - 1
            other = lax.ppermute(both, axis, [(i, i ^ apart) for i in range(size)])
            after = ()
            if level == 0 or last:
                after = sent = send(both)
            both = join(both, other, after, axis, apart, last)
    else:
        sent = send(both)
        both = lax.all_gather(both[0], ("fsdp", "tensor"), axis=0, tiled=True)
        sent = send(both)

    tile = 128 if units % 128 == 0 else units
    hidden, d_rows = [], None
    pieces = shares(units // tile, 5)
    for first, count in pieces:
        part, d_rows = layer(both, w_gate, w_up, w_down, d_rows, sent, tile, first, count)
        hidden.append(part)
        last = len(hidden) == len(pieces)
        sent = send(d_rows, parcel=(both, *hidden) if last else ())
    cotangents = ScatteredSum(d_rows, ("fsdp", "tensor"))

    news = ()
    patched = 0
    hidden_t = outs = None

    def gathered(after):
        blocks, places = [], []
        for way in range(2):
            for hop in range(reach[way]):
                blocks.append(got[parcel_from + LAG * hop][way])
                places.append(blocks[-1].shape[0] - both.shape[0])
        return collect(
            failed, n, both, hidden, blocks, places, 3 * chunk, width, after
        )

    def update_part(first, count, after):
        return update(
            failed, n, hidden_t, outs, state, news, after, block, first, count
        )

    def patch_to(step, after):
        nonlocal patched
        arrivals = [(s, way) for s in range(patched, step) for way in (True, False)]
        if not arrivals:
            return news
        blocks = [b for s in range(patched, step) for b in got[s]]
        patched = step
        return patch(failed, n, hidden_t, outs, blocks, arrivals, news, after, chunks)

    block = largest((b for b in range(TILE, 193, TILE) if rows % b == 0), rows)
    blocks = rows // block
    early = blocks // 4
    ready = parcel_from + LAG * reach[0] + 1
    while len(got) < steps:
        sent = send(*cotangents.advance(sent), *news[:1])
        if len(got) == ready and early and len(got) < steps:
            hidden_t, outs = gathered(sent)
            news = update_part(0, early, (hidden_t,))
            news = patch_to(len(got) // 2, ())
    if hidden_t is None:
        hidden_t, outs = gathered(sent)
        early = 0
    news = update_part(early, blocks - early, sent)
    for step in (steps - 2, steps - 1, steps):
        news = patch_to(step, ())
    while not cotangents.done:
        cotangents.advance(sent)
    return (cotangents.value[None], *news)


def solution(mesh):
    placed = (
        P("replica", ("fsdp", "tensor"), None),
        P("replica", ("fsdp", "tensor"), None),
        P(None, ("fsdp", "tensor")),
        P(None, ("fsdp", "tensor")),
        P(("fsdp", "tensor"), None),
        P(("fsdp", "tensor")),
        P(None, ("fsdp", "tensor"), "replica"),
        P(None, ("fsdp", "tensor"), "replica"),
        P(None, ("fsdp", "tensor"), "replica"),
    )
    return jax.shard_map(
        per_device,
        mesh=mesh,
        in_specs=placed,
        out_specs=(
            P("replica", ("fsdp", "tensor"), None),
            P(("fsdp", "tensor"), "replica"),
            P(("fsdp", "tensor"), "replica"),
            P(("fsdp", "tensor"), "replica"),
        ),
        check_vma=False,
    )
```

```python
import functools

import jax
import jax.numpy as jnp
from jax import lax
from jax.experimental import pallas as pl
from jax.experimental.pallas import tpu as pltpu
from jax.sharding import PartitionSpec as P

BF16, F32 = jnp.bfloat16, jnp.float32
SUM_AFTER = 1
LAG = 2
MOST_CHUNKS = 24
TILE = 16
BUFFERS = 3
FETCHED = 4
VMEM = 50 << 20

ANY = pl.BlockSpec(memory_space=pl.ANY)
SMEM = pl.BlockSpec(memory_space=pltpu.SMEM)
WHOLE = pl.BlockSpec(memory_space=pltpu.VMEM)
PARAMS = pltpu.CompilerParams(vmem_limit_bytes=VMEM)


def ring_order(n):
    return [0, 1, 3, 2] if n == 4 else list(range(n))


def entry(table, index):
    found = jnp.int32(0)
    for at, value in enumerate(table):
        found = jnp.where(index == at, jnp.int32(value), found)
    return found


class Roles:
    def __init__(self, failed, n):
        self.n = n
        self.order = ring_order(n)
        self.spots = [self.order.index(i) for i in range(n)]
        self.me = lax.axis_index("replica").astype(jnp.int32)
        self.failed = failed[0]
        self.source = lax.rem(self.failed + 1, n)
        self.lost = self.me == self.failed

    def ahead(self):
        apart = entry(self.spots, self.failed) - entry(self.spots, self.source)
        return lax.rem(apart + self.n, self.n)

    def neighbour(self, hops):
        spot = lax.rem(entry(self.spots, self.me) + hops, self.n)
        return entry(self.order, spot)


def largest(options, default):
    options = list(options)
    return max(options) if options else default


def shares(total, parts):
    parts = min(parts, total)
    edges = [total * i // parts for i in range(parts + 1)]
    return [(a, b - a) for a, b in zip(edges, edges[1:])]


def row_group(rows):
    return largest((g for g in (16, 32) if rows % g == 0), rows)


def cost(flops, bytes_accessed, transcendentals=0):
    return pl.CostEstimate(
        flops=flops, bytes_accessed=bytes_accessed, transcendentals=transcendentals
    )


def updated(master_old, first_old, second_old, total, healthy):
    first_new = 0.9 * first_old + (0.1 / healthy) * total
    second_new = 0.95 * second_old + (0.05 / healthy**2) * (total * total)
    root = second_new * lax.rsqrt(second_new)
    step = first_new * pl.reciprocal(root + 1e-08)
    return master_old - 0.01 * step, first_new, second_new


def column_pieces(lengths, width):
    moves, column = [], 0
    for part, length in enumerate(lengths):
        begin = 0
        while begin < length:
            piece, to = divmod(column, width)
            run = min(length - begin, width - to)
            moves.append((part, begin, piece, to, run))
            begin, column = begin + run, column + run
    return moves


def pack_body(*refs, n, places, chunk, slabs, passed, counts):
    count_seen, count_parts, count_after = counts
    if count_seen:
        roles, refs = Roles(refs[0], n), refs[1:]
    state = refs[0:3]
    seen = refs[3 : 3 + count_seen]
    rest = refs[3 + count_seen :]
    if count_parts:
        both, parts, rest = rest[0], rest[1 : 1 + count_parts], rest[1 + count_parts :]
    sends = rest[count_after : count_after + 2]
    held, made, sem, out_sem, below_sem = rest[count_after + 2 :]
    width = held.shape[2]
    size = 3 * chunk

    def rows_of(j):
        way, k = divmod(j, 3)
        return way, pl.ds(k * chunk, chunk)

    def fetch(j):
        way, k = divmod(j, 3)
        rows = pl.ds(places[way] * chunk, chunk)
        return pltpu.make_async_copy(state[k].at[1, rows], held.at[j], sem.at[j])

    def take(j):
        way, rows = rows_of(j)
        return pltpu.make_async_copy(seen[way].at[rows], made.at[way, rows], sem.at[j])

    def store(j):
        way, rows = rows_of(j)
        return pltpu.make_async_copy(
            made.at[way, rows], sends[way].at[rows], out_sem.at[j]
        )

    def convert():
        for j in range(6):
            fetch(j).start()
        for j in range(6):
            way, rows = rows_of(j)
            fetch(j).wait()
            made[way, rows] = held[j].astype(BF16)
            store(j).start()
        for j in range(6):
            store(j).wait()

    def relay():
        for j in range(6):
            take(j).start()
        for j in range(6):
            take(j).wait()
            store(j).start()
        for j in range(6):
            store(j).wait()

    def below(way, inward):
        rows = pl.ds(size, passed[way] or sends[way].shape[0] - size)
        here = made.at[way, rows]
        if inward:
            return pltpu.make_async_copy(seen[way].at[rows], here, below_sem.at[way])
        return pltpu.make_async_copy(here, sends[way].at[rows], below_sem.at[way])

    for way in range(2):
        if passed[way]:
            below(way, True).start()
        if slabs[way]:
            tokens, features = both.shape[0], both.shape[1] // 2
            moves = column_pieces([part.shape[1] for part in parts], width)
            for part, begin, piece, to, run in moves:
                units = parts[part][:, begin : begin + run]
                made[way, pl.ds(size + piece * tokens, tokens), pl.ds(to, run)] = (
                    jnp.where(roles.lost, jnp.zeros_like(units), units)
                )
            row = size + (1 + moves[-1][2]) * tokens
            for far in range(slabs[way], 0, -1):
                target = roles.neighbour(far if way == 0 else n - far)
                slab = pl.ds(pl.multiple_of(features + target * width, 128), width)
                made[way, pl.ds(row, tokens)] = both[:, slab]
                row += tokens
            below(way, False).start()

    for way in range(2):
        if passed[way]:
            below(way, True).wait()
            below(way, False).start()

    if seen:
        pl.when(roles.me == roles.source)(convert)
        pl.when(roles.me != roles.source)(relay)
    else:
        convert()

    for way in range(2):
        if slabs[way] or passed[way]:
            below(way, False).wait()


def pack(failed, n, state, seen, parcel, after, places, chunk, slabs, passed):
    width = state[0].shape[2]
    extra = list(passed)
    if parcel:
        tokens = parcel[0].shape[0]
        pieces = -(-sum(part.shape[1] for part in parcel[1:]) // width)
        extra = [tokens * (pieces + count) if count else 0 for count in slabs]
    counts = (len(seen), max(len(parcel) - 1, 0), len(after))
    return pl.pallas_call(
        functools.partial(
            pack_body,
            n=n,
            places=places,
            chunk=chunk,
            slabs=slabs,
            passed=passed,
            counts=counts,
        ),
        in_specs=[SMEM] * bool(seen)
        + [ANY] * (3 + len(seen))
        + [WHOLE] * len(parcel)
        + [ANY] * len(after),
        out_specs=[ANY, ANY],
        out_shape=[
            jax.ShapeDtypeStruct((3 * chunk + more, width), BF16) for more in extra
        ],
        scratch_shapes=[
            pltpu.VMEM((6, chunk, width), F32),
            pltpu.VMEM((2, 3 * chunk + max(extra), width), BF16),
            pltpu.SemaphoreType.DMA((6,)),
            pltpu.SemaphoreType.DMA((6,)),
            pltpu.SemaphoreType.DMA((2,)),
        ],
        compiler_params=PARAMS,
        cost_estimate=cost(0, 2 * 3 * chunk * width * 6),
        name="pack",
    )(*([failed] if seen else []), *state, *seen, *parcel, *after)


def beside_body(*refs):
    tokens, d_out, out = refs[0], refs[1], refs[-1]
    width = tokens.shape[1]
    out[0, :, :width] = tokens[...]
    out[0, :, width:] = d_out[...]


def beside(tokens, d_out, after):
    rows, width = tokens.shape
    return pl.pallas_call(
        beside_body,
        in_specs=[WHOLE, WHOLE] + [ANY] * len(after),
        out_specs=WHOLE,
        out_shape=jax.ShapeDtypeStruct((1, rows, 2 * width), tokens.dtype),
        compiler_params=PARAMS,
        cost_estimate=cost(0, 4 * rows * width * 2),
        name="beside",
    )(tokens, d_out, *after)


def join_body(own, other, *refs, axis, apart, last):
    out = refs[-1]
    count, rows = own.shape[:2]
    second = lax.rem(lax.div(lax.axis_index(axis).astype(jnp.int32), apart), 2)
    if not last:
        out[pl.ds(second * count, count)] = own[...]
        out[pl.ds((1 - second) * count, count)] = other[...]
        return
    for i in range(2 * count):
        here, there = (own, other) if i < count else (other, own)
        value = jnp.where(second == 1, there[i % count], here[i % count])
        out[pl.ds(i * rows, rows)] = value


def join(own, other, after, axis, apart, last):
    count, rows, width = own.shape
    shape = (2 * count * rows, width) if last else (2 * count, rows, width)
    return pl.pallas_call(
        functools.partial(join_body, axis=axis, apart=apart, last=last),
        in_specs=[WHOLE, WHOLE] + [ANY] * len(after),
        out_specs=WHOLE,
        out_shape=jax.ShapeDtypeStruct(shape, own.dtype),
        compiler_params=PARAMS,
        cost_estimate=cost(0, 8 * count * rows * width),
        name="join",
    )(own, other, *after)


def by_rows(a, b):
    return lax.dot_general(a, b, (((1,), (1,)), ((), ())), preferred_element_type=F32)


def layer_body(both, *refs, resumed, tile, first, count):
    weights = refs[:3]
    hidden_ref, sum_ref = refs[-2:]
    features = weights[0].shape[0]
    rows = both.shape[0]
    joined = tile % 128 == 0
    sum_ref[...] = refs[3][...] if resumed else jnp.zeros_like(sum_ref)

    def step(gate_ref, up_ref, down_ref, hidden):
        x, dy = both[:, :features], both[:, features:]
        w_gate, w_up = gate_ref[...], up_ref[...]
        if joined:
            w_both = jnp.concatenate([w_gate, w_up], axis=1)
            gate_up = jnp.dot(x, w_both, preferred_element_type=F32)
            gate, up = gate_up[:, :tile], gate_up[:, tile:]
        else:
            gate = jnp.dot(x, w_gate, preferred_element_type=F32)
            up = jnp.dot(x, w_up, preferred_element_type=F32)
        d_hidden = by_rows(dy, down_ref[...])
        sig = 1.0 / (1.0 + jnp.exp(-gate))
        hidden[...] = (gate * sig * up).astype(BF16)
        d_gate = (d_hidden * up * sig * (1.0 + gate * (1.0 - sig))).astype(BF16)
        d_up = (d_hidden * gate * sig).astype(BF16)
        if joined:
            sum_ref[...] += by_rows(jnp.concatenate([d_gate, d_up], axis=1), w_both)
        else:
            sum_ref[...] += by_rows(d_gate, w_gate) + by_rows(d_up, w_up)

    deep = pl.Buffered(min(BUFFERS, count + 1))
    across = pl.BlockSpec((features, tile), lambda i: (0, first + i), pipeline_mode=deep)
    pltpu.emit_pipeline(
        step,
        grid=(count,),
        in_specs=[
            across,
            across,
            pl.BlockSpec((tile, features), lambda i: (first + i, 0), pipeline_mode=deep),
        ],
        out_specs=[pl.BlockSpec((rows, tile), lambda i: (0, i))],
    )(*weights, hidden_ref)


def layer(both, w_gate, w_up, w_down, partial_sum, after, tile, first, count):
    rows = both.shape[0]
    features = w_gate.shape[0]
    resumed = partial_sum is not None
    return pl.pallas_call(
        functools.partial(layer_body, resumed=resumed, tile=tile, first=first, count=count),
        in_specs=[WHOLE] + [ANY] * 3 + [WHOLE] * resumed + [ANY] * len(after),
        out_specs=[ANY, WHOLE],
        out_shape=[
            jax.ShapeDtypeStruct((rows, count * tile), BF16),
            jax.ShapeDtypeStruct((rows, features), F32),
        ],
        compiler_params=PARAMS,
        cost_estimate=cost(
            10 * rows * features * count * tile,
            3 * features * count * tile * 2,
            rows * count * tile,
        ),
        name="layer",
    )(both, w_gate, w_up, w_down, *([partial_sum] if resumed else []), *after)


def halve_body(bit, *refs, arrived, final):
    value = refs[0][...]
    if arrived:
        value = value + refs[1][...]
    if final:
        refs[-1][...] = value.astype(BF16)
        return
    kept, sent = refs[-2:]
    half = value.shape[0] // 2
    low, high = value[:half], value[half:]
    upper = bit[0] == 1
    kept[...] = jnp.where(upper, high, low)
    sent[...] = jnp.where(upper, low, high)


def halve(bit, value, arrived, after, final):
    rows, features = value.shape
    if final:
        out_shape = jax.ShapeDtypeStruct((rows, features), BF16)
    else:
        out_shape = [jax.ShapeDtypeStruct((rows // 2, features), F32)] * 2
    return pl.pallas_call(
        functools.partial(halve_body, arrived=bool(arrived), final=final),
        in_specs=[SMEM] + [WHOLE] * (1 + len(arrived)) + [ANY] * len(after),
        out_specs=WHOLE if final else [WHOLE, WHOLE],
        out_shape=out_shape,
        compiler_params=PARAMS,
        cost_estimate=cost(0, 3 * rows * features * 4),
        name="halve",
    )(bit, value, *arrived, *after)


class ScatteredSum:
    def __init__(self, value, axes):
        sizes = [lax.axis_size(axis) for axis in axes]
        self.value, self.arrived, self.levels = value, (), []
        self.done = any(size & (size - 1) for size in sizes)
        if self.done:
            summed = lax.psum_scatter(value, axes, scatter_dimension=0, tiled=True)
            self.value = summed.astype(BF16)
            return
        for axis, size in zip(axes, sizes):
            apart = size // 2
            while apart:
                self.levels.append((axis, size, apart))
                apart //= 2

    def advance(self, after):
        if self.done:
            return ()
        if self.levels:
            axis, size, apart = self.levels.pop(0)
            bit = ((lax.axis_index(axis) // apart) % 2).astype(jnp.int32)[None]
            self.value, sent = halve(bit, self.value, self.arrived, after, False)
            route = [(i, i ^ apart) for i in range(size)]
            self.arrived = (lax.ppermute(sent, axis, route),)
        else:
            bit = jnp.zeros((1,), jnp.int32)
            self.value = halve(bit, self.value, self.arrived, after, True)
            self.done = True
        return (self.value,)


def collect_body(failed, both, *refs, n, places, parts_count, size, pieces):
    roles = Roles(failed, n)
    parts = refs[:parts_count]
    blocks = refs[parts_count : parts_count + len(places)]
    hidden_t, outs, held, sem = refs[-4:]
    tokens, features = both.shape[0], both.shape[1] // 2
    width = outs.shape[1]

    def fetch(j, part):
        rows = pl.ds(size, pieces * tokens) if part == 0 else pl.ds(places[j], tokens)
        here = pl.ds(0, pieces * tokens) if part == 0 else pl.ds(pieces * tokens, tokens)
        return pltpu.make_async_copy(
            blocks[j].at[rows], held.at[j + 1, here], sem.at[j, part]
        )

    for j in range(len(places)):
        for part in range(2):
            fetch(j, part).start()
    for part, begin, piece, to, run in column_pieces([p.shape[1] for p in parts], width):
        units = parts[part][:, begin : begin + run]
        held[0, pl.ds(piece * tokens, tokens), pl.ds(to, run)] = jnp.where(
            roles.lost, jnp.zeros_like(units), units
        )
    slab = pl.ds(pl.multiple_of(features + roles.me * width, 128), width)
    held[0, pl.ds(pieces * tokens, tokens)] = both[:, slab]
    for j in range(len(places)):
        for part in range(2):
            fetch(j, part).wait()

    count = len(places) + 1
    for j in range(count):
        outs[pl.ds(j * tokens, tokens)] = held[j, pl.ds(pieces * tokens, tokens)]
    for piece in range(pieces):
        run = min(width, hidden_t.shape[0] - piece * width)
        rows = pl.ds(piece * tokens, tokens)
        hidden = jnp.concatenate([held[j, rows, :run] for j in range(count)], axis=0)
        hidden_t[pl.ds(piece * width, run)] = hidden.astype(F32).T.astype(BF16)


def collect(failed, n, both, parts, blocks, places, size, width, after):
    tokens = both.shape[0]
    units = sum(part.shape[1] for part in parts)
    pieces = -(-units // width)
    depth = tokens * (len(blocks) + 1)
    return pl.pallas_call(
        functools.partial(
            collect_body,
            n=n,
            places=places,
            parts_count=len(parts),
            size=size,
            pieces=pieces,
        ),
        in_specs=[SMEM]
        + [WHOLE] * (1 + len(parts))
        + [ANY] * (len(blocks) + len(after)),
        out_specs=[WHOLE, WHOLE],
        out_shape=[
            jax.ShapeDtypeStruct((units, depth), BF16),
            jax.ShapeDtypeStruct((depth, width), BF16),
        ],
        scratch_shapes=[
            pltpu.VMEM((len(blocks) + 1, (pieces + 1) * tokens, width), BF16),
            pltpu.SemaphoreType.DMA((len(blocks), 2)),
        ],
        compiler_params=PARAMS,
        cost_estimate=cost(0, 4 * depth * (units + width)),
        name="collect",
    )(failed, both, *parts, *blocks, *after)


def update_body(failed, hid_ref, out_ref, *refs, n, block, first, count, unread):
    state, news = refs[:3], refs[3 + unread : 6 + unread]
    total = refs[6 + unread]
    width = out_ref.shape[1]
    group = row_group(block)

    def step(hid, m_ref, a_ref, b_ref, m_new, a_new, b_new):
        total[...] = jnp.dot(hid[...], out_ref[...], preferred_element_type=F32)

        @pl.loop(0, block // group)
        def _(i):
            here = pl.ds(pl.multiple_of(i * group, group), group)
            m_new[here], a_new[here], b_new[here] = updated(
                m_ref[0, here], a_ref[0, here], b_ref[0, here], total[here], n - 1.0
            )

    deep = pl.Buffered(min(BUFFERS, count + 1))
    old = pl.BlockSpec(
        (1, block, width), lambda i: (0, first + i, 0), pipeline_mode=deep
    )
    new = pl.BlockSpec((block, width), lambda i: (first + i, 0))

    @pl.when(jnp.logical_not(Roles(failed, n).lost))
    def _():
        pltpu.emit_pipeline(
            step,
            grid=(count,),
            in_specs=[
                pl.BlockSpec((block, hid_ref.shape[1]), lambda i: (first + i, 0)),
                old,
                old,
                old,
            ],
            out_specs=[new] * 3,
        )(hid_ref, *state, *news)


def update(failed, n, hidden_t, outs, state, news, after, block, first, count):
    _, rows, width = state[0].shape
    depth = hidden_t.shape[1]
    shape = jax.ShapeDtypeStruct((rows, width), F32)
    unread = len(news) + len(after)
    return pl.pallas_call(
        functools.partial(
            update_body,
            n=n,
            block=block,
            first=first,
            count=count,
            unread=unread,
        ),
        in_specs=[SMEM, ANY, WHOLE] + [ANY] * (3 + unread),
        out_specs=[ANY] * 3,
        out_shape=[shape] * 3,
        scratch_shapes=[pltpu.VMEM((block, width), F32)],
        input_output_aliases={6 + k: k for k in range(len(news))},
        compiler_params=PARAMS,
        cost_estimate=cost(
            2 * count * block * width * depth,
            6 * count * block * width * 4,
            2 * count * block * width,
        ),
        name="update",
    )(failed, hidden_t, outs, *state, *news, *after)


def patch_body(failed, hid_ref, out_ref, *refs, arrivals, chunks, n, count_after):
    count = len(arrivals)
    got = refs[:count]
    rest = refs[count + 3 + count_after :]
    news = rest[:3]
    held, made, total, in_sem, out_sem = rest[3:]
    chunk = made.shape[2]
    group = row_group(chunk)
    roles = Roles(failed, n)
    ahead = roles.ahead()
    lag_of = {True: LAG * (ahead - 1), False: LAG * (n - ahead - 1)}

    def fetch(j):
        rows = got[j].at[pl.ds(0, 3 * chunk)]
        return pltpu.make_async_copy(rows, held.at[j % FETCHED], in_sem.at[j % FETCHED])

    def first_row(j):
        step, forward = arrivals[j]
        place = step - lag_of[forward]
        if not forward:
            place = chunks - 1 - place
        return pl.multiple_of(jnp.clip(place, 0, chunks - 1) * chunk, TILE)

    def store(j, k):
        return pltpu.make_async_copy(
            made.at[j % BUFFERS, k],
            news[k].at[pl.ds(first_row(j), chunk)],
            out_sem.at[j % BUFFERS, k],
        )

    def valid(j):
        step, forward = arrivals[j]
        return step >= lag_of[forward]

    def finish(j):
        @pl.when(valid(j))
        def _():
            for k in range(3):
                store(j, k).wait()

    @pl.when(roles.lost)
    def _():
        for j in range(min(FETCHED - 1, count)):
            fetch(j).start()
        for j in range(count):
            if j + FETCHED - 1 < count:
                fetch(j + FETCHED - 1).start()
            fetch(j).wait()
            if j >= BUFFERS:
                finish(j - BUFFERS)

            @pl.when(valid(j))
            def _(j=j, slot=j % FETCHED, out_slot=j % BUFFERS):
                first = first_row(j)

                units = hid_ref[pl.ds(first, chunk)]
                total[...] = jnp.dot(units, out_ref[...], preferred_element_type=F32)

                @pl.loop(0, chunk // group)
                def _(i):
                    base = pl.multiple_of(i * group, group)
                    old = [
                        held[slot, pl.ds(k * chunk + base, group)].astype(F32)
                        for k in range(3)
                    ]
                    new = updated(*old, total[pl.ds(base, group)], n - 1.0)
                    for k in range(3):
                        made[out_slot, k, pl.ds(base, group)] = new[k]

                for k in range(3):
                    store(j, k).start()

        for j in range(max(count - BUFFERS, 0), count):
            finish(j)


def patch(failed, n, hidden_t, outs, got, arrivals, news, after, chunks):
    rows, width = news[0].shape
    chunk = rows // chunks
    count = len(got)
    shape = jax.ShapeDtypeStruct((rows, width), F32)
    return pl.pallas_call(
        functools.partial(
            patch_body, arrivals=arrivals, chunks=chunks, n=n, count_after=len(after)
        ),
        in_specs=[SMEM, WHOLE, WHOLE] + [ANY] * (count + 3 + len(after)),
        out_specs=[ANY] * 3,
        out_shape=[shape] * 3,
        scratch_shapes=[
            pltpu.VMEM((FETCHED, 3 * chunk, width), BF16),
            pltpu.VMEM((BUFFERS, 3, chunk, width), F32),
            pltpu.VMEM((chunk, width), F32),
            pltpu.SemaphoreType.DMA((FETCHED,)),
            pltpu.SemaphoreType.DMA((BUFFERS, 3)),
        ],
        input_output_aliases={3 + count + k: k for k in range(3)},
        compiler_params=PARAMS,
        cost_estimate=cost(
            2 * count * chunk * width * hidden_t.shape[1],
            count * 3 * chunk * width * 6,
            2 * count * chunk * width,
        ),
        name="patch",
    )(failed, hidden_t, outs, *got, *news, *after)


def per_device(tokens, d_out, w_gate, w_up, w_down, failed, master, moment1, moment2):
    n = lax.axis_size("replica")
    _, rows, width = master.shape
    features, units = w_gate.shape

    order = ring_order(n)

    state = (master, moment1, moment2)
    chunks = largest(
        (c for c in range(2, MOST_CHUNKS + 1, 2) if rows % (TILE * c) == 0), 2
    )
    chunk = rows // chunks
    steps = (chunks + LAG * (n - 2)) // 2
    reach = (n // 2, (n - 1) // 2)
    forward = [(order[p], order[(p + 1) % n]) for p in range(n)]
    backward = [(b, a) for a, b in forward]
    sends, got = [], []
    parcel_from = None

    def send(*after, parcel=()):
        nonlocal parcel_from
        step = len(got)
        seen = got[step - LAG] if step >= LAG else ()
        here = min(step, chunks - 1)
        slabs, passed = (0, 0), (0, 0)
        if parcel:
            parcel_from, slabs = step, reach
        elif parcel_from is not None and (step - parcel_from) % LAG == 0:
            hop = (step - parcel_from) // LAG
            passed = tuple(
                seen[way].shape[0] - 3 * chunk - both.shape[0]
                if hop < reach[way]
                else 0
                for way in range(2)
            )
        sends.append(
            pack(
                failed,
                n,
                state,
                seen,
                parcel,
                after,
                (here, chunks - 1 - here),
                chunk,
                slabs,
                passed,
            )
        )
        got.append(
            (
                lax.ppermute(sends[-1][0], "replica", forward),
                lax.ppermute(sends[-1][1], "replica", backward),
            )
        )
        return (sends[-1][0],)

    sent = send()
    both = beside(tokens[0], d_out[0], sent)
    exchanges = []
    for axis in ("tensor", "fsdp"):
        size = lax.axis_size(axis)
        exchanges += [(axis, size, 1 << k) for k in range((size - 1).bit_length())]
    if all(size & (size - 1) == 0 for _, size, _ in exchanges):
        for level, (axis, size, apart) in enumerate(exchanges):
            last = level == len(exchanges) - 1
            other = lax.ppermute(both, axis, [(i, i ^ apart) for i in range(size)])
            after = ()
            if level == 0 or last:
                after = sent = send(both)
            both = join(both, other, after, axis, apart, last)
    else:
        sent = send(both)
        both = lax.all_gather(both[0], ("fsdp", "tensor"), axis=0, tiled=True)
        sent = send(both)

    tile = 128 if units % 128 == 0 else units
    hidden, d_rows = [], None
    pieces = shares(units // tile, 4)
    for first, count in pieces:
        part, d_rows = layer(both, w_gate, w_up, w_down, d_rows, sent, tile, first, count)
        hidden.append(part)
        last = len(hidden) == len(pieces)
        sent = send(d_rows, parcel=(both, *hidden) if last else ())
    cotangents = ScatteredSum(d_rows, ("fsdp", "tensor"))

    news = ()
    patched = 0
    hidden_t = outs = None

    def gathered(after):
        blocks, places = [], []
        for way in range(2):
            for hop in range(reach[way]):
                blocks.append(got[parcel_from + LAG * hop][way])
                places.append(blocks[-1].shape[0] - both.shape[0])
        return collect(
            failed, n, both, hidden, blocks, places, 3 * chunk, width, after
        )

    def update_part(first, count, after):
        return update(
            failed, n, hidden_t, outs, state, news, after, block, first, count
        )

    def patch_to(step, after):
        nonlocal patched
        arrivals = [(s, way) for s in range(patched, step) for way in (True, False)]
        if not arrivals:
            return news
        blocks = [b for s in range(patched, step) for b in got[s]]
        patched = step
        return patch(failed, n, hidden_t, outs, blocks, arrivals, news, after, chunks)

    block = largest((b for b in range(TILE, 193, TILE) if rows % b == 0), rows)
    blocks = rows // block
    early = blocks // 4
    ready = parcel_from + LAG * reach[0] + 1
    while len(got) < steps:
        ready_sum = len(got) > parcel_from + SUM_AFTER
        sent = send(*(cotangents.advance(sent) if ready_sum else ()), *news[:1])
        if len(got) == ready and early and len(got) < steps:
            hidden_t, outs = gathered(sent)
            news = update_part(0, early, (hidden_t,))
            news = patch_to(len(got) // 2, ())
    if hidden_t is None:
        hidden_t, outs = gathered(sent)
        early = 0
    news = update_part(early, blocks - early, sent)
    for step in (steps - 2, steps - 1, steps):
        news = patch_to(step, ())
    while not cotangents.done:
        cotangents.advance(sent)
    return (cotangents.value[None], *news)


def solution(mesh):
    placed = (
        P("replica", ("fsdp", "tensor"), None),
        P("replica", ("fsdp", "tensor"), None),
        P(None, ("fsdp", "tensor")),
        P(None, ("fsdp", "tensor")),
        P(("fsdp", "tensor"), None),
        P(("fsdp", "tensor")),
        P(None, ("fsdp", "tensor"), "replica"),
        P(None, ("fsdp", "tensor"), "replica"),
        P(None, ("fsdp", "tensor"), "replica"),
    )
    return jax.shard_map(
        per_device,
        mesh=mesh,
        in_specs=placed,
        out_specs=(
            P("replica", ("fsdp", "tensor"), None),
            P(("fsdp", "tensor"), "replica"),
            P(("fsdp", "tensor"), "replica"),
            P(("fsdp", "tensor"), "replica"),
        ),
        check_vma=False,
    )
```

```python
import functools

import jax
import jax.numpy as jnp
from jax import lax
from jax.experimental import pallas as pl
from jax.experimental.pallas import tpu as pltpu
from jax.sharding import PartitionSpec as P

BF16, F32 = jnp.bfloat16, jnp.float32
SUM_AFTER = 1
LAG = 2
MOST_CHUNKS = 24
TILE = 16
BUFFERS = 3
PIECES = 4
FETCHED = 4
VMEM = 50 << 20

ANY = pl.BlockSpec(memory_space=pl.ANY)
SMEM = pl.BlockSpec(memory_space=pltpu.SMEM)
WHOLE = pl.BlockSpec(memory_space=pltpu.VMEM)
PARAMS = pltpu.CompilerParams(vmem_limit_bytes=VMEM)


def ring_order(n):
    return [0, 1, 3, 2] if n == 4 else list(range(n))


def entry(table, index):
    found = jnp.int32(0)
    for at, value in enumerate(table):
        found = jnp.where(index == at, jnp.int32(value), found)
    return found


class Roles:
    def __init__(self, failed, n):
        self.n = n
        self.order = ring_order(n)
        self.spots = [self.order.index(i) for i in range(n)]
        self.me = lax.axis_index("replica").astype(jnp.int32)
        self.failed = failed[0]
        self.source = lax.rem(self.failed + 1, n)
        self.lost = self.me == self.failed

    def ahead(self):
        apart = entry(self.spots, self.failed) - entry(self.spots, self.source)
        return lax.rem(apart + self.n, self.n)

    def neighbour(self, hops):
        spot = lax.rem(entry(self.spots, self.me) + hops, self.n)
        return entry(self.order, spot)


def largest(options, default):
    options = list(options)
    return max(options) if options else default


def shares(total, parts):
    parts = min(parts, total)
    edges = [total * i // parts for i in range(parts + 1)]
    return [(a, b - a) for a, b in zip(edges, edges[1:])]


def row_group(rows):
    return largest((g for g in (16, 32) if rows % g == 0), rows)


def cost(flops, bytes_accessed, transcendentals=0):
    return pl.CostEstimate(
        flops=flops, bytes_accessed=bytes_accessed, transcendentals=transcendentals
    )


def updated(master_old, first_old, second_old, total, healthy):
    first_new = 0.9 * first_old + (0.1 / healthy) * total
    second_new = 0.95 * second_old + (0.05 / healthy**2) * (total * total)
    root = second_new * lax.rsqrt(second_new)
    step = first_new * pl.reciprocal(root + 1e-08)
    return master_old - 0.01 * step, first_new, second_new


def column_pieces(lengths, width):
    moves, column = [], 0
    for part, length in enumerate(lengths):
        begin = 0
        while begin < length:
            piece, to = divmod(column, width)
            run = min(length - begin, width - to)
            moves.append((part, begin, piece, to, run))
            begin, column = begin + run, column + run
    return moves


class Packing:
    def __init__(self, failed, n, state, seen, sends, scratch, plan):
        self.state, self.seen, self.sends, self.n = state, seen, sends, n
        self.held, self.made, self.sem, self.out_sem, self.below_sem = scratch
        self.places, self.chunk, self.slabs, self.passed = plan
        self.size = 3 * self.chunk
        self.roles = Roles(failed, n) if seen else None

    def rows_of(self, j):
        way, k = divmod(j, 3)
        return way, pl.ds(k * self.chunk, self.chunk)

    def fetch(self, j):
        way, k = divmod(j, 3)
        rows = pl.ds(self.places[way] * self.chunk, self.chunk)
        return pltpu.make_async_copy(
            self.state[k].at[1, rows], self.held.at[j], self.sem.at[j]
        )

    def take(self, j):
        way, rows = self.rows_of(j)
        return pltpu.make_async_copy(
            self.seen[way].at[rows], self.made.at[way, rows], self.sem.at[j]
        )

    def store(self, j):
        way, rows = self.rows_of(j)
        return pltpu.make_async_copy(
            self.made.at[way, rows], self.sends[way].at[rows], self.out_sem.at[j]
        )

    def below(self, way, inward):
        count = self.passed[way] or self.sends[way].shape[0] - self.size
        rows = pl.ds(self.size, count)
        here, sem = self.made.at[way, rows], self.below_sem.at[way]
        if inward:
            return pltpu.make_async_copy(self.seen[way].at[rows], here, sem)
        return pltpu.make_async_copy(here, self.sends[way].at[rows], sem)

    def by_role(self, on_source, elsewhere):
        if not self.seen:
            on_source()
            return
        pl.when(self.roles.me == self.roles.source)(on_source)
        pl.when(self.roles.me != self.roles.source)(elsewhere)

    def start(self):
        def fetch_all():
            for j in range(6):
                self.fetch(j).start()

        def take_all():
            for j in range(6):
                self.take(j).start()

        self.by_role(fetch_all, take_all)
        for way in range(2):
            if self.passed[way]:
                self.below(way, True).start()

    def turn_round(self):
        def convert():
            for j in range(6):
                way, rows = self.rows_of(j)
                self.fetch(j).wait()
                self.made[way, rows] = self.held[j].astype(BF16)
                self.store(j).start()

        def relay():
            for j in range(6):
                self.take(j).wait()
                self.store(j).start()

        self.by_role(convert, relay)
        for way in range(2):
            if self.passed[way]:
                self.below(way, True).wait()
                self.below(way, False).start()

    def add_parcels(self, both, parts):
        tokens, features = both.shape[0], both.shape[1] // 2
        width = self.held.shape[2]
        moves = column_pieces([part.shape[1] for part in parts], width)
        for way in range(2):
            if not self.slabs[way]:
                continue
            for part, begin, piece, to, run in moves:
                units = parts[part][:, begin : begin + run]
                rows = pl.ds(self.size + piece * tokens, tokens)
                self.made[way, rows, pl.ds(to, run)] = jnp.where(
                    self.roles.lost, jnp.zeros_like(units), units
                )
            row = self.size + (1 + moves[-1][2]) * tokens
            for far in range(self.slabs[way], 0, -1):
                target = self.roles.neighbour(far if way == 0 else self.n - far)
                slab = pl.ds(pl.multiple_of(features + target * width, 128), width)
                self.made[way, pl.ds(row, tokens)] = both[:, slab]
                row += tokens
            self.below(way, False).start()

    def finish(self):
        for j in range(6):
            self.store(j).wait()
        for way in range(2):
            if self.slabs[way] or self.passed[way]:
                self.below(way, False).wait()


def packed_shapes(extra, chunk, width):
    shapes = [jax.ShapeDtypeStruct((3 * chunk + more, width), BF16) for more in extra]
    scratch = [
        pltpu.VMEM((6, chunk, width), F32),
        pltpu.VMEM((2, 3 * chunk + max(extra), width), BF16),
        pltpu.SemaphoreType.DMA((6,)),
        pltpu.SemaphoreType.DMA((6,)),
        pltpu.SemaphoreType.DMA((2,)),
    ]
    return shapes, scratch


def pack_body(*refs, n, plan, count_seen, count_after):
    failed, refs = (refs[0], refs[1:]) if count_seen else (None, refs)
    state, seen = refs[0:3], refs[3 : 3 + count_seen]
    rest = refs[3 + count_seen + count_after :]
    packing = Packing(failed, n, state, seen, rest[:2], rest[2:], plan)
    packing.start()
    packing.turn_round()
    packing.finish()


def pack(failed, n, state, seen, after, extra, plan):
    chunk, width = plan[1], state[0].shape[2]
    shapes, scratch = packed_shapes(extra, chunk, width)
    return pl.pallas_call(
        functools.partial(
            pack_body, n=n, plan=plan, count_seen=len(seen), count_after=len(after)
        ),
        in_specs=[SMEM] * bool(seen) + [ANY] * (3 + len(seen) + len(after)),
        out_specs=[ANY, ANY],
        out_shape=shapes,
        scratch_shapes=scratch,
        compiler_params=PARAMS,
        cost_estimate=cost(0, 2 * 3 * chunk * width * 6),
        name="pack",
    )(*([failed] if seen else []), *state, *seen, *after)


def beside_body(*refs):
    tokens, d_out, out = refs[0], refs[1], refs[-1]
    width = tokens.shape[1]
    out[0, :, :width] = tokens[...]
    out[0, :, width:] = d_out[...]


def beside(tokens, d_out, after):
    rows, width = tokens.shape
    return pl.pallas_call(
        beside_body,
        in_specs=[WHOLE, WHOLE] + [ANY] * len(after),
        out_specs=WHOLE,
        out_shape=jax.ShapeDtypeStruct((1, rows, 2 * width), tokens.dtype),
        compiler_params=PARAMS,
        cost_estimate=cost(0, 4 * rows * width * 2),
        name="beside",
    )(tokens, d_out, *after)


def join_body(own, other, *refs, axis, apart, last):
    out = refs[-1]
    count, rows = own.shape[:2]
    second = lax.rem(lax.div(lax.axis_index(axis).astype(jnp.int32), apart), 2)
    if not last:
        out[pl.ds(second * count, count)] = own[...]
        out[pl.ds((1 - second) * count, count)] = other[...]
        return
    for i in range(2 * count):
        here, there = (own, other) if i < count else (other, own)
        value = jnp.where(second == 1, there[i % count], here[i % count])
        out[pl.ds(i * rows, rows)] = value


def join(own, other, after, axis, apart, last):
    count, rows, width = own.shape
    shape = (2 * count * rows, width) if last else (2 * count, rows, width)
    return pl.pallas_call(
        functools.partial(join_body, axis=axis, apart=apart, last=last),
        in_specs=[WHOLE, WHOLE] + [ANY] * len(after),
        out_specs=WHOLE,
        out_shape=jax.ShapeDtypeStruct(shape, own.dtype),
        compiler_params=PARAMS,
        cost_estimate=cost(0, 8 * count * rows * width),
        name="join",
    )(own, other, *after)


def by_rows(a, b):
    return lax.dot_general(a, b, (((1,), (1,)), ((), ())), preferred_element_type=F32)


def layer_body(failed, both, *refs, n, tile, first, count, plan, counts):
    count_sums, count_parts, count_seen, count_after = counts
    weights, refs = refs[:3], refs[3:]
    sums, refs = refs[:count_sums], refs[count_sums:]
    parts, refs = refs[:count_parts], refs[count_parts:]
    state, seen = refs[:3], refs[3 : 3 + count_seen]
    hidden_ref, sum_ref, *rest = refs[3 + count_seen + count_after :]
    done = rest[-1]
    packing = Packing(failed, n, state, seen, rest[:2], rest[2:-1], plan)
    features = weights[0].shape[0]
    joined = tile % 128 == 0

    packing.start()
    done[0] = 0
    sum_ref[...] = sums[0][...] if sums else jnp.zeros_like(sum_ref)

    def step(gate_ref, up_ref, down_ref):
        at = done[0]
        pl.when(at == min(1, count - 1))(packing.turn_round)
        x, dy = both[:, :features], both[:, features:]
        w_gate, w_up = gate_ref[...], up_ref[...]
        if joined:
            w_both = jnp.concatenate([w_gate, w_up], axis=1)
            gate_up = jnp.dot(x, w_both, preferred_element_type=F32)
            gate, up = gate_up[:, :tile], gate_up[:, tile:]
        else:
            gate = jnp.dot(x, w_gate, preferred_element_type=F32)
            up = jnp.dot(x, w_up, preferred_element_type=F32)
        d_hidden = by_rows(dy, down_ref[...])
        sig = 1.0 / (1.0 + jnp.exp(-gate))
        hidden = (gate * sig * up).astype(BF16)
        if count == 1:
            hidden_ref[...] = hidden
        else:
            hidden_ref[:, pl.ds(pl.multiple_of(at * tile, 128), tile)] = hidden
        d_gate = (d_hidden * up * sig * (1.0 + gate * (1.0 - sig))).astype(BF16)
        d_up = (d_hidden * gate * sig).astype(BF16)
        if joined:
            sum_ref[...] += by_rows(jnp.concatenate([d_gate, d_up], axis=1), w_both)
        else:
            sum_ref[...] += by_rows(d_gate, w_gate) + by_rows(d_up, w_up)
        done[0] = at + 1

    deep = pl.Buffered(min(BUFFERS, count + 1))
    across = pl.BlockSpec((features, tile), lambda i: (0, first + i), pipeline_mode=deep)
    pltpu.emit_pipeline(
        step,
        grid=(count,),
        in_specs=[
            across,
            across,
            pl.BlockSpec((tile, features), lambda i: (first + i, 0), pipeline_mode=deep),
        ],
    )(*weights)
    if any(packing.slabs):
        packing.add_parcels(both, [*parts, hidden_ref])
    packing.finish()


def layer(
    failed, n, both, weights, partial_sum, parts, state, seen, after, extra, plan, share, tile
):
    first, count = share
    rows, features = both.shape[0], weights[0].shape[0]
    chunk, width = plan[1], state[0].shape[2]
    sums = [] if partial_sum is None else [partial_sum]
    shapes, scratch = packed_shapes(extra, chunk, width)
    counts = (len(sums), len(parts), len(seen), len(after))
    return pl.pallas_call(
        functools.partial(
            layer_body, n=n, tile=tile, first=first, count=count, plan=plan, counts=counts
        ),
        in_specs=[SMEM, WHOLE]
        + [ANY] * 3
        + [WHOLE] * (len(sums) + len(parts))
        + [ANY] * (3 + len(seen) + len(after)),
        out_specs=[WHOLE, WHOLE, ANY, ANY],
        out_shape=[
            jax.ShapeDtypeStruct((rows, count * tile), BF16),
            jax.ShapeDtypeStruct((rows, features), F32),
            *shapes,
        ],
        scratch_shapes=[*scratch, pltpu.SMEM((1,), jnp.int32)],
        compiler_params=PARAMS,
        cost_estimate=cost(
            10 * rows * features * count * tile,
            3 * features * count * tile * 2,
            rows * count * tile,
        ),
        name="layer",
    )(failed, both, *weights, *sums, *parts, *state, *seen, *after)


def halve_body(bit, *refs, arrived, final):
    value = refs[0][...]
    if arrived:
        value = value + refs[1][...]
    if final:
        refs[-1][...] = value.astype(BF16)
        return
    kept, sent = refs[-2:]
    half = value.shape[0] // 2
    low, high = value[:half], value[half:]
    upper = bit[0] == 1
    kept[...] = jnp.where(upper, high, low)
    sent[...] = jnp.where(upper, low, high)


def halve(bit, value, arrived, after, final):
    rows, features = value.shape
    if final:
        out_shape = jax.ShapeDtypeStruct((rows, features), BF16)
    else:
        out_shape = [jax.ShapeDtypeStruct((rows // 2, features), F32)] * 2
    return pl.pallas_call(
        functools.partial(halve_body, arrived=bool(arrived), final=final),
        in_specs=[SMEM] + [WHOLE] * (1 + len(arrived)) + [ANY] * len(after),
        out_specs=WHOLE if final else [WHOLE, WHOLE],
        out_shape=out_shape,
        compiler_params=PARAMS,
        cost_estimate=cost(0, 3 * rows * features * 4),
        name="halve",
    )(bit, value, *arrived, *after)


class ScatteredSum:
    def __init__(self, value, axes):
        sizes = [lax.axis_size(axis) for axis in axes]
        self.value, self.arrived, self.levels = value, (), []
        self.done = any(size & (size - 1) for size in sizes)
        if self.done:
            summed = lax.psum_scatter(value, axes, scatter_dimension=0, tiled=True)
            self.value = summed.astype(BF16)
            return
        for axis, size in zip(axes, sizes):
            apart = size // 2
            while apart:
                self.levels.append((axis, size, apart))
                apart //= 2

    def advance(self, after):
        if self.done:
            return ()
        if self.levels:
            axis, size, apart = self.levels.pop(0)
            bit = ((lax.axis_index(axis) // apart) % 2).astype(jnp.int32)[None]
            self.value, sent = halve(bit, self.value, self.arrived, after, False)
            route = [(i, i ^ apart) for i in range(size)]
            self.arrived = (lax.ppermute(sent, axis, route),)
        else:
            bit = jnp.zeros((1,), jnp.int32)
            self.value = halve(bit, self.value, self.arrived, after, True)
            self.done = True
        return (self.value,)


def collect_body(failed, both, *refs, n, places, parts_count, size, pieces):
    roles = Roles(failed, n)
    parts = refs[:parts_count]
    blocks = refs[parts_count : parts_count + len(places)]
    hidden_t, outs, held, sem = refs[-4:]
    tokens, features = both.shape[0], both.shape[1] // 2
    width = outs.shape[1]

    def fetch(j, part):
        rows = pl.ds(size, pieces * tokens) if part == 0 else pl.ds(places[j], tokens)
        here = pl.ds(0, pieces * tokens) if part == 0 else pl.ds(pieces * tokens, tokens)
        return pltpu.make_async_copy(
            blocks[j].at[rows], held.at[j + 1, here], sem.at[j, part]
        )

    for j in range(len(places)):
        for part in range(2):
            fetch(j, part).start()
    for part, begin, piece, to, run in column_pieces([p.shape[1] for p in parts], width):
        units = parts[part][:, begin : begin + run]
        held[0, pl.ds(piece * tokens, tokens), pl.ds(to, run)] = jnp.where(
            roles.lost, jnp.zeros_like(units), units
        )
    slab = pl.ds(pl.multiple_of(features + roles.me * width, 128), width)
    held[0, pl.ds(pieces * tokens, tokens)] = both[:, slab]
    for j in range(len(places)):
        for part in range(2):
            fetch(j, part).wait()

    count = len(places) + 1
    for j in range(count):
        outs[pl.ds(j * tokens, tokens)] = held[j, pl.ds(pieces * tokens, tokens)]
    for piece in range(pieces):
        run = min(width, hidden_t.shape[0] - piece * width)
        rows = pl.ds(piece * tokens, tokens)
        hidden = jnp.concatenate([held[j, rows, :run] for j in range(count)], axis=0)
        hidden_t[pl.ds(piece * width, run)] = hidden.astype(F32).T.astype(BF16)


def collect(failed, n, both, parts, blocks, places, size, width, after):
    tokens = both.shape[0]
    units = sum(part.shape[1] for part in parts)
    pieces = -(-units // width)
    depth = tokens * (len(blocks) + 1)
    return pl.pallas_call(
        functools.partial(
            collect_body,
            n=n,
            places=places,
            parts_count=len(parts),
            size=size,
            pieces=pieces,
        ),
        in_specs=[SMEM]
        + [WHOLE] * (1 + len(parts))
        + [ANY] * (len(blocks) + len(after)),
        out_specs=[WHOLE, WHOLE],
        out_shape=[
            jax.ShapeDtypeStruct((units, depth), BF16),
            jax.ShapeDtypeStruct((depth, width), BF16),
        ],
        scratch_shapes=[
            pltpu.VMEM((len(blocks) + 1, (pieces + 1) * tokens, width), BF16),
            pltpu.SemaphoreType.DMA((len(blocks), 2)),
        ],
        compiler_params=PARAMS,
        cost_estimate=cost(0, 4 * depth * (units + width)),
        name="collect",
    )(failed, both, *parts, *blocks, *after)


def update_body(failed, hid_ref, out_ref, *refs, n, block, first, count, unread):
    state, news = refs[:3], refs[3 + unread : 6 + unread]
    total = refs[6 + unread]
    width = out_ref.shape[1]
    group = row_group(block)

    def step(hid, m_ref, a_ref, b_ref, m_new, a_new, b_new):
        total[...] = jnp.dot(hid[...], out_ref[...], preferred_element_type=F32)

        @pl.loop(0, block // group)
        def _(i):
            here = pl.ds(pl.multiple_of(i * group, group), group)
            m_new[here], a_new[here], b_new[here] = updated(
                m_ref[0, here], a_ref[0, here], b_ref[0, here], total[here], n - 1.0
            )

    deep = pl.Buffered(min(BUFFERS, count + 1))
    old = pl.BlockSpec(
        (1, block, width), lambda i: (0, first + i, 0), pipeline_mode=deep
    )
    new = pl.BlockSpec((block, width), lambda i: (first + i, 0))

    @pl.when(jnp.logical_not(Roles(failed, n).lost))
    def _():
        pltpu.emit_pipeline(
            step,
            grid=(count,),
            in_specs=[
                pl.BlockSpec((block, hid_ref.shape[1]), lambda i: (first + i, 0)),
                old,
                old,
                old,
            ],
            out_specs=[new] * 3,
        )(hid_ref, *state, *news)


def update(failed, n, hidden_t, outs, state, news, after, block, first, count):
    _, rows, width = state[0].shape
    depth = hidden_t.shape[1]
    shape = jax.ShapeDtypeStruct((rows, width), F32)
    unread = len(news) + len(after)
    return pl.pallas_call(
        functools.partial(
            update_body,
            n=n,
            block=block,
            first=first,
            count=count,
            unread=unread,
        ),
        in_specs=[SMEM, ANY, WHOLE] + [ANY] * (3 + unread),
        out_specs=[ANY] * 3,
        out_shape=[shape] * 3,
        scratch_shapes=[pltpu.VMEM((block, width), F32)],
        input_output_aliases={6 + k: k for k in range(len(news))},
        compiler_params=PARAMS,
        cost_estimate=cost(
            2 * count * block * width * depth,
            6 * count * block * width * 4,
            2 * count * block * width,
        ),
        name="update",
    )(failed, hidden_t, outs, *state, *news, *after)


def patch_body(failed, hid_ref, out_ref, *refs, arrivals, chunks, n, count_after):
    count = len(arrivals)
    got = refs[:count]
    rest = refs[count + 3 + count_after :]
    news = rest[:3]
    held, made, total, in_sem, out_sem = rest[3:]
    chunk = made.shape[2]
    group = row_group(chunk)
    roles = Roles(failed, n)
    ahead = roles.ahead()
    lag_of = {True: LAG * (ahead - 1), False: LAG * (n - ahead - 1)}

    def fetch(j):
        rows = got[j].at[pl.ds(0, 3 * chunk)]
        return pltpu.make_async_copy(rows, held.at[j % FETCHED], in_sem.at[j % FETCHED])

    def first_row(j):
        step, forward = arrivals[j]
        place = step - lag_of[forward]
        if not forward:
            place = chunks - 1 - place
        return pl.multiple_of(jnp.clip(place, 0, chunks - 1) * chunk, TILE)

    def store(j, k):
        return pltpu.make_async_copy(
            made.at[j % BUFFERS, k],
            news[k].at[pl.ds(first_row(j), chunk)],
            out_sem.at[j % BUFFERS, k],
        )

    def valid(j):
        step, forward = arrivals[j]
        return step >= lag_of[forward]

    def finish(j):
        @pl.when(valid(j))
        def _():
            for k in range(3):
                store(j, k).wait()

    @pl.when(roles.lost)
    def _():
        for j in range(min(FETCHED - 1, count)):
            fetch(j).start()
        for j in range(count):
            if j + FETCHED - 1 < count:
                fetch(j + FETCHED - 1).start()
            fetch(j).wait()
            if j >= BUFFERS:
                finish(j - BUFFERS)

            @pl.when(valid(j))
            def _(j=j, slot=j % FETCHED, out_slot=j % BUFFERS):
                first = first_row(j)

                units = hid_ref[pl.ds(first, chunk)]
                total[...] = jnp.dot(units, out_ref[...], preferred_element_type=F32)

                @pl.loop(0, chunk // group)
                def _(i):
                    base = pl.multiple_of(i * group, group)
                    old = [
                        held[slot, pl.ds(k * chunk + base, group)].astype(F32)
                        for k in range(3)
                    ]
                    new = updated(*old, total[pl.ds(base, group)], n - 1.0)
                    for k in range(3):
                        made[out_slot, k, pl.ds(base, group)] = new[k]

                for k in range(3):
                    store(j, k).start()

        for j in range(max(count - BUFFERS, 0), count):
            finish(j)


def patch(failed, n, hidden_t, outs, got, arrivals, news, after, chunks):
    rows, width = news[0].shape
    chunk = rows // chunks
    count = len(got)
    shape = jax.ShapeDtypeStruct((rows, width), F32)
    return pl.pallas_call(
        functools.partial(
            patch_body, arrivals=arrivals, chunks=chunks, n=n, count_after=len(after)
        ),
        in_specs=[SMEM, WHOLE, WHOLE] + [ANY] * (count + 3 + len(after)),
        out_specs=[ANY] * 3,
        out_shape=[shape] * 3,
        scratch_shapes=[
            pltpu.VMEM((FETCHED, 3 * chunk, width), BF16),
            pltpu.VMEM((BUFFERS, 3, chunk, width), F32),
            pltpu.VMEM((chunk, width), F32),
            pltpu.SemaphoreType.DMA((FETCHED,)),
            pltpu.SemaphoreType.DMA((BUFFERS, 3)),
        ],
        input_output_aliases={3 + count + k: k for k in range(3)},
        compiler_params=PARAMS,
        cost_estimate=cost(
            2 * count * chunk * width * hidden_t.shape[1],
            count * 3 * chunk * width * 6,
            2 * count * chunk * width,
        ),
        name="patch",
    )(failed, hidden_t, outs, *got, *news, *after)


def per_device(tokens, d_out, w_gate, w_up, w_down, failed, master, moment1, moment2):
    n = lax.axis_size("replica")
    _, rows, width = master.shape
    features, units = w_gate.shape

    order = ring_order(n)

    state = (master, moment1, moment2)
    chunks = largest(
        (c for c in range(2, MOST_CHUNKS + 1, 2) if rows % (TILE * c) == 0), 2
    )
    chunk = rows // chunks
    steps = (chunks + LAG * (n - 2)) // 2
    reach = (n // 2, (n - 1) // 2)
    forward = [(order[p], order[(p + 1) % n]) for p in range(n)]
    backward = [(b, a) for a, b in forward]
    got = []
    parcel_from = d_rows = None
    tile = 128 if units % 128 == 0 else units
    hidden = []

    def send(*after, share=None):
        nonlocal d_rows, parcel_from
        step = len(got)
        seen = got[step - LAG] if step >= LAG else ()
        here = min(step, chunks - 1)
        slabs, passed, extra = (0, 0), (0, 0), (0, 0)
        if share is not None and sum(share) == units // tile:
            parcel_from, slabs = step, reach
            pieces = -(-units // width)
            extra = [both.shape[0] * (pieces + count) if count else 0 for count in slabs]
        elif parcel_from is not None and (step - parcel_from) % LAG == 0:
            hop = (step - parcel_from) // LAG
            passed = extra = tuple(
                seen[way].shape[0] - 3 * chunk - both.shape[0] if hop < reach[way] else 0
                for way in range(2)
            )
        plan = ((here, chunks - 1 - here), chunk, slabs, passed)
        if share is None:
            packed = pack(failed, n, state, seen, after, extra, plan)
        else:
            parts = hidden if any(slabs) else []
            part, d_rows, *packed = layer(
                failed,
                n,
                both,
                (w_gate, w_up, w_down),
                d_rows,
                parts,
                state,
                seen,
                after,
                extra,
                plan,
                share,
                tile,
            )
            hidden.append(part)
        got.append(
            (
                lax.ppermute(packed[0], "replica", forward),
                lax.ppermute(packed[1], "replica", backward),
            )
        )
        return (packed[0],)

    sent = send()
    both = beside(tokens[0], d_out[0], sent)
    sent = send(both)
    exchanges = []
    for axis in ("tensor", "fsdp"):
        size = lax.axis_size(axis)
        exchanges += [(axis, size, 1 << k) for k in range((size - 1).bit_length())]
    if all(size & (size - 1) == 0 for _, size, _ in exchanges):
        after = sent
        for level, (axis, size, apart) in enumerate(exchanges):
            other = lax.ppermute(both, axis, [(i, i ^ apart) for i in range(size)])
            last = level == len(exchanges) - 1
            both = join(both, other, after, axis, apart, last)
            after = ()
    else:
        both = lax.all_gather(both[0], ("fsdp", "tensor"), axis=0, tiled=True)
    sent = send(both)

    for share in shares(units // tile, PIECES):
        sent = send(*sent, share=share)
    cotangents = ScatteredSum(d_rows, ("fsdp", "tensor"))

    news = ()
    patched = 0
    hidden_t = outs = None

    def gathered(after):
        blocks, places = [], []
        for way in range(2):
            for hop in range(reach[way]):
                blocks.append(got[parcel_from + LAG * hop][way])
                places.append(blocks[-1].shape[0] - both.shape[0])
        return collect(
            failed, n, both, hidden, blocks, places, 3 * chunk, width, after
        )

    def update_part(first, count, after):
        return update(
            failed, n, hidden_t, outs, state, news, after, block, first, count
        )

    def patch_to(step, after):
        nonlocal patched
        arrivals = [(s, way) for s in range(patched, step) for way in (True, False)]
        if not arrivals:
            return news
        blocks = [b for s in range(patched, step) for b in got[s]]
        patched = step
        return patch(failed, n, hidden_t, outs, blocks, arrivals, news, after, chunks)

    block = largest((b for b in range(TILE, 193, TILE) if rows % b == 0), rows)
    blocks = rows // block
    early = blocks // 4
    ready = parcel_from + LAG * reach[0] + 1
    while len(got) < steps:
        ready_sum = len(got) > parcel_from + SUM_AFTER
        sent = send(*(cotangents.advance(sent) if ready_sum else ()), *news[:1])
        if len(got) == ready and early and len(got) < steps:
            hidden_t, outs = gathered(sent)
            news = update_part(0, early, (hidden_t,))
            news = patch_to(len(got) // 2, ())
    if hidden_t is None:
        hidden_t, outs = gathered(sent)
        early = 0
    news = update_part(early, blocks - early, sent)
    for step in (steps - 2, steps - 1, steps):
        news = patch_to(step, ())
    while not cotangents.done:
        cotangents.advance(sent)
    return (cotangents.value[None], *news)


def solution(mesh):
    placed = (
        P("replica", ("fsdp", "tensor"), None),
        P("replica", ("fsdp", "tensor"), None),
        P(None, ("fsdp", "tensor")),
        P(None, ("fsdp", "tensor")),
        P(("fsdp", "tensor"), None),
        P(("fsdp", "tensor")),
        P(None, ("fsdp", "tensor"), "replica"),
        P(None, ("fsdp", "tensor"), "replica"),
        P(None, ("fsdp", "tensor"), "replica"),
    )
    return jax.shard_map(
        per_device,
        mesh=mesh,
        in_specs=placed,
        out_specs=(
            P("replica", ("fsdp", "tensor"), None),
            P(("fsdp", "tensor"), "replica"),
            P(("fsdp", "tensor"), "replica"),
            P(("fsdp", "tensor"), "replica"),
        ),
        check_vma=False,
    )
```

```python
import functools

import jax
import jax.numpy as jnp
from jax import lax
from jax.experimental import pallas as pl
from jax.experimental.pallas import tpu as pltpu
from jax.sharding import PartitionSpec as P

BF16, F32 = jnp.bfloat16, jnp.float32
SUM_AFTER = 1
LAG = 2
MOST_CHUNKS = 24
TILE = 16
BUFFERS = 3
PIECES = 6
FETCHED = 4
VMEM = 50 << 20

ANY = pl.BlockSpec(memory_space=pl.ANY)
SMEM = pl.BlockSpec(memory_space=pltpu.SMEM)
WHOLE = pl.BlockSpec(memory_space=pltpu.VMEM)
PARAMS = pltpu.CompilerParams(vmem_limit_bytes=VMEM)


def ring_order(n):
    return [0, 1, 3, 2] if n == 4 else list(range(n))


def entry(table, index):
    found = jnp.int32(0)
    for at, value in enumerate(table):
        found = jnp.where(index == at, jnp.int32(value), found)
    return found


class Roles:
    def __init__(self, failed, n):
        self.n = n
        self.order = ring_order(n)
        self.spots = [self.order.index(i) for i in range(n)]
        self.me = lax.axis_index("replica").astype(jnp.int32)
        self.failed = failed[0]
        self.source = lax.rem(self.failed + 1, n)
        self.lost = self.me == self.failed

    def ahead(self):
        apart = entry(self.spots, self.failed) - entry(self.spots, self.source)
        return lax.rem(apart + self.n, self.n)

    def neighbour(self, hops):
        spot = lax.rem(entry(self.spots, self.me) + hops, self.n)
        return entry(self.order, spot)


def largest(options, default):
    options = list(options)
    return max(options) if options else default


def shares(total, parts):
    parts = min(parts, total)
    edges = [total * i // parts for i in range(parts + 1)]
    return [(a, b - a) for a, b in zip(edges, edges[1:])]


def row_group(rows):
    return largest((g for g in (16, 32) if rows % g == 0), rows)


def cost(flops, bytes_accessed, transcendentals=0):
    return pl.CostEstimate(
        flops=flops, bytes_accessed=bytes_accessed, transcendentals=transcendentals
    )


def updated(master_old, first_old, second_old, total, healthy):
    first_new = 0.9 * first_old + (0.1 / healthy) * total
    second_new = 0.95 * second_old + (0.05 / healthy**2) * (total * total)
    root = second_new * lax.rsqrt(second_new)
    step = first_new * pl.reciprocal(root + 1e-08)
    return master_old - 0.01 * step, first_new, second_new


def column_pieces(lengths, width):
    moves, column = [], 0
    for part, length in enumerate(lengths):
        begin = 0
        while begin < length:
            piece, to = divmod(column, width)
            run = min(length - begin, width - to)
            moves.append((part, begin, piece, to, run))
            begin, column = begin + run, column + run
    return moves


def pack_body(*refs, n, places, chunk, slabs, passed, counts):
    count_seen, count_parts, count_after = counts
    if count_seen:
        roles, refs = Roles(refs[0], n), refs[1:]
    state = refs[0:3]
    seen = refs[3 : 3 + count_seen]
    rest = refs[3 + count_seen :]
    if count_parts:
        both, parts, rest = rest[0], rest[1 : 1 + count_parts], rest[1 + count_parts :]
    sends = rest[count_after : count_after + 2]
    held, made, sem, out_sem, below_sem = rest[count_after + 2 :]
    width = held.shape[2]
    size = 3 * chunk

    def rows_of(j):
        way, k = divmod(j, 3)
        return way, pl.ds(k * chunk, chunk)

    def fetch(j):
        way, k = divmod(j, 3)
        rows = pl.ds(places[way] * chunk, chunk)
        return pltpu.make_async_copy(state[k].at[1, rows], held.at[j], sem.at[j])

    def take(j):
        way, rows = rows_of(j)
        return pltpu.make_async_copy(seen[way].at[rows], made.at[way, rows], sem.at[j])

    def store(j):
        way, rows = rows_of(j)
        return pltpu.make_async_copy(
            made.at[way, rows], sends[way].at[rows], out_sem.at[j]
        )

    def convert():
        for j in range(6):
            fetch(j).start()
        for j in range(6):
            way, rows = rows_of(j)
            fetch(j).wait()
            made[way, rows] = held[j].astype(BF16)
            store(j).start()
        for j in range(6):
            store(j).wait()

    def relay():
        for j in range(6):
            take(j).start()
        for j in range(6):
            take(j).wait()
            store(j).start()
        for j in range(6):
            store(j).wait()

    def below(way, inward):
        rows = pl.ds(size, passed[way] or sends[way].shape[0] - size)
        here = made.at[way, rows]
        if inward:
            return pltpu.make_async_copy(seen[way].at[rows], here, below_sem.at[way])
        return pltpu.make_async_copy(here, sends[way].at[rows], below_sem.at[way])

    for way in range(2):
        if passed[way]:
            below(way, True).start()
        if slabs[way]:
            tokens, features = both.shape[0], both.shape[1] // 2
            moves = column_pieces([part.shape[1] for part in parts], width)
            for part, begin, piece, to, run in moves:
                units = parts[part][:, begin : begin + run]
                made[way, pl.ds(size + piece * tokens, tokens), pl.ds(to, run)] = (
                    jnp.where(roles.lost, jnp.zeros_like(units), units)
                )
            row = size + (1 + moves[-1][2]) * tokens
            for far in range(slabs[way], 0, -1):
                target = roles.neighbour(far if way == 0 else n - far)
                slab = pl.ds(pl.multiple_of(features + target * width, 128), width)
                made[way, pl.ds(row, tokens)] = both[:, slab]
                row += tokens
            below(way, False).start()

    for way in range(2):
        if passed[way]:
            below(way, True).wait()
            below(way, False).start()

    if seen:
        pl.when(roles.me == roles.source)(convert)
        pl.when(roles.me != roles.source)(relay)
    else:
        convert()

    for way in range(2):
        if slabs[way] or passed[way]:
            below(way, False).wait()


def pack(failed, n, state, seen, parcel, after, places, chunk, slabs, passed):
    width = state[0].shape[2]
    extra = list(passed)
    if parcel:
        tokens = parcel[0].shape[0]
        pieces = -(-sum(part.shape[1] for part in parcel[1:]) // width)
        extra = [tokens * (pieces + count) if count else 0 for count in slabs]
    counts = (len(seen), max(len(parcel) - 1, 0), len(after))
    return pl.pallas_call(
        functools.partial(
            pack_body,
            n=n,
            places=places,
            chunk=chunk,
            slabs=slabs,
            passed=passed,
            counts=counts,
        ),
        in_specs=[SMEM] * bool(seen)
        + [ANY] * (3 + len(seen))
        + [WHOLE] * len(parcel)
        + [ANY] * len(after),
        out_specs=[ANY, ANY],
        out_shape=[
            jax.ShapeDtypeStruct((3 * chunk + more, width), BF16) for more in extra
        ],
        scratch_shapes=[
            pltpu.VMEM((6, chunk, width), F32),
            pltpu.VMEM((2, 3 * chunk + max(extra), width), BF16),
            pltpu.SemaphoreType.DMA((6,)),
            pltpu.SemaphoreType.DMA((6,)),
            pltpu.SemaphoreType.DMA((2,)),
        ],
        compiler_params=PARAMS,
        cost_estimate=cost(0, 2 * 3 * chunk * width * 6),
        name="pack",
    )(*([failed] if seen else []), *state, *seen, *parcel, *after)


def beside_body(*refs):
    tokens, d_out, out = refs[0], refs[1], refs[-1]
    width = tokens.shape[1]
    out[0, :, :width] = tokens[...]
    out[0, :, width:] = d_out[...]


def beside(tokens, d_out, after):
    rows, width = tokens.shape
    return pl.pallas_call(
        beside_body,
        in_specs=[WHOLE, WHOLE] + [ANY] * len(after),
        out_specs=WHOLE,
        out_shape=jax.ShapeDtypeStruct((1, rows, 2 * width), tokens.dtype),
        compiler_params=PARAMS,
        cost_estimate=cost(0, 4 * rows * width * 2),
        name="beside",
    )(tokens, d_out, *after)


def join_body(own, other, *refs, axis, apart, last):
    out = refs[-1]
    count, rows = own.shape[:2]
    second = lax.rem(lax.div(lax.axis_index(axis).astype(jnp.int32), apart), 2)
    if not last:
        out[pl.ds(second * count, count)] = own[...]
        out[pl.ds((1 - second) * count, count)] = other[...]
        return
    for i in range(2 * count):
        here, there = (own, other) if i < count else (other, own)
        value = jnp.where(second == 1, there[i % count], here[i % count])
        out[pl.ds(i * rows, rows)] = value


def join(own, other, after, axis, apart, last):
    count, rows, width = own.shape
    shape = (2 * count * rows, width) if last else (2 * count, rows, width)
    return pl.pallas_call(
        functools.partial(join_body, axis=axis, apart=apart, last=last),
        in_specs=[WHOLE, WHOLE] + [ANY] * len(after),
        out_specs=WHOLE,
        out_shape=jax.ShapeDtypeStruct(shape, own.dtype),
        compiler_params=PARAMS,
        cost_estimate=cost(0, 8 * count * rows * width),
        name="join",
    )(own, other, *after)


def by_rows(a, b):
    return lax.dot_general(a, b, (((1,), (1,)), ((), ())), preferred_element_type=F32)


def layer_body(both, *refs, resumed, tile, first, count):
    weights = refs[:3]
    hidden_ref, sum_ref = refs[-2:]
    features = weights[0].shape[0]
    rows = both.shape[0]
    joined = tile % 128 == 0
    sum_ref[...] = refs[3][...] if resumed else jnp.zeros_like(sum_ref)

    def step(gate_ref, up_ref, down_ref, hidden):
        x, dy = both[:, :features], both[:, features:]
        w_gate, w_up = gate_ref[...], up_ref[...]
        if joined:
            w_both = jnp.concatenate([w_gate, w_up], axis=1)
            gate_up = jnp.dot(x, w_both, preferred_element_type=F32)
            gate, up = gate_up[:, :tile], gate_up[:, tile:]
        else:
            gate = jnp.dot(x, w_gate, preferred_element_type=F32)
            up = jnp.dot(x, w_up, preferred_element_type=F32)
        d_hidden = by_rows(dy, down_ref[...])
        sig = 1.0 / (1.0 + jnp.exp(-gate))
        hidden[...] = (gate * sig * up).astype(BF16)
        d_gate = (d_hidden * up * sig * (1.0 + gate * (1.0 - sig))).astype(BF16)
        d_up = (d_hidden * gate * sig).astype(BF16)
        if joined:
            sum_ref[...] += by_rows(jnp.concatenate([d_gate, d_up], axis=1), w_both)
        else:
            sum_ref[...] += by_rows(d_gate, w_gate) + by_rows(d_up, w_up)

    deep = pl.Buffered(min(BUFFERS, count + 1))
    across = pl.BlockSpec((features, tile), lambda i: (0, first + i), pipeline_mode=deep)
    pltpu.emit_pipeline(
        step,
        grid=(count,),
        in_specs=[
            across,
            across,
            pl.BlockSpec((tile, features), lambda i: (first + i, 0), pipeline_mode=deep),
        ],
        out_specs=[pl.BlockSpec((rows, tile), lambda i: (0, i))],
    )(*weights, hidden_ref)


def layer(both, w_gate, w_up, w_down, partial_sum, after, tile, first, count):
    rows = both.shape[0]
    features = w_gate.shape[0]
    resumed = partial_sum is not None
    return pl.pallas_call(
        functools.partial(layer_body, resumed=resumed, tile=tile, first=first, count=count),
        in_specs=[WHOLE] + [ANY] * 3 + [WHOLE] * resumed + [ANY] * len(after),
        out_specs=[ANY, WHOLE],
        out_shape=[
            jax.ShapeDtypeStruct((rows, count * tile), BF16),
            jax.ShapeDtypeStruct((rows, features), F32),
        ],
        compiler_params=PARAMS,
        cost_estimate=cost(
            10 * rows * features * count * tile,
            3 * features * count * tile * 2,
            rows * count * tile,
        ),
        name="layer",
    )(both, w_gate, w_up, w_down, *([partial_sum] if resumed else []), *after)


def halve_body(bit, *refs, arrived, final):
    value = refs[0][...]
    if arrived:
        value = value + refs[1][...]
    if final:
        refs[-1][...] = value.astype(BF16)
        return
    kept, sent = refs[-2:]
    half = value.shape[0] // 2
    low, high = value[:half], value[half:]
    upper = bit[0] == 1
    kept[...] = jnp.where(upper, high, low)
    sent[...] = jnp.where(upper, low, high)


def halve(bit, value, arrived, after, final):
    rows, features = value.shape
    if final:
        out_shape = jax.ShapeDtypeStruct((rows, features), BF16)
    else:
        out_shape = [jax.ShapeDtypeStruct((rows // 2, features), F32)] * 2
    return pl.pallas_call(
        functools.partial(halve_body, arrived=bool(arrived), final=final),
        in_specs=[SMEM] + [WHOLE] * (1 + len(arrived)) + [ANY] * len(after),
        out_specs=WHOLE if final else [WHOLE, WHOLE],
        out_shape=out_shape,
        compiler_params=PARAMS,
        cost_estimate=cost(0, 3 * rows * features * 4),
        name="halve",
    )(bit, value, *arrived, *after)


class ScatteredSum:
    def __init__(self, value, axes):
        sizes = [lax.axis_size(axis) for axis in axes]
        self.value, self.arrived, self.levels = value, (), []
        self.done = any(size & (size - 1) for size in sizes)
        if self.done:
            summed = lax.psum_scatter(value, axes, scatter_dimension=0, tiled=True)
            self.value = summed.astype(BF16)
            return
        for axis, size in zip(axes, sizes):
            apart = size // 2
            while apart:
                self.levels.append((axis, size, apart))
                apart //= 2

    def advance(self, after):
        if self.done:
            return ()
        if self.levels:
            axis, size, apart = self.levels.pop(0)
            bit = ((lax.axis_index(axis) // apart) % 2).astype(jnp.int32)[None]
            self.value, sent = halve(bit, self.value, self.arrived, after, False)
            route = [(i, i ^ apart) for i in range(size)]
            self.arrived = (lax.ppermute(sent, axis, route),)
        else:
            bit = jnp.zeros((1,), jnp.int32)
            self.value = halve(bit, self.value, self.arrived, after, True)
            self.done = True
        return (self.value,)


def collect_body(failed, both, *refs, n, places, parts_count, size, pieces):
    roles = Roles(failed, n)
    parts = refs[:parts_count]
    blocks = refs[parts_count : parts_count + len(places)]
    hidden_t, outs, held, sem = refs[-4:]
    tokens, features = both.shape[0], both.shape[1] // 2
    width = outs.shape[1]

    def fetch(j, part):
        rows = pl.ds(size, pieces * tokens) if part == 0 else pl.ds(places[j], tokens)
        here = pl.ds(0, pieces * tokens) if part == 0 else pl.ds(pieces * tokens, tokens)
        return pltpu.make_async_copy(
            blocks[j].at[rows], held.at[j + 1, here], sem.at[j, part]
        )

    for j in range(len(places)):
        for part in range(2):
            fetch(j, part).start()
    for part, begin, piece, to, run in column_pieces([p.shape[1] for p in parts], width):
        units = parts[part][:, begin : begin + run]
        held[0, pl.ds(piece * tokens, tokens), pl.ds(to, run)] = jnp.where(
            roles.lost, jnp.zeros_like(units), units
        )
    slab = pl.ds(pl.multiple_of(features + roles.me * width, 128), width)
    held[0, pl.ds(pieces * tokens, tokens)] = both[:, slab]
    for j in range(len(places)):
        for part in range(2):
            fetch(j, part).wait()

    count = len(places) + 1
    for j in range(count):
        outs[pl.ds(j * tokens, tokens)] = held[j, pl.ds(pieces * tokens, tokens)]
    for piece in range(pieces):
        run = min(width, hidden_t.shape[0] - piece * width)
        rows = pl.ds(piece * tokens, tokens)
        hidden = jnp.concatenate([held[j, rows, :run] for j in range(count)], axis=0)
        hidden_t[pl.ds(piece * width, run)] = hidden.astype(F32).T.astype(BF16)


def collect(failed, n, both, parts, blocks, places, size, width, after):
    tokens = both.shape[0]
    units = sum(part.shape[1] for part in parts)
    pieces = -(-units // width)
    depth = tokens * (len(blocks) + 1)
    return pl.pallas_call(
        functools.partial(
            collect_body,
            n=n,
            places=places,
            parts_count=len(parts),
            size=size,
            pieces=pieces,
        ),
        in_specs=[SMEM]
        + [WHOLE] * (1 + len(parts))
        + [ANY] * (len(blocks) + len(after)),
        out_specs=[WHOLE, WHOLE],
        out_shape=[
            jax.ShapeDtypeStruct((units, depth), BF16),
            jax.ShapeDtypeStruct((depth, width), BF16),
        ],
        scratch_shapes=[
            pltpu.VMEM((len(blocks) + 1, (pieces + 1) * tokens, width), BF16),
            pltpu.SemaphoreType.DMA((len(blocks), 2)),
        ],
        compiler_params=PARAMS,
        cost_estimate=cost(0, 4 * depth * (units + width)),
        name="collect",
    )(failed, both, *parts, *blocks, *after)


def update_body(failed, hid_ref, out_ref, *refs, n, block, first, count, unread):
    state, news = refs[:3], refs[3 + unread : 6 + unread]
    total = refs[6 + unread]
    width = out_ref.shape[1]
    group = row_group(block)

    def step(hid, m_ref, a_ref, b_ref, m_new, a_new, b_new):
        total[...] = jnp.dot(hid[...], out_ref[...], preferred_element_type=F32)

        @pl.loop(0, block // group)
        def _(i):
            here = pl.ds(pl.multiple_of(i * group, group), group)
            m_new[here], a_new[here], b_new[here] = updated(
                m_ref[0, here], a_ref[0, here], b_ref[0, here], total[here], n - 1.0
            )

    deep = pl.Buffered(min(BUFFERS, count + 1))
    old = pl.BlockSpec(
        (1, block, width), lambda i: (0, first + i, 0), pipeline_mode=deep
    )
    new = pl.BlockSpec((block, width), lambda i: (first + i, 0))

    @pl.when(jnp.logical_not(Roles(failed, n).lost))
    def _():
        pltpu.emit_pipeline(
            step,
            grid=(count,),
            in_specs=[
                pl.BlockSpec((block, hid_ref.shape[1]), lambda i: (first + i, 0)),
                old,
                old,
                old,
            ],
            out_specs=[new] * 3,
        )(hid_ref, *state, *news)


def update(failed, n, hidden_t, outs, state, news, after, block, first, count):
    _, rows, width = state[0].shape
    depth = hidden_t.shape[1]
    shape = jax.ShapeDtypeStruct((rows, width), F32)
    unread = len(news) + len(after)
    return pl.pallas_call(
        functools.partial(
            update_body,
            n=n,
            block=block,
            first=first,
            count=count,
            unread=unread,
        ),
        in_specs=[SMEM, ANY, WHOLE] + [ANY] * (3 + unread),
        out_specs=[ANY] * 3,
        out_shape=[shape] * 3,
        scratch_shapes=[pltpu.VMEM((block, width), F32)],
        input_output_aliases={6 + k: k for k in range(len(news))},
        compiler_params=PARAMS,
        cost_estimate=cost(
            2 * count * block * width * depth,
            6 * count * block * width * 4,
            2 * count * block * width,
        ),
        name="update",
    )(failed, hidden_t, outs, *state, *news, *after)


def patch_body(failed, hid_ref, out_ref, *refs, arrivals, chunks, n, count_after):
    count = len(arrivals)
    got = refs[:count]
    rest = refs[count + 3 + count_after :]
    news = rest[:3]
    held, made, total, in_sem, out_sem = rest[3:]
    chunk = made.shape[2]
    group = row_group(chunk)
    roles = Roles(failed, n)
    ahead = roles.ahead()
    lag_of = {True: LAG * (ahead - 1), False: LAG * (n - ahead - 1)}

    def fetch(j):
        rows = got[j].at[pl.ds(0, 3 * chunk)]
        return pltpu.make_async_copy(rows, held.at[j % FETCHED], in_sem.at[j % FETCHED])

    def first_row(j):
        step, forward = arrivals[j]
        place = step - lag_of[forward]
        if not forward:
            place = chunks - 1 - place
        return pl.multiple_of(jnp.clip(place, 0, chunks - 1) * chunk, TILE)

    def store(j, k):
        return pltpu.make_async_copy(
            made.at[j % BUFFERS, k],
            news[k].at[pl.ds(first_row(j), chunk)],
            out_sem.at[j % BUFFERS, k],
        )

    def valid(j):
        step, forward = arrivals[j]
        return step >= lag_of[forward]

    def finish(j):
        @pl.when(valid(j))
        def _():
            for k in range(3):
                store(j, k).wait()

    @pl.when(roles.lost)
    def _():
        for j in range(min(FETCHED - 1, count)):
            fetch(j).start()
        for j in range(count):
            if j + FETCHED - 1 < count:
                fetch(j + FETCHED - 1).start()
            fetch(j).wait()
            if j >= BUFFERS:
                finish(j - BUFFERS)

            @pl.when(valid(j))
            def _(j=j, slot=j % FETCHED, out_slot=j % BUFFERS):
                first = first_row(j)

                units = hid_ref[pl.ds(first, chunk)]
                total[...] = jnp.dot(units, out_ref[...], preferred_element_type=F32)

                @pl.loop(0, chunk // group)
                def _(i):
                    base = pl.multiple_of(i * group, group)
                    old = [
                        held[slot, pl.ds(k * chunk + base, group)].astype(F32)
                        for k in range(3)
                    ]
                    new = updated(*old, total[pl.ds(base, group)], n - 1.0)
                    for k in range(3):
                        made[out_slot, k, pl.ds(base, group)] = new[k]

                for k in range(3):
                    store(j, k).start()

        for j in range(max(count - BUFFERS, 0), count):
            finish(j)


def patch(failed, n, hidden_t, outs, got, arrivals, news, after, chunks):
    rows, width = news[0].shape
    chunk = rows // chunks
    count = len(got)
    shape = jax.ShapeDtypeStruct((rows, width), F32)
    return pl.pallas_call(
        functools.partial(
            patch_body, arrivals=arrivals, chunks=chunks, n=n, count_after=len(after)
        ),
        in_specs=[SMEM, WHOLE, WHOLE] + [ANY] * (count + 3 + len(after)),
        out_specs=[ANY] * 3,
        out_shape=[shape] * 3,
        scratch_shapes=[
            pltpu.VMEM((FETCHED, 3 * chunk, width), BF16),
            pltpu.VMEM((BUFFERS, 3, chunk, width), F32),
            pltpu.VMEM((chunk, width), F32),
            pltpu.SemaphoreType.DMA((FETCHED,)),
            pltpu.SemaphoreType.DMA((BUFFERS, 3)),
        ],
        input_output_aliases={3 + count + k: k for k in range(3)},
        compiler_params=PARAMS,
        cost_estimate=cost(
            2 * count * chunk * width * hidden_t.shape[1],
            count * 3 * chunk * width * 6,
            2 * count * chunk * width,
        ),
        name="patch",
    )(failed, hidden_t, outs, *got, *news, *after)


def per_device(tokens, d_out, w_gate, w_up, w_down, failed, master, moment1, moment2):
    n = lax.axis_size("replica")
    _, rows, width = master.shape
    features, units = w_gate.shape

    order = ring_order(n)

    state = (master, moment1, moment2)
    chunks = largest(
        (c for c in range(2, MOST_CHUNKS + 1, 2) if rows % (TILE * c) == 0), 2
    )
    chunk = rows // chunks
    steps = (chunks + LAG * (n - 2)) // 2
    reach = (n // 2, (n - 1) // 2)
    forward = [(order[p], order[(p + 1) % n]) for p in range(n)]
    backward = [(b, a) for a, b in forward]
    sends, got = [], []
    parcel_from = None

    def send(*after, parcel=()):
        nonlocal parcel_from
        step = len(got)
        seen = got[step - LAG] if step >= LAG else ()
        here = min(step, chunks - 1)
        slabs, passed = (0, 0), (0, 0)
        if parcel:
            parcel_from, slabs = step, reach
        elif parcel_from is not None and (step - parcel_from) % LAG == 0:
            hop = (step - parcel_from) // LAG
            passed = tuple(
                seen[way].shape[0] - 3 * chunk - both.shape[0]
                if hop < reach[way]
                else 0
                for way in range(2)
            )
        sends.append(
            pack(
                failed,
                n,
                state,
                seen,
                parcel,
                after,
                (here, chunks - 1 - here),
                chunk,
                slabs,
                passed,
            )
        )
        got.append(
            (
                lax.ppermute(sends[-1][0], "replica", forward),
                lax.ppermute(sends[-1][1], "replica", backward),
            )
        )
        return (sends[-1][0],)

    sent = send()
    both = beside(tokens[0], d_out[0], sent)
    sent = send(both)
    exchanges = []
    for axis in ("tensor", "fsdp"):
        size = lax.axis_size(axis)
        exchanges += [(axis, size, 1 << k) for k in range((size - 1).bit_length())]
    if all(size & (size - 1) == 0 for _, size, _ in exchanges):
        after = sent
        for level, (axis, size, apart) in enumerate(exchanges):
            other = lax.ppermute(both, axis, [(i, i ^ apart) for i in range(size)])
            last = level == len(exchanges) - 1
            both = join(both, other, after, axis, apart, last)
            after = ()
    else:
        both = lax.all_gather(both[0], ("fsdp", "tensor"), axis=0, tiled=True)
    sent = send(both)

    tile = 128 if units % 128 == 0 else units
    hidden, d_rows = [], None
    pieces = shares(units // tile, PIECES)
    for first, count in pieces:
        part, d_rows = layer(both, w_gate, w_up, w_down, d_rows, sent, tile, first, count)
        hidden.append(part)
        last = len(hidden) == len(pieces)
        sent = send(d_rows, parcel=(both, *hidden) if last else ())
    cotangents = ScatteredSum(d_rows, ("fsdp", "tensor"))

    news = ()
    patched = 0
    hidden_t = outs = None

    def gathered(after):
        blocks, places = [], []
        for way in range(2):
            for hop in range(reach[way]):
                blocks.append(got[parcel_from + LAG * hop][way])
                places.append(blocks[-1].shape[0] - both.shape[0])
        return collect(
            failed, n, both, hidden, blocks, places, 3 * chunk, width, after
        )

    def update_part(first, count, after):
        return update(
            failed, n, hidden_t, outs, state, news, after, block, first, count
        )

    def patch_to(step, after):
        nonlocal patched
        arrivals = [(s, way) for s in range(patched, step) for way in (True, False)]
        if not arrivals:
            return news
        blocks = [b for s in range(patched, step) for b in got[s]]
        patched = step
        return patch(failed, n, hidden_t, outs, blocks, arrivals, news, after, chunks)

    block = largest((b for b in range(TILE, 193, TILE) if rows % b == 0), rows)
    blocks = rows // block
    early = blocks // 4
    ready = parcel_from + LAG * reach[0] + 1
    while len(got) < steps:
        ready_sum = len(got) > parcel_from + SUM_AFTER
        sent = send(*(cotangents.advance(sent) if ready_sum else ()), *news[:1])
        if len(got) == ready and early and len(got) < steps:
            hidden_t, outs = gathered(sent)
            news = update_part(0, early, (hidden_t,))
            news = patch_to(len(got) // 2, ())
    if hidden_t is None:
        hidden_t, outs = gathered(sent)
        early = 0
    news = update_part(early, blocks - early, sent)
    for step in (steps - 2, steps - 1, steps):
        news = patch_to(step, ())
    while not cotangents.done:
        cotangents.advance(sent)
    return (cotangents.value[None], *news)


def solution(mesh):
    placed = (
        P("replica", ("fsdp", "tensor"), None),
        P("replica", ("fsdp", "tensor"), None),
        P(None, ("fsdp", "tensor")),
        P(None, ("fsdp", "tensor")),
        P(("fsdp", "tensor"), None),
        P(("fsdp", "tensor")),
        P(None, ("fsdp", "tensor"), "replica"),
        P(None, ("fsdp", "tensor"), "replica"),
        P(None, ("fsdp", "tensor"), "replica"),
    )
    return jax.shard_map(
        per_device,
        mesh=mesh,
        in_specs=placed,
        out_specs=(
            P("replica", ("fsdp", "tensor"), None),
            P(("fsdp", "tensor"), "replica"),
            P(("fsdp", "tensor"), "replica"),
            P(("fsdp", "tensor"), "replica"),
        ),
        check_vma=False,
    )
```

```python
import functools

import jax
import jax.numpy as jnp
from jax import lax
from jax.experimental import pallas as pl
from jax.experimental.pallas import tpu as pltpu
from jax.sharding import PartitionSpec as P

BF16, F32 = jnp.bfloat16, jnp.float32
SUM_AFTER = 1
LAG = 2
MOST_CHUNKS = 20
TILE = 16
BUFFERS = 3
PIECES = 4
FETCHED = 4
VMEM = 50 << 20

ANY = pl.BlockSpec(memory_space=pl.ANY)
SMEM = pl.BlockSpec(memory_space=pltpu.SMEM)
WHOLE = pl.BlockSpec(memory_space=pltpu.VMEM)
PARAMS = pltpu.CompilerParams(vmem_limit_bytes=VMEM)


def ring_order(n):
    return [0, 1, 3, 2] if n == 4 else list(range(n))


def entry(table, index):
    found = jnp.int32(0)
    for at, value in enumerate(table):
        found = jnp.where(index == at, jnp.int32(value), found)
    return found


class Roles:
    def __init__(self, failed, n):
        self.n = n
        self.order = ring_order(n)
        self.spots = [self.order.index(i) for i in range(n)]
        self.me = lax.axis_index("replica").astype(jnp.int32)
        self.failed = failed[0]
        self.source = lax.rem(self.failed + 1, n)
        self.lost = self.me == self.failed

    def ahead(self):
        apart = entry(self.spots, self.failed) - entry(self.spots, self.source)
        return lax.rem(apart + self.n, self.n)

    def neighbour(self, hops):
        spot = lax.rem(entry(self.spots, self.me) + hops, self.n)
        return entry(self.order, spot)


def largest(options, default):
    options = list(options)
    return max(options) if options else default


def shares(total, parts):
    parts = min(parts, total)
    edges = [total * i // parts for i in range(parts + 1)]
    return [(a, b - a) for a, b in zip(edges, edges[1:])]


def row_group(rows):
    return largest((g for g in (16, 32) if rows % g == 0), rows)


def cost(flops, bytes_accessed, transcendentals=0):
    return pl.CostEstimate(
        flops=flops, bytes_accessed=bytes_accessed, transcendentals=transcendentals
    )


def updated(master_old, first_old, second_old, total, healthy):
    first_new = 0.9 * first_old + (0.1 / healthy) * total
    second_new = 0.95 * second_old + (0.05 / healthy**2) * (total * total)
    root = second_new * lax.rsqrt(second_new)
    step = first_new * pl.reciprocal(root + 1e-08)
    return master_old - 0.01 * step, first_new, second_new


def column_pieces(lengths, width):
    moves, column = [], 0
    for part, length in enumerate(lengths):
        begin = 0
        while begin < length:
            piece, to = divmod(column, width)
            run = min(length - begin, width - to)
            moves.append((part, begin, piece, to, run))
            begin, column = begin + run, column + run
    return moves


def pack_body(*refs, n, places, chunk, slabs, passed, counts):
    count_seen, count_parts, count_after = counts
    if count_seen:
        roles, refs = Roles(refs[0], n), refs[1:]
    state = refs[0:3]
    seen = refs[3 : 3 + count_seen]
    rest = refs[3 + count_seen :]
    if count_parts:
        both, parts, rest = rest[0], rest[1 : 1 + count_parts], rest[1 + count_parts :]
    sends = rest[count_after : count_after + 2]
    held, made, sem, out_sem, below_sem = rest[count_after + 2 :]
    width = held.shape[2]
    size = 3 * chunk

    def rows_of(j):
        way, k = divmod(j, 3)
        return way, pl.ds(k * chunk, chunk)

    def fetch(j):
        way, k = divmod(j, 3)
        rows = pl.ds(places[way] * chunk, chunk)
        return pltpu.make_async_copy(state[k].at[1, rows], held.at[j], sem.at[j])

    def take(j):
        way, rows = rows_of(j)
        return pltpu.make_async_copy(seen[way].at[rows], made.at[way, rows], sem.at[j])

    def store(j):
        way, rows = rows_of(j)
        return pltpu.make_async_copy(
            made.at[way, rows], sends[way].at[rows], out_sem.at[j]
        )

    def convert():
        for j in range(6):
            fetch(j).start()
        for j in range(6):
            way, rows = rows_of(j)
            fetch(j).wait()
            made[way, rows] = held[j].astype(BF16)
            store(j).start()
        for j in range(6):
            store(j).wait()

    def relay():
        for j in range(6):
            take(j).start()
        for j in range(6):
            take(j).wait()
            store(j).start()
        for j in range(6):
            store(j).wait()

    def below(way, inward):
        rows = pl.ds(size, passed[way] or sends[way].shape[0] - size)
        here = made.at[way, rows]
        if inward:
            return pltpu.make_async_copy(seen[way].at[rows], here, below_sem.at[way])
        return pltpu.make_async_copy(here, sends[way].at[rows], below_sem.at[way])

    for way in range(2):
        if passed[way]:
            below(way, True).start()
        if slabs[way]:
            tokens, features = both.shape[0], both.shape[1] // 2
            moves = column_pieces([part.shape[1] for part in parts], width)
            for part, begin, piece, to, run in moves:
                units = parts[part][:, begin : begin + run]
                made[way, pl.ds(size + piece * tokens, tokens), pl.ds(to, run)] = (
                    jnp.where(roles.lost, jnp.zeros_like(units), units)
                )
            row = size + (1 + moves[-1][2]) * tokens
            for far in range(slabs[way], 0, -1):
                target = roles.neighbour(far if way == 0 else n - far)
                slab = pl.ds(pl.multiple_of(features + target * width, 128), width)
                made[way, pl.ds(row, tokens)] = both[:, slab]
                row += tokens
            below(way, False).start()

    for way in range(2):
        if passed[way]:
            below(way, True).wait()
            below(way, False).start()

    if seen:
        pl.when(roles.me == roles.source)(convert)
        pl.when(roles.me != roles.source)(relay)
    else:
        convert()

    for way in range(2):
        if slabs[way] or passed[way]:
            below(way, False).wait()


def pack(failed, n, state, seen, parcel, after, places, chunk, slabs, passed):
    width = state[0].shape[2]
    extra = list(passed)
    if parcel:
        tokens = parcel[0].shape[0]
        pieces = -(-sum(part.shape[1] for part in parcel[1:]) // width)
        extra = [tokens * (pieces + count) if count else 0 for count in slabs]
    counts = (len(seen), max(len(parcel) - 1, 0), len(after))
    return pl.pallas_call(
        functools.partial(
            pack_body,
            n=n,
            places=places,
            chunk=chunk,
            slabs=slabs,
            passed=passed,
            counts=counts,
        ),
        in_specs=[SMEM] * bool(seen)
        + [ANY] * (3 + len(seen))
        + [WHOLE] * len(parcel)
        + [ANY] * len(after),
        out_specs=[ANY, ANY],
        out_shape=[
            jax.ShapeDtypeStruct((3 * chunk + more, width), BF16) for more in extra
        ],
        scratch_shapes=[
            pltpu.VMEM((6, chunk, width), F32),
            pltpu.VMEM((2, 3 * chunk + max(extra), width), BF16),
            pltpu.SemaphoreType.DMA((6,)),
            pltpu.SemaphoreType.DMA((6,)),
            pltpu.SemaphoreType.DMA((2,)),
        ],
        compiler_params=PARAMS,
        cost_estimate=cost(0, 2 * 3 * chunk * width * 6),
        name="pack",
    )(*([failed] if seen else []), *state, *seen, *parcel, *after)


def beside_body(*refs):
    tokens, d_out, out = refs[0], refs[1], refs[-1]
    width = tokens.shape[1]
    out[0, :, :width] = tokens[...]
    out[0, :, width:] = d_out[...]


def beside(tokens, d_out, after):
    rows, width = tokens.shape
    return pl.pallas_call(
        beside_body,
        in_specs=[WHOLE, WHOLE] + [ANY] * len(after),
        out_specs=WHOLE,
        out_shape=jax.ShapeDtypeStruct((1, rows, 2 * width), tokens.dtype),
        compiler_params=PARAMS,
        cost_estimate=cost(0, 4 * rows * width * 2),
        name="beside",
    )(tokens, d_out, *after)


def join_body(own, other, *refs, axis, apart, last):
    out = refs[-1]
    count, rows = own.shape[:2]
    second = lax.rem(lax.div(lax.axis_index(axis).astype(jnp.int32), apart), 2)
    if not last:
        out[pl.ds(second * count, count)] = own[...]
        out[pl.ds((1 - second) * count, count)] = other[...]
        return
    for i in range(2 * count):
        here, there = (own, other) if i < count else (other, own)
        value = jnp.where(second == 1, there[i % count], here[i % count])
        out[pl.ds(i * rows, rows)] = value


def join(own, other, after, axis, apart, last):
    count, rows, width = own.shape
    shape = (2 * count * rows, width) if last else (2 * count, rows, width)
    return pl.pallas_call(
        functools.partial(join_body, axis=axis, apart=apart, last=last),
        in_specs=[WHOLE, WHOLE] + [ANY] * len(after),
        out_specs=WHOLE,
        out_shape=jax.ShapeDtypeStruct(shape, own.dtype),
        compiler_params=PARAMS,
        cost_estimate=cost(0, 8 * count * rows * width),
        name="join",
    )(own, other, *after)


def by_rows(a, b):
    return lax.dot_general(a, b, (((1,), (1,)), ((), ())), preferred_element_type=F32)


def layer_body(both, *refs, resumed, tile, first, count):
    weights = refs[:3]
    hidden_ref, sum_ref = refs[-2:]
    features = weights[0].shape[0]
    rows = both.shape[0]
    joined = tile % 128 == 0
    sum_ref[...] = refs[3][...] if resumed else jnp.zeros_like(sum_ref)

    def step(gate_ref, up_ref, down_ref, hidden):
        x, dy = both[:, :features], both[:, features:]
        w_gate, w_up = gate_ref[...], up_ref[...]
        if joined:
            w_both = jnp.concatenate([w_gate, w_up], axis=1)
            gate_up = jnp.dot(x, w_both, preferred_element_type=F32)
            gate, up = gate_up[:, :tile], gate_up[:, tile:]
        else:
            gate = jnp.dot(x, w_gate, preferred_element_type=F32)
            up = jnp.dot(x, w_up, preferred_element_type=F32)
        d_hidden = by_rows(dy, down_ref[...])
        sig = 1.0 / (1.0 + jnp.exp(-gate))
        hidden[...] = (gate * sig * up).astype(BF16)
        d_gate = (d_hidden * up * sig * (1.0 + gate * (1.0 - sig))).astype(BF16)
        d_up = (d_hidden * gate * sig).astype(BF16)
        if joined:
            sum_ref[...] += by_rows(jnp.concatenate([d_gate, d_up], axis=1), w_both)
        else:
            sum_ref[...] += by_rows(d_gate, w_gate) + by_rows(d_up, w_up)

    deep = pl.Buffered(min(BUFFERS, count + 1))
    across = pl.BlockSpec((features, tile), lambda i: (0, first + i), pipeline_mode=deep)
    pltpu.emit_pipeline(
        step,
        grid=(count,),
        in_specs=[
            across,
            across,
            pl.BlockSpec((tile, features), lambda i: (first + i, 0), pipeline_mode=deep),
        ],
        out_specs=[pl.BlockSpec((rows, tile), lambda i: (0, i))],
    )(*weights, hidden_ref)


def layer(both, w_gate, w_up, w_down, partial_sum, after, tile, first, count):
    rows = both.shape[0]
    features = w_gate.shape[0]
    resumed = partial_sum is not None
    return pl.pallas_call(
        functools.partial(layer_body, resumed=resumed, tile=tile, first=first, count=count),
        in_specs=[WHOLE] + [ANY] * 3 + [WHOLE] * resumed + [ANY] * len(after),
        out_specs=[ANY, WHOLE],
        out_shape=[
            jax.ShapeDtypeStruct((rows, count * tile), BF16),
            jax.ShapeDtypeStruct((rows, features), F32),
        ],
        compiler_params=PARAMS,
        cost_estimate=cost(
            10 * rows * features * count * tile,
            3 * features * count * tile * 2,
            rows * count * tile,
        ),
        name="layer",
    )(both, w_gate, w_up, w_down, *([partial_sum] if resumed else []), *after)


def halve_body(bit, *refs, arrived, final):
    value = refs[0][...]
    if arrived:
        value = value + refs[1][...]
    if final:
        refs[-1][...] = value.astype(BF16)
        return
    kept, sent = refs[-2:]
    half = value.shape[0] // 2
    low, high = value[:half], value[half:]
    upper = bit[0] == 1
    kept[...] = jnp.where(upper, high, low)
    sent[...] = jnp.where(upper, low, high)


def halve(bit, value, arrived, after, final):
    rows, features = value.shape
    if final:
        out_shape = jax.ShapeDtypeStruct((rows, features), BF16)
    else:
        out_shape = [jax.ShapeDtypeStruct((rows // 2, features), F32)] * 2
    return pl.pallas_call(
        functools.partial(halve_body, arrived=bool(arrived), final=final),
        in_specs=[SMEM] + [WHOLE] * (1 + len(arrived)) + [ANY] * len(after),
        out_specs=WHOLE if final else [WHOLE, WHOLE],
        out_shape=out_shape,
        compiler_params=PARAMS,
        cost_estimate=cost(0, 3 * rows * features * 4),
        name="halve",
    )(bit, value, *arrived, *after)


class ScatteredSum:
    def __init__(self, value, axes):
        sizes = [lax.axis_size(axis) for axis in axes]
        self.value, self.arrived, self.levels = value, (), []
        self.done = any(size & (size - 1) for size in sizes)
        if self.done:
            summed = lax.psum_scatter(value, axes, scatter_dimension=0, tiled=True)
            self.value = summed.astype(BF16)
            return
        for axis, size in zip(axes, sizes):
            apart = size // 2
            while apart:
                self.levels.append((axis, size, apart))
                apart //= 2

    def advance(self, after):
        if self.done:
            return ()
        if self.levels:
            axis, size, apart = self.levels.pop(0)
            bit = ((lax.axis_index(axis) // apart) % 2).astype(jnp.int32)[None]
            self.value, sent = halve(bit, self.value, self.arrived, after, False)
            route = [(i, i ^ apart) for i in range(size)]
            self.arrived = (lax.ppermute(sent, axis, route),)
        else:
            bit = jnp.zeros((1,), jnp.int32)
            self.value = halve(bit, self.value, self.arrived, after, True)
            self.done = True
        return (self.value,)


def collect_body(failed, both, *refs, n, places, parts_count, size, pieces):
    roles = Roles(failed, n)
    parts = refs[:parts_count]
    blocks = refs[parts_count : parts_count + len(places)]
    hidden_t, outs, held, sem = refs[-4:]
    tokens, features = both.shape[0], both.shape[1] // 2
    width = outs.shape[1]

    def fetch(j, part):
        rows = pl.ds(size, pieces * tokens) if part == 0 else pl.ds(places[j], tokens)
        here = pl.ds(0, pieces * tokens) if part == 0 else pl.ds(pieces * tokens, tokens)
        return pltpu.make_async_copy(
            blocks[j].at[rows], held.at[j + 1, here], sem.at[j, part]
        )

    for j in range(len(places)):
        for part in range(2):
            fetch(j, part).start()
    for part, begin, piece, to, run in column_pieces([p.shape[1] for p in parts], width):
        units = parts[part][:, begin : begin + run]
        held[0, pl.ds(piece * tokens, tokens), pl.ds(to, run)] = jnp.where(
            roles.lost, jnp.zeros_like(units), units
        )
    slab = pl.ds(pl.multiple_of(features + roles.me * width, 128), width)
    held[0, pl.ds(pieces * tokens, tokens)] = both[:, slab]
    for j in range(len(places)):
        for part in range(2):
            fetch(j, part).wait()

    count = len(places) + 1
    for j in range(count):
        outs[pl.ds(j * tokens, tokens)] = held[j, pl.ds(pieces * tokens, tokens)]
    for piece in range(pieces):
        run = min(width, hidden_t.shape[0] - piece * width)
        rows = pl.ds(piece * tokens, tokens)
        hidden = jnp.concatenate([held[j, rows, :run] for j in range(count)], axis=0)
        hidden_t[pl.ds(piece * width, run)] = hidden.astype(F32).T.astype(BF16)


def collect(failed, n, both, parts, blocks, places, size, width, after):
    tokens = both.shape[0]
    units = sum(part.shape[1] for part in parts)
    pieces = -(-units // width)
    depth = tokens * (len(blocks) + 1)
    return pl.pallas_call(
        functools.partial(
            collect_body,
            n=n,
            places=places,
            parts_count=len(parts),
            size=size,
            pieces=pieces,
        ),
        in_specs=[SMEM]
        + [WHOLE] * (1 + len(parts))
        + [ANY] * (len(blocks) + len(after)),
        out_specs=[WHOLE, WHOLE],
        out_shape=[
            jax.ShapeDtypeStruct((units, depth), BF16),
            jax.ShapeDtypeStruct((depth, width), BF16),
        ],
        scratch_shapes=[
            pltpu.VMEM((len(blocks) + 1, (pieces + 1) * tokens, width), BF16),
            pltpu.SemaphoreType.DMA((len(blocks), 2)),
        ],
        compiler_params=PARAMS,
        cost_estimate=cost(0, 4 * depth * (units + width)),
        name="collect",
    )(failed, both, *parts, *blocks, *after)


def update_body(failed, hid_ref, out_ref, *refs, n, block, first, count, unread):
    state, news = refs[:3], refs[3 + unread : 6 + unread]
    total = refs[6 + unread]
    width = out_ref.shape[1]
    group = row_group(block)

    def step(hid, m_ref, a_ref, b_ref, m_new, a_new, b_new):
        total[...] = jnp.dot(hid[...], out_ref[...], preferred_element_type=F32)

        @pl.loop(0, block // group)
        def _(i):
            here = pl.ds(pl.multiple_of(i * group, group), group)
            m_new[here], a_new[here], b_new[here] = updated(
                m_ref[0, here], a_ref[0, here], b_ref[0, here], total[here], n - 1.0
            )

    deep = pl.Buffered(min(BUFFERS, count + 1))
    old = pl.BlockSpec(
        (1, block, width), lambda i: (0, first + i, 0), pipeline_mode=deep
    )
    new = pl.BlockSpec((block, width), lambda i: (first + i, 0))

    @pl.when(jnp.logical_not(Roles(failed, n).lost))
    def _():
        pltpu.emit_pipeline(
            step,
            grid=(count,),
            in_specs=[
                pl.BlockSpec((block, hid_ref.shape[1]), lambda i: (first + i, 0)),
                old,
                old,
                old,
            ],
            out_specs=[new] * 3,
        )(hid_ref, *state, *news)


def update(failed, n, hidden_t, outs, state, news, after, block, first, count):
    _, rows, width = state[0].shape
    depth = hidden_t.shape[1]
    shape = jax.ShapeDtypeStruct((rows, width), F32)
    unread = len(news) + len(after)
    return pl.pallas_call(
        functools.partial(
            update_body,
            n=n,
            block=block,
            first=first,
            count=count,
            unread=unread,
        ),
        in_specs=[SMEM, ANY, WHOLE] + [ANY] * (3 + unread),
        out_specs=[ANY] * 3,
        out_shape=[shape] * 3,
        scratch_shapes=[pltpu.VMEM((block, width), F32)],
        input_output_aliases={6 + k: k for k in range(len(news))},
        compiler_params=PARAMS,
        cost_estimate=cost(
            2 * count * block * width * depth,
            6 * count * block * width * 4,
            2 * count * block * width,
        ),
        name="update",
    )(failed, hidden_t, outs, *state, *news, *after)


def patch_body(failed, hid_ref, out_ref, *refs, arrivals, chunks, n, count_after):
    count = len(arrivals)
    got = refs[:count]
    rest = refs[count + 3 + count_after :]
    news = rest[:3]
    held, made, total, in_sem, out_sem = rest[3:]
    chunk = made.shape[2]
    group = row_group(chunk)
    roles = Roles(failed, n)
    ahead = roles.ahead()
    lag_of = {True: LAG * (ahead - 1), False: LAG * (n - ahead - 1)}

    def fetch(j):
        rows = got[j].at[pl.ds(0, 3 * chunk)]
        return pltpu.make_async_copy(rows, held.at[j % FETCHED], in_sem.at[j % FETCHED])

    def first_row(j):
        step, forward = arrivals[j]
        place = step - lag_of[forward]
        if not forward:
            place = chunks - 1 - place
        return pl.multiple_of(jnp.clip(place, 0, chunks - 1) * chunk, TILE)

    def store(j, k):
        return pltpu.make_async_copy(
            made.at[j % BUFFERS, k],
            news[k].at[pl.ds(first_row(j), chunk)],
            out_sem.at[j % BUFFERS, k],
        )

    def valid(j):
        step, forward = arrivals[j]
        return step >= lag_of[forward]

    def finish(j):
        @pl.when(valid(j))
        def _():
            for k in range(3):
                store(j, k).wait()

    @pl.when(roles.lost)
    def _():
        for j in range(min(FETCHED - 1, count)):
            fetch(j).start()
        for j in range(count):
            if j + FETCHED - 1 < count:
                fetch(j + FETCHED - 1).start()
            fetch(j).wait()
            if j >= BUFFERS:
                finish(j - BUFFERS)

            @pl.when(valid(j))
            def _(j=j, slot=j % FETCHED, out_slot=j % BUFFERS):
                first = first_row(j)

                units = hid_ref[pl.ds(first, chunk)]
                total[...] = jnp.dot(units, out_ref[...], preferred_element_type=F32)

                @pl.loop(0, chunk // group)
                def _(i):
                    base = pl.multiple_of(i * group, group)
                    old = [
                        held[slot, pl.ds(k * chunk + base, group)].astype(F32)
                        for k in range(3)
                    ]
                    new = updated(*old, total[pl.ds(base, group)], n - 1.0)
                    for k in range(3):
                        made[out_slot, k, pl.ds(base, group)] = new[k]

                for k in range(3):
                    store(j, k).start()

        for j in range(max(count - BUFFERS, 0), count):
            finish(j)


def patch(failed, n, hidden_t, outs, got, arrivals, news, after, chunks):
    rows, width = news[0].shape
    chunk = rows // chunks
    count = len(got)
    shape = jax.ShapeDtypeStruct((rows, width), F32)
    return pl.pallas_call(
        functools.partial(
            patch_body, arrivals=arrivals, chunks=chunks, n=n, count_after=len(after)
        ),
        in_specs=[SMEM, WHOLE, WHOLE] + [ANY] * (count + 3 + len(after)),
        out_specs=[ANY] * 3,
        out_shape=[shape] * 3,
        scratch_shapes=[
            pltpu.VMEM((FETCHED, 3 * chunk, width), BF16),
            pltpu.VMEM((BUFFERS, 3, chunk, width), F32),
            pltpu.VMEM((chunk, width), F32),
            pltpu.SemaphoreType.DMA((FETCHED,)),
            pltpu.SemaphoreType.DMA((BUFFERS, 3)),
        ],
        input_output_aliases={3 + count + k: k for k in range(3)},
        compiler_params=PARAMS,
        cost_estimate=cost(
            2 * count * chunk * width * hidden_t.shape[1],
            count * 3 * chunk * width * 6,
            2 * count * chunk * width,
        ),
        name="patch",
    )(failed, hidden_t, outs, *got, *news, *after)


def per_device(tokens, d_out, w_gate, w_up, w_down, failed, master, moment1, moment2):
    n = lax.axis_size("replica")
    _, rows, width = master.shape
    features, units = w_gate.shape

    order = ring_order(n)

    state = (master, moment1, moment2)
    chunks = largest(
        (c for c in range(2, MOST_CHUNKS + 1, 2) if rows % (TILE * c) == 0), 2
    )
    chunk = rows // chunks
    steps = (chunks + LAG * (n - 2)) // 2
    reach = (n // 2, (n - 1) // 2)
    forward = [(order[p], order[(p + 1) % n]) for p in range(n)]
    backward = [(b, a) for a, b in forward]
    sends, got = [], []
    parcel_from = None

    def send(*after, parcel=()):
        nonlocal parcel_from
        step = len(got)
        seen = got[step - LAG] if step >= LAG else ()
        here = min(step, chunks - 1)
        slabs, passed = (0, 0), (0, 0)
        if parcel:
            parcel_from, slabs = step, reach
        elif parcel_from is not None and (step - parcel_from) % LAG == 0:
            hop = (step - parcel_from) // LAG
            passed = tuple(
                seen[way].shape[0] - 3 * chunk - both.shape[0]
                if hop < reach[way]
                else 0
                for way in range(2)
            )
        sends.append(
            pack(
                failed,
                n,
                state,
                seen,
                parcel,
                after,
                (here, chunks - 1 - here),
                chunk,
                slabs,
                passed,
            )
        )
        got.append(
            (
                lax.ppermute(sends[-1][0], "replica", forward),
                lax.ppermute(sends[-1][1], "replica", backward),
            )
        )
        return (sends[-1][0],)

    sent = send()
    both = beside(tokens[0], d_out[0], sent)
    sent = send(both)
    exchanges = []
    for axis in ("tensor", "fsdp"):
        size = lax.axis_size(axis)
        exchanges += [(axis, size, 1 << k) for k in range((size - 1).bit_length())]
    if all(size & (size - 1) == 0 for _, size, _ in exchanges):
        after = sent
        for level, (axis, size, apart) in enumerate(exchanges):
            other = lax.ppermute(both, axis, [(i, i ^ apart) for i in range(size)])
            last = level == len(exchanges) - 1
            both = join(both, other, after, axis, apart, last)
            after = ()
    else:
        both = lax.all_gather(both[0], ("fsdp", "tensor"), axis=0, tiled=True)
    sent = send(both)

    tile = 128 if units % 128 == 0 else units
    hidden, d_rows = [], None
    pieces = shares(units // tile, PIECES)
    for first, count in pieces:
        part, d_rows = layer(both, w_gate, w_up, w_down, d_rows, sent, tile, first, count)
        hidden.append(part)
        last = len(hidden) == len(pieces)
        sent = send(d_rows, parcel=(both, *hidden) if last else ())
    cotangents = ScatteredSum(d_rows, ("fsdp", "tensor"))

    news = ()
    patched = 0
    hidden_t = outs = None

    def gathered(after):
        blocks, places = [], []
        for way in range(2):
            for hop in range(reach[way]):
                blocks.append(got[parcel_from + LAG * hop][way])
                places.append(blocks[-1].shape[0] - both.shape[0])
        return collect(
            failed, n, both, hidden, blocks, places, 3 * chunk, width, after
        )

    def update_part(first, count, after):
        return update(
            failed, n, hidden_t, outs, state, news, after, block, first, count
        )

    def patch_to(step, after):
        nonlocal patched
        arrivals = [(s, way) for s in range(patched, step) for way in (True, False)]
        if not arrivals:
            return news
        blocks = [b for s in range(patched, step) for b in got[s]]
        patched = step
        return patch(failed, n, hidden_t, outs, blocks, arrivals, news, after, chunks)

    block = largest((b for b in range(TILE, 193, TILE) if rows % b == 0), rows)
    blocks = rows // block
    early = blocks // 4
    ready = parcel_from + LAG * reach[0] + 1
    while len(got) < steps:
        ready_sum = len(got) > parcel_from + SUM_AFTER
        sent = send(*(cotangents.advance(sent) if ready_sum else ()), *news[:1])
        if len(got) == ready and early and len(got) < steps:
            hidden_t, outs = gathered(sent)
            news = update_part(0, early, (hidden_t,))
            news = patch_to(len(got) // 2, ())
    if hidden_t is None:
        hidden_t, outs = gathered(sent)
        early = 0
    news = update_part(early, blocks - early, sent)
    for step in (steps - 2, steps - 1, steps):
        news = patch_to(step, ())
    while not cotangents.done:
        cotangents.advance(sent)
    return (cotangents.value[None], *news)


def solution(mesh):
    placed = (
        P("replica", ("fsdp", "tensor"), None),
        P("replica", ("fsdp", "tensor"), None),
        P(None, ("fsdp", "tensor")),
        P(None, ("fsdp", "tensor")),
        P(("fsdp", "tensor"), None),
        P(("fsdp", "tensor")),
        P(None, ("fsdp", "tensor"), "replica"),
        P(None, ("fsdp", "tensor"), "replica"),
        P(None, ("fsdp", "tensor"), "replica"),
    )
    return jax.shard_map(
        per_device,
        mesh=mesh,
        in_specs=placed,
        out_specs=(
            P("replica", ("fsdp", "tensor"), None),
            P(("fsdp", "tensor"), "replica"),
            P(("fsdp", "tensor"), "replica"),
            P(("fsdp", "tensor"), "replica"),
        ),
        check_vma=False,
    )
```

```python
import functools

import jax
import jax.numpy as jnp
from jax import lax
from jax.experimental import pallas as pl
from jax.experimental.pallas import tpu as pltpu
from jax.sharding import PartitionSpec as P

BF16, F32 = jnp.bfloat16, jnp.float32
SUM_AFTER = 1
LAG = 2
MOST_CHUNKS = 24
TILE = 16
BUFFERS = 3
PIECES = 6
FETCHED = 4
VMEM = 50 << 20

ANY = pl.BlockSpec(memory_space=pl.ANY)
SMEM = pl.BlockSpec(memory_space=pltpu.SMEM)
WHOLE = pl.BlockSpec(memory_space=pltpu.VMEM)
PARAMS = pltpu.CompilerParams(vmem_limit_bytes=VMEM)


def ring_order(n):
    return [0, 1, 3, 2] if n == 4 else list(range(n))


def entry(table, index):
    found = jnp.int32(0)
    for at, value in enumerate(table):
        found = jnp.where(index == at, jnp.int32(value), found)
    return found


class Roles:
    def __init__(self, failed, n):
        self.n = n
        self.order = ring_order(n)
        self.spots = [self.order.index(i) for i in range(n)]
        self.me = lax.axis_index("replica").astype(jnp.int32)
        self.failed = failed[0]
        self.source = lax.rem(self.failed + 1, n)
        self.lost = self.me == self.failed

    def ahead(self):
        apart = entry(self.spots, self.failed) - entry(self.spots, self.source)
        return lax.rem(apart + self.n, self.n)

    def neighbour(self, hops):
        spot = lax.rem(entry(self.spots, self.me) + hops, self.n)
        return entry(self.order, spot)


def largest(options, default):
    options = list(options)
    return max(options) if options else default


def shares(total, parts):
    parts = min(parts, total)
    edges = [total * i // parts for i in range(parts + 1)]
    return [(a, b - a) for a, b in zip(edges, edges[1:])]


def row_group(rows):
    return largest((g for g in (16, 32) if rows % g == 0), rows)


def cost(flops, bytes_accessed, transcendentals=0):
    return pl.CostEstimate(
        flops=flops, bytes_accessed=bytes_accessed, transcendentals=transcendentals
    )


def updated(master_old, first_old, second_old, total, healthy):
    first_new = 0.9 * first_old + (0.1 / healthy) * total
    second_new = 0.95 * second_old + (0.05 / healthy**2) * (total * total)
    root = second_new * lax.rsqrt(second_new)
    step = first_new * pl.reciprocal(root + 1e-08)
    return master_old - 0.01 * step, first_new, second_new


def column_pieces(lengths, width):
    moves, column = [], 0
    for part, length in enumerate(lengths):
        begin = 0
        while begin < length:
            piece, to = divmod(column, width)
            run = min(length - begin, width - to)
            moves.append((part, begin, piece, to, run))
            begin, column = begin + run, column + run
    return moves


def pack_body(*refs, n, places, chunk, slabs, passed, counts):
    count_seen, count_parts, count_after = counts
    if count_seen:
        roles, refs = Roles(refs[0], n), refs[1:]
    state = refs[0:3]
    seen = refs[3 : 3 + count_seen]
    rest = refs[3 + count_seen :]
    if count_parts:
        both, parts, rest = rest[0], rest[1 : 1 + count_parts], rest[1 + count_parts :]
    sends = rest[count_after : count_after + 2]
    held, made, sem, out_sem, below_sem = rest[count_after + 2 :]
    width = held.shape[2]
    size = 3 * chunk

    def rows_of(j):
        way, k = divmod(j, 3)
        return way, pl.ds(k * chunk, chunk)

    def fetch(j):
        way, k = divmod(j, 3)
        rows = pl.ds(places[way] * chunk, chunk)
        return pltpu.make_async_copy(state[k].at[1, rows], held.at[j], sem.at[j])

    def take(j):
        way, rows = rows_of(j)
        return pltpu.make_async_copy(seen[way].at[rows], made.at[way, rows], sem.at[j])

    def store(j):
        way, rows = rows_of(j)
        return pltpu.make_async_copy(
            made.at[way, rows], sends[way].at[rows], out_sem.at[j]
        )

    def convert():
        for j in range(6):
            fetch(j).start()
        for j in range(6):
            way, rows = rows_of(j)
            fetch(j).wait()
            made[way, rows] = held[j].astype(BF16)
            store(j).start()
        for j in range(6):
            store(j).wait()

    def relay():
        for j in range(6):
            take(j).start()
        for j in range(6):
            take(j).wait()
            store(j).start()
        for j in range(6):
            store(j).wait()

    def below(way, inward):
        rows = pl.ds(size, passed[way] or sends[way].shape[0] - size)
        here = made.at[way, rows]
        if inward:
            return pltpu.make_async_copy(seen[way].at[rows], here, below_sem.at[way])
        return pltpu.make_async_copy(here, sends[way].at[rows], below_sem.at[way])

    for way in range(2):
        if passed[way]:
            below(way, True).start()
        if slabs[way]:
            tokens, features = both.shape[0], both.shape[1] // 2
            moves = column_pieces([part.shape[1] for part in parts], width)
            for part, begin, piece, to, run in moves:
                units = parts[part][:, begin : begin + run]
                made[way, pl.ds(size + piece * tokens, tokens), pl.ds(to, run)] = (
                    jnp.where(roles.lost, jnp.zeros_like(units), units)
                )
            row = size + (1 + moves[-1][2]) * tokens
            for far in range(slabs[way], 0, -1):
                target = roles.neighbour(far if way == 0 else n - far)
                slab = pl.ds(pl.multiple_of(features + target * width, 128), width)
                made[way, pl.ds(row, tokens)] = both[:, slab]
                row += tokens
            below(way, False).start()

    for way in range(2):
        if passed[way]:
            below(way, True).wait()
            below(way, False).start()

    if seen:
        pl.when(roles.me == roles.source)(convert)
        pl.when(roles.me != roles.source)(relay)
    else:
        convert()

    for way in range(2):
        if slabs[way] or passed[way]:
            below(way, False).wait()


def pack(failed, n, state, seen, parcel, after, places, chunk, slabs, passed):
    width = state[0].shape[2]
    extra = list(passed)
    if parcel:
        tokens = parcel[0].shape[0]
        pieces = -(-sum(part.shape[1] for part in parcel[1:]) // width)
        extra = [tokens * (pieces + count) if count else 0 for count in slabs]
    counts = (len(seen), max(len(parcel) - 1, 0), len(after))
    return pl.pallas_call(
        functools.partial(
            pack_body,
            n=n,
            places=places,
            chunk=chunk,
            slabs=slabs,
            passed=passed,
            counts=counts,
        ),
        in_specs=[SMEM] * bool(seen)
        + [ANY] * (3 + len(seen))
        + [WHOLE] * len(parcel)
        + [ANY] * len(after),
        out_specs=[ANY, ANY],
        out_shape=[
            jax.ShapeDtypeStruct((3 * chunk + more, width), BF16) for more in extra
        ],
        scratch_shapes=[
            pltpu.VMEM((6, chunk, width), F32),
            pltpu.VMEM((2, 3 * chunk + max(extra), width), BF16),
            pltpu.SemaphoreType.DMA((6,)),
            pltpu.SemaphoreType.DMA((6,)),
            pltpu.SemaphoreType.DMA((2,)),
        ],
        compiler_params=PARAMS,
        cost_estimate=cost(0, 2 * 3 * chunk * width * 6),
        name="pack",
    )(*([failed] if seen else []), *state, *seen, *parcel, *after)


def beside_body(*refs):
    tokens, d_out, out = refs[0], refs[1], refs[-1]
    width = tokens.shape[1]
    out[0, :, :width] = tokens[...]
    out[0, :, width:] = d_out[...]


def beside(tokens, d_out, after):
    rows, width = tokens.shape
    return pl.pallas_call(
        beside_body,
        in_specs=[WHOLE, WHOLE] + [ANY] * len(after),
        out_specs=WHOLE,
        out_shape=jax.ShapeDtypeStruct((1, rows, 2 * width), tokens.dtype),
        compiler_params=PARAMS,
        cost_estimate=cost(0, 4 * rows * width * 2),
        name="beside",
    )(tokens, d_out, *after)


def join_body(own, other, *refs, axis, apart, last):
    out = refs[-1]
    count, rows = own.shape[:2]
    second = lax.rem(lax.div(lax.axis_index(axis).astype(jnp.int32), apart), 2)
    if not last:
        out[pl.ds(second * count, count)] = own[...]
        out[pl.ds((1 - second) * count, count)] = other[...]
        return
    for i in range(2 * count):
        here, there = (own, other) if i < count else (other, own)
        value = jnp.where(second == 1, there[i % count], here[i % count])
        out[pl.ds(i * rows, rows)] = value


def join(own, other, after, axis, apart, last):
    count, rows, width = own.shape
    shape = (2 * count * rows, width) if last else (2 * count, rows, width)
    return pl.pallas_call(
        functools.partial(join_body, axis=axis, apart=apart, last=last),
        in_specs=[WHOLE, WHOLE] + [ANY] * len(after),
        out_specs=WHOLE,
        out_shape=jax.ShapeDtypeStruct(shape, own.dtype),
        compiler_params=PARAMS,
        cost_estimate=cost(0, 8 * count * rows * width),
        name="join",
    )(own, other, *after)


def by_rows(a, b):
    return lax.dot_general(a, b, (((1,), (1,)), ((), ())), preferred_element_type=F32)


def layer_body(both, *refs, resumed, tile, first, count):
    weights = refs[:3]
    hidden_ref, sum_ref = refs[-2:]
    features = weights[0].shape[0]
    rows = both.shape[0]
    joined = tile % 128 == 0
    sum_ref[...] = refs[3][...] if resumed else jnp.zeros_like(sum_ref)

    def step(gate_ref, up_ref, down_ref, hidden):
        x, dy = both[:, :features], both[:, features:]
        w_gate, w_up = gate_ref[...], up_ref[...]
        if joined:
            w_both = jnp.concatenate([w_gate, w_up], axis=1)
            gate_up = jnp.dot(x, w_both, preferred_element_type=F32)
            gate, up = gate_up[:, :tile], gate_up[:, tile:]
        else:
            gate = jnp.dot(x, w_gate, preferred_element_type=F32)
            up = jnp.dot(x, w_up, preferred_element_type=F32)
        d_hidden = by_rows(dy, down_ref[...])
        sig = 1.0 / (1.0 + jnp.exp(-gate))
        hidden[...] = (gate * sig * up).astype(BF16)
        d_gate = (d_hidden * up * sig * (1.0 + gate * (1.0 - sig))).astype(BF16)
        d_up = (d_hidden * gate * sig).astype(BF16)
        if joined:
            sum_ref[...] += by_rows(jnp.concatenate([d_gate, d_up], axis=1), w_both)
        else:
            sum_ref[...] += by_rows(d_gate, w_gate) + by_rows(d_up, w_up)

    deep = pl.Buffered(min(BUFFERS, count + 1))
    across = pl.BlockSpec((features, tile), lambda i: (0, first + i), pipeline_mode=deep)
    pltpu.emit_pipeline(
        step,
        grid=(count,),
        in_specs=[
            across,
            across,
            pl.BlockSpec((tile, features), lambda i: (first + i, 0), pipeline_mode=deep),
        ],
        out_specs=[pl.BlockSpec((rows, tile), lambda i: (0, i))],
    )(*weights, hidden_ref)


def layer(both, w_gate, w_up, w_down, partial_sum, after, tile, first, count):
    rows = both.shape[0]
    features = w_gate.shape[0]
    resumed = partial_sum is not None
    return pl.pallas_call(
        functools.partial(layer_body, resumed=resumed, tile=tile, first=first, count=count),
        in_specs=[WHOLE] + [ANY] * 3 + [WHOLE] * resumed + [ANY] * len(after),
        out_specs=[ANY, WHOLE],
        out_shape=[
            jax.ShapeDtypeStruct((rows, count * tile), BF16),
            jax.ShapeDtypeStruct((rows, features), F32),
        ],
        compiler_params=PARAMS,
        cost_estimate=cost(
            10 * rows * features * count * tile,
            3 * features * count * tile * 2,
            rows * count * tile,
        ),
        name="layer",
    )(both, w_gate, w_up, w_down, *([partial_sum] if resumed else []), *after)


def halve_body(bit, *refs, arrived, final):
    value = refs[0][...]
    if arrived:
        value = value + refs[1][...]
    if final:
        refs[-1][...] = value.astype(BF16)
        return
    kept, sent = refs[-2:]
    half = value.shape[0] // 2
    low, high = value[:half], value[half:]
    upper = bit[0] == 1
    kept[...] = jnp.where(upper, high, low)
    sent[...] = jnp.where(upper, low, high)


def halve(bit, value, arrived, after, final):
    rows, features = value.shape
    if final:
        out_shape = jax.ShapeDtypeStruct((rows, features), BF16)
    else:
        out_shape = [jax.ShapeDtypeStruct((rows // 2, features), F32)] * 2
    return pl.pallas_call(
        functools.partial(halve_body, arrived=bool(arrived), final=final),
        in_specs=[SMEM] + [WHOLE] * (1 + len(arrived)) + [ANY] * len(after),
        out_specs=WHOLE if final else [WHOLE, WHOLE],
        out_shape=out_shape,
        compiler_params=PARAMS,
        cost_estimate=cost(0, 3 * rows * features * 4),
        name="halve",
    )(bit, value, *arrived, *after)


class ScatteredSum:
    def __init__(self, value, axes):
        sizes = [lax.axis_size(axis) for axis in axes]
        self.value, self.arrived, self.levels = value, (), []
        self.done = any(size & (size - 1) for size in sizes)
        if self.done:
            summed = lax.psum_scatter(value, axes, scatter_dimension=0, tiled=True)
            self.value = summed.astype(BF16)
            return
        for axis, size in zip(axes, sizes):
            apart = size // 2
            while apart:
                self.levels.append((axis, size, apart))
                apart //= 2

    def advance(self, after):
        if self.done:
            return ()
        if self.levels:
            axis, size, apart = self.levels.pop(0)
            bit = ((lax.axis_index(axis) // apart) % 2).astype(jnp.int32)[None]
            self.value, sent = halve(bit, self.value, self.arrived, after, False)
            route = [(i, i ^ apart) for i in range(size)]
            self.arrived = (lax.ppermute(sent, axis, route),)
        else:
            bit = jnp.zeros((1,), jnp.int32)
            self.value = halve(bit, self.value, self.arrived, after, True)
            self.done = True
        return (self.value,)


def collect_body(failed, both, *refs, n, places, parts_count, size, pieces):
    roles = Roles(failed, n)
    parts = refs[:parts_count]
    blocks = refs[parts_count : parts_count + len(places)]
    hidden_t, outs, held, sem = refs[-4:]
    tokens, features = both.shape[0], both.shape[1] // 2
    width = outs.shape[1]

    def fetch(j, part):
        rows = pl.ds(size, pieces * tokens) if part == 0 else pl.ds(places[j], tokens)
        here = pl.ds(0, pieces * tokens) if part == 0 else pl.ds(pieces * tokens, tokens)
        return pltpu.make_async_copy(
            blocks[j].at[rows], held.at[j + 1, here], sem.at[j, part]
        )

    for j in range(len(places)):
        for part in range(2):
            fetch(j, part).start()
    for part, begin, piece, to, run in column_pieces([p.shape[1] for p in parts], width):
        units = parts[part][:, begin : begin + run]
        held[0, pl.ds(piece * tokens, tokens), pl.ds(to, run)] = jnp.where(
            roles.lost, jnp.zeros_like(units), units
        )
    slab = pl.ds(pl.multiple_of(features + roles.me * width, 128), width)
    held[0, pl.ds(pieces * tokens, tokens)] = both[:, slab]
    for j in range(len(places)):
        for part in range(2):
            fetch(j, part).wait()

    count = len(places) + 1
    for j in range(count):
        outs[pl.ds(j * tokens, tokens)] = held[j, pl.ds(pieces * tokens, tokens)]
    for piece in range(pieces):
        run = min(width, hidden_t.shape[0] - piece * width)
        rows = pl.ds(piece * tokens, tokens)
        hidden = jnp.concatenate([held[j, rows, :run] for j in range(count)], axis=0)
        hidden_t[pl.ds(piece * width, run)] = hidden.astype(F32).T.astype(BF16)


def collect(failed, n, both, parts, blocks, places, size, width, after):
    tokens = both.shape[0]
    units = sum(part.shape[1] for part in parts)
    pieces = -(-units // width)
    depth = tokens * (len(blocks) + 1)
    return pl.pallas_call(
        functools.partial(
            collect_body,
            n=n,
            places=places,
            parts_count=len(parts),
            size=size,
            pieces=pieces,
        ),
        in_specs=[SMEM]
        + [WHOLE] * (1 + len(parts))
        + [ANY] * (len(blocks) + len(after)),
        out_specs=[WHOLE, WHOLE],
        out_shape=[
            jax.ShapeDtypeStruct((units, depth), BF16),
            jax.ShapeDtypeStruct((depth, width), BF16),
        ],
        scratch_shapes=[
            pltpu.VMEM((len(blocks) + 1, (pieces + 1) * tokens, width), BF16),
            pltpu.SemaphoreType.DMA((len(blocks), 2)),
        ],
        compiler_params=PARAMS,
        cost_estimate=cost(0, 4 * depth * (units + width)),
        name="collect",
    )(failed, both, *parts, *blocks, *after)


def update_body(failed, hid_ref, out_ref, *refs, n, block, first, count, unread):
    state, news = refs[:3], refs[3 + unread : 6 + unread]
    total = refs[6 + unread]
    width = out_ref.shape[1]
    group = row_group(block)

    def step(hid, m_ref, a_ref, b_ref, m_new, a_new, b_new):
        total[...] = jnp.dot(hid[...], out_ref[...], preferred_element_type=F32)

        @pl.loop(0, block // group)
        def _(i):
            here = pl.ds(pl.multiple_of(i * group, group), group)
            m_new[here], a_new[here], b_new[here] = updated(
                m_ref[0, here], a_ref[0, here], b_ref[0, here], total[here], n - 1.0
            )

    deep = pl.Buffered(min(BUFFERS, count + 1))
    old = pl.BlockSpec(
        (1, block, width), lambda i: (0, first + i, 0), pipeline_mode=deep
    )
    new = pl.BlockSpec((block, width), lambda i: (first + i, 0))

    @pl.when(jnp.logical_not(Roles(failed, n).lost))
    def _():
        pltpu.emit_pipeline(
            step,
            grid=(count,),
            in_specs=[
                pl.BlockSpec((block, hid_ref.shape[1]), lambda i: (first + i, 0)),
                old,
                old,
                old,
            ],
            out_specs=[new] * 3,
        )(hid_ref, *state, *news)


def update(failed, n, hidden_t, outs, state, news, after, block, first, count):
    _, rows, width = state[0].shape
    depth = hidden_t.shape[1]
    shape = jax.ShapeDtypeStruct((rows, width), F32)
    unread = len(news) + len(after)
    return pl.pallas_call(
        functools.partial(
            update_body,
            n=n,
            block=block,
            first=first,
            count=count,
            unread=unread,
        ),
        in_specs=[SMEM, ANY, WHOLE] + [ANY] * (3 + unread),
        out_specs=[ANY] * 3,
        out_shape=[shape] * 3,
        scratch_shapes=[pltpu.VMEM((block, width), F32)],
        input_output_aliases={6 + k: k for k in range(len(news))},
        compiler_params=PARAMS,
        cost_estimate=cost(
            2 * count * block * width * depth,
            6 * count * block * width * 4,
            2 * count * block * width,
        ),
        name="update",
    )(failed, hidden_t, outs, *state, *news, *after)


def patch_body(failed, hid_ref, out_ref, *refs, arrivals, chunks, n, count_after):
    count = len(arrivals)
    got = refs[:count]
    rest = refs[count + 3 + count_after :]
    news = rest[:3]
    held, made, total, in_sem, out_sem = rest[3:]
    chunk = made.shape[2]
    group = row_group(chunk)
    roles = Roles(failed, n)
    ahead = roles.ahead()
    lag_of = {True: LAG * (ahead - 1), False: LAG * (n - ahead - 1)}

    def fetch(j):
        rows = got[j].at[pl.ds(0, 3 * chunk)]
        return pltpu.make_async_copy(rows, held.at[j % FETCHED], in_sem.at[j % FETCHED])

    def first_row(j):
        step, forward = arrivals[j]
        place = step - lag_of[forward]
        if not forward:
            place = chunks - 1 - place
        return pl.multiple_of(jnp.clip(place, 0, chunks - 1) * chunk, TILE)

    def store(j, k):
        return pltpu.make_async_copy(
            made.at[j % BUFFERS, k],
            news[k].at[pl.ds(first_row(j), chunk)],
            out_sem.at[j % BUFFERS, k],
        )

    def valid(j):
        step, forward = arrivals[j]
        return step >= lag_of[forward]

    def finish(j):
        @pl.when(valid(j))
        def _():
            for k in range(3):
                store(j, k).wait()

    @pl.when(roles.lost)
    def _():
        for j in range(min(FETCHED - 1, count)):
            fetch(j).start()
        for j in range(count):
            if j + FETCHED - 1 < count:
                fetch(j + FETCHED - 1).start()
            fetch(j).wait()
            if j >= BUFFERS:
                finish(j - BUFFERS)

            @pl.when(valid(j))
            def _(j=j, slot=j % FETCHED, out_slot=j % BUFFERS):
                first = first_row(j)

                units = hid_ref[pl.ds(first, chunk)]
                total[...] = jnp.dot(units, out_ref[...], preferred_element_type=F32)

                @pl.loop(0, chunk // group)
                def _(i):
                    base = pl.multiple_of(i * group, group)
                    old = [
                        held[slot, pl.ds(k * chunk + base, group)].astype(F32)
                        for k in range(3)
                    ]
                    new = updated(*old, total[pl.ds(base, group)], n - 1.0)
                    for k in range(3):
                        made[out_slot, k, pl.ds(base, group)] = new[k]

                for k in range(3):
                    store(j, k).start()

        for j in range(max(count - BUFFERS, 0), count):
            finish(j)


def patch(failed, n, hidden_t, outs, got, arrivals, news, after, chunks):
    rows, width = news[0].shape
    chunk = rows // chunks
    count = len(got)
    shape = jax.ShapeDtypeStruct((rows, width), F32)
    return pl.pallas_call(
        functools.partial(
            patch_body, arrivals=arrivals, chunks=chunks, n=n, count_after=len(after)
        ),
        in_specs=[SMEM, WHOLE, WHOLE] + [ANY] * (count + 3 + len(after)),
        out_specs=[ANY] * 3,
        out_shape=[shape] * 3,
        scratch_shapes=[
            pltpu.VMEM((FETCHED, 3 * chunk, width), BF16),
            pltpu.VMEM((BUFFERS, 3, chunk, width), F32),
            pltpu.VMEM((chunk, width), F32),
            pltpu.SemaphoreType.DMA((FETCHED,)),
            pltpu.SemaphoreType.DMA((BUFFERS, 3)),
        ],
        input_output_aliases={3 + count + k: k for k in range(3)},
        compiler_params=PARAMS,
        cost_estimate=cost(
            2 * count * chunk * width * hidden_t.shape[1],
            count * 3 * chunk * width * 6,
            2 * count * chunk * width,
        ),
        name="patch",
    )(failed, hidden_t, outs, *got, *news, *after)


def per_device(tokens, d_out, w_gate, w_up, w_down, failed, master, moment1, moment2):
    n = lax.axis_size("replica")
    _, rows, width = master.shape
    features, units = w_gate.shape

    order = ring_order(n)

    state = (master, moment1, moment2)
    chunks = largest(
        (c for c in range(2, MOST_CHUNKS + 1, 2) if rows % (TILE * c) == 0), 2
    )
    chunk = rows // chunks
    steps = (chunks + LAG * (n - 2)) // 2
    reach = (n // 2, (n - 1) // 2)
    forward = [(order[p], order[(p + 1) % n]) for p in range(n)]
    backward = [(b, a) for a, b in forward]
    sends, got = [], []
    parcel_from = None

    def send(*after, parcel=()):
        nonlocal parcel_from
        step = len(got)
        seen = got[step - LAG] if step >= LAG else ()
        here = min(step, chunks - 1)
        slabs, passed = (0, 0), (0, 0)
        if parcel:
            parcel_from, slabs = step, reach
        elif parcel_from is not None and (step - parcel_from) % LAG == 0:
            hop = (step - parcel_from) // LAG
            passed = tuple(
                seen[way].shape[0] - 3 * chunk - both.shape[0]
                if hop < reach[way]
                else 0
                for way in range(2)
            )
        sends.append(
            pack(
                failed,
                n,
                state,
                seen,
                parcel,
                after,
                (here, chunks - 1 - here),
                chunk,
                slabs,
                passed,
            )
        )
        got.append(
            (
                lax.ppermute(sends[-1][0], "replica", forward),
                lax.ppermute(sends[-1][1], "replica", backward),
            )
        )
        return (sends[-1][0],)

    sent = send()
    both = beside(tokens[0], d_out[0], sent)
    sent = send(both)
    exchanges = []
    for axis in ("tensor", "fsdp"):
        size = lax.axis_size(axis)
        exchanges += [(axis, size, 1 << k) for k in range((size - 1).bit_length())]
    if all(size & (size - 1) == 0 for _, size, _ in exchanges):
        after = sent
        for level, (axis, size, apart) in enumerate(exchanges):
            other = lax.ppermute(both, axis, [(i, i ^ apart) for i in range(size)])
            last = level == len(exchanges) - 1
            both = join(both, other, after, axis, apart, last)
            after = ()
    else:
        both = lax.all_gather(both[0], ("fsdp", "tensor"), axis=0, tiled=True)
    sent = send(both)

    tile = 128 if units % 128 == 0 else units
    hidden, d_rows = [], None
    pieces = shares(units // tile, PIECES)
    for first, count in pieces:
        part, d_rows = layer(both, w_gate, w_up, w_down, d_rows, sent, tile, first, count)
        hidden.append(part)
        last = len(hidden) == len(pieces)
        sent = send(d_rows, parcel=(both, *hidden) if last else ())
    cotangents = ScatteredSum(d_rows, ("fsdp", "tensor"))

    news = ()
    patched = 0
    hidden_t = outs = None

    def gathered(after):
        blocks, places = [], []
        for way in range(2):
            for hop in range(reach[way]):
                blocks.append(got[parcel_from + LAG * hop][way])
                places.append(blocks[-1].shape[0] - both.shape[0])
        return collect(
            failed, n, both, hidden, blocks, places, 3 * chunk, width, after
        )

    def update_part(first, count, after):
        return update(
            failed, n, hidden_t, outs, state, news, after, block, first, count
        )

    def patch_to(step, after):
        nonlocal patched
        arrivals = [(s, way) for s in range(patched, step) for way in (True, False)]
        if not arrivals:
            return news
        blocks = [b for s in range(patched, step) for b in got[s]]
        patched = step
        return patch(failed, n, hidden_t, outs, blocks, arrivals, news, after, chunks)

    block = largest((b for b in range(TILE, 193, TILE) if rows % b == 0), rows)
    blocks = rows // block
    early = blocks // 3
    ready = parcel_from + LAG * reach[0] + 1
    while len(got) < steps:
        ready_sum = len(got) > parcel_from + SUM_AFTER
        sent = send(*(cotangents.advance(sent) if ready_sum else ()), *news[:1])
        if len(got) == ready and early and len(got) < steps:
            hidden_t, outs = gathered(sent)
            news = update_part(0, early, (hidden_t,))
            news = patch_to(len(got) // 3, ())
    if hidden_t is None:
        hidden_t, outs = gathered(sent)
        early = 0
    news = update_part(early, blocks - early, sent)
    for step in (steps - 2, steps - 1, steps):
        news = patch_to(step, ())
    while not cotangents.done:
        cotangents.advance(sent)
    return (cotangents.value[None], *news)


def solution(mesh):
    placed = (
        P("replica", ("fsdp", "tensor"), None),
        P("replica", ("fsdp", "tensor"), None),
        P(None, ("fsdp", "tensor")),
        P(None, ("fsdp", "tensor")),
        P(("fsdp", "tensor"), None),
        P(("fsdp", "tensor")),
        P(None, ("fsdp", "tensor"), "replica"),
        P(None, ("fsdp", "tensor"), "replica"),
        P(None, ("fsdp", "tensor"), "replica"),
    )
    return jax.shard_map(
        per_device,
        mesh=mesh,
        in_specs=placed,
        out_specs=(
            P("replica", ("fsdp", "tensor"), None),
            P(("fsdp", "tensor"), "replica"),
            P(("fsdp", "tensor"), "replica"),
            P(("fsdp", "tensor"), "replica"),
        ),
        check_vma=False,
    )
```

```python
import functools

import jax
import jax.numpy as jnp
from jax import lax
from jax.experimental import pallas as pl
from jax.experimental.pallas import tpu as pltpu
from jax.sharding import PartitionSpec as P

BF16, F32 = jnp.bfloat16, jnp.float32
SUM_AFTER = 1
LAG = 2
MOST_CHUNKS = 24
TILE = 16
BUFFERS = 3
PIECES = 6
FETCHED = 4
VMEM = 50 << 20

ANY = pl.BlockSpec(memory_space=pl.ANY)
SMEM = pl.BlockSpec(memory_space=pltpu.SMEM)
WHOLE = pl.BlockSpec(memory_space=pltpu.VMEM)
PARAMS = pltpu.CompilerParams(vmem_limit_bytes=VMEM)


def ring_order(n):
    return [0, 1, 3, 2] if n == 4 else list(range(n))


def entry(table, index):
    found = jnp.int32(0)
    for at, value in enumerate(table):
        found = jnp.where(index == at, jnp.int32(value), found)
    return found


class Roles:
    def __init__(self, failed, n):
        self.n = n
        self.order = ring_order(n)
        self.spots = [self.order.index(i) for i in range(n)]
        self.me = lax.axis_index("replica").astype(jnp.int32)
        self.failed = failed[0]
        self.source = lax.rem(self.failed + 1, n)
        self.lost = self.me == self.failed

    def ahead(self):
        apart = entry(self.spots, self.failed) - entry(self.spots, self.source)
        return lax.rem(apart + self.n, self.n)

    def neighbour(self, hops):
        spot = lax.rem(entry(self.spots, self.me) + hops, self.n)
        return entry(self.order, spot)


def largest(options, default):
    options = list(options)
    return max(options) if options else default


def shares(total, parts):
    parts = min(parts, total)
    edges = [total * i // parts for i in range(parts + 1)]
    return [(a, b - a) for a, b in zip(edges, edges[1:])]


def row_group(rows):
    return largest((g for g in (16, 32) if rows % g == 0), rows)


def cost(flops, bytes_accessed, transcendentals=0):
    return pl.CostEstimate(
        flops=flops, bytes_accessed=bytes_accessed, transcendentals=transcendentals
    )


def updated(master_old, first_old, second_old, total, healthy):
    first_new = 0.9 * first_old + (0.1 / healthy) * total
    second_new = 0.95 * second_old + (0.05 / healthy**2) * (total * total)
    root = second_new * lax.rsqrt(second_new)
    step = first_new * pl.reciprocal(root + 1e-08)
    return master_old - 0.01 * step, first_new, second_new


def column_pieces(lengths, width):
    moves, column = [], 0
    for part, length in enumerate(lengths):
        begin = 0
        while begin < length:
            piece, to = divmod(column, width)
            run = min(length - begin, width - to)
            moves.append((part, begin, piece, to, run))
            begin, column = begin + run, column + run
    return moves


def pack_body(*refs, n, places, chunk, slabs, passed, counts):
    count_seen, count_parts, count_after = counts
    if count_seen:
        roles, refs = Roles(refs[0], n), refs[1:]
    state = refs[0:3]
    seen = refs[3 : 3 + count_seen]
    rest = refs[3 + count_seen :]
    if count_parts:
        both, parts, rest = rest[0], rest[1 : 1 + count_parts], rest[1 + count_parts :]
    sends = rest[count_after : count_after + 2]
    held, made, sem, out_sem, below_sem = rest[count_after + 2 :]
    width = held.shape[2]
    size = 3 * chunk

    def rows_of(j):
        way, k = divmod(j, 3)
        return way, pl.ds(k * chunk, chunk)

    def fetch(j):
        way, k = divmod(j, 3)
        rows = pl.ds(places[way] * chunk, chunk)
        return pltpu.make_async_copy(state[k].at[1, rows], held.at[j], sem.at[j])

    def take(j):
        way, rows = rows_of(j)
        return pltpu.make_async_copy(seen[way].at[rows], made.at[way, rows], sem.at[j])

    def store(j):
        way, rows = rows_of(j)
        return pltpu.make_async_copy(
            made.at[way, rows], sends[way].at[rows], out_sem.at[j]
        )

    def convert():
        for j in range(6):
            fetch(j).start()
        for j in range(6):
            way, rows = rows_of(j)
            fetch(j).wait()
            made[way, rows] = held[j].astype(BF16)
            store(j).start()
        for j in range(6):
            store(j).wait()

    def relay():
        for j in range(6):
            take(j).start()
        for j in range(6):
            take(j).wait()
            store(j).start()
        for j in range(6):
            store(j).wait()

    def below(way, inward):
        rows = pl.ds(size, passed[way] or sends[way].shape[0] - size)
        here = made.at[way, rows]
        if inward:
            return pltpu.make_async_copy(seen[way].at[rows], here, below_sem.at[way])
        return pltpu.make_async_copy(here, sends[way].at[rows], below_sem.at[way])

    for way in range(2):
        if passed[way]:
            below(way, True).start()
        if slabs[way]:
            tokens, features = both.shape[0], both.shape[1] // 2
            moves = column_pieces([part.shape[1] for part in parts], width)
            for part, begin, piece, to, run in moves:
                units = parts[part][:, begin : begin + run]
                made[way, pl.ds(size + piece * tokens, tokens), pl.ds(to, run)] = (
                    jnp.where(roles.lost, jnp.zeros_like(units), units)
                )
            row = size + (1 + moves[-1][2]) * tokens
            for far in range(slabs[way], 0, -1):
                target = roles.neighbour(far if way == 0 else n - far)
                slab = pl.ds(pl.multiple_of(features + target * width, 128), width)
                made[way, pl.ds(row, tokens)] = both[:, slab]
                row += tokens
            below(way, False).start()

    for way in range(2):
        if passed[way]:
            below(way, True).wait()
            below(way, False).start()

    if seen:
        pl.when(roles.me == roles.source)(convert)
        pl.when(roles.me != roles.source)(relay)
    else:
        convert()

    for way in range(2):
        if slabs[way] or passed[way]:
            below(way, False).wait()


def pack(failed, n, state, seen, parcel, after, places, chunk, slabs, passed):
    width = state[0].shape[2]
    extra = list(passed)
    if parcel:
        tokens = parcel[0].shape[0]
        pieces = -(-sum(part.shape[1] for part in parcel[1:]) // width)
        extra = [tokens * (pieces + count) if count else 0 for count in slabs]
    counts = (len(seen), max(len(parcel) - 1, 0), len(after))
    return pl.pallas_call(
        functools.partial(
            pack_body,
            n=n,
            places=places,
            chunk=chunk,
            slabs=slabs,
            passed=passed,
            counts=counts,
        ),
        in_specs=[SMEM] * bool(seen)
        + [ANY] * (3 + len(seen))
        + [WHOLE] * len(parcel)
        + [ANY] * len(after),
        out_specs=[ANY, ANY],
        out_shape=[
            jax.ShapeDtypeStruct((3 * chunk + more, width), BF16) for more in extra
        ],
        scratch_shapes=[
            pltpu.VMEM((6, chunk, width), F32),
            pltpu.VMEM((2, 3 * chunk + max(extra), width), BF16),
            pltpu.SemaphoreType.DMA((6,)),
            pltpu.SemaphoreType.DMA((6,)),
            pltpu.SemaphoreType.DMA((2,)),
        ],
        compiler_params=PARAMS,
        cost_estimate=cost(0, 2 * 3 * chunk * width * 6),
        name="pack",
    )(*([failed] if seen else []), *state, *seen, *parcel, *after)


def beside_body(*refs):
    tokens, d_out, out = refs[0], refs[1], refs[-1]
    width = tokens.shape[1]
    out[0, :, :width] = tokens[...]
    out[0, :, width:] = d_out[...]


def beside(tokens, d_out, after):
    rows, width = tokens.shape
    return pl.pallas_call(
        beside_body,
        in_specs=[WHOLE, WHOLE] + [ANY] * len(after),
        out_specs=WHOLE,
        out_shape=jax.ShapeDtypeStruct((1, rows, 2 * width), tokens.dtype),
        compiler_params=PARAMS,
        cost_estimate=cost(0, 4 * rows * width * 2),
        name="beside",
    )(tokens, d_out, *after)


def join_body(own, other, *refs, axis, apart, last):
    out = refs[-1]
    count, rows = own.shape[:2]
    second = lax.rem(lax.div(lax.axis_index(axis).astype(jnp.int32), apart), 2)
    if not last:
        out[pl.ds(second * count, count)] = own[...]
        out[pl.ds((1 - second) * count, count)] = other[...]
        return
    for i in range(2 * count):
        here, there = (own, other) if i < count else (other, own)
        value = jnp.where(second == 1, there[i % count], here[i % count])
        out[pl.ds(i * rows, rows)] = value


def join(own, other, after, axis, apart, last):
    count, rows, width = own.shape
    shape = (2 * count * rows, width) if last else (2 * count, rows, width)
    return pl.pallas_call(
        functools.partial(join_body, axis=axis, apart=apart, last=last),
        in_specs=[WHOLE, WHOLE] + [ANY] * len(after),
        out_specs=WHOLE,
        out_shape=jax.ShapeDtypeStruct(shape, own.dtype),
        compiler_params=PARAMS,
        cost_estimate=cost(0, 8 * count * rows * width),
        name="join",
    )(own, other, *after)


def by_rows(a, b):
    return lax.dot_general(a, b, (((1,), (1,)), ((), ())), preferred_element_type=F32)


def layer_body(both, *refs, resumed, tile, first, count):
    weights = refs[:3]
    hidden_ref, sum_ref = refs[-2:]
    features = weights[0].shape[0]
    rows = both.shape[0]
    joined = tile % 128 == 0
    sum_ref[...] = refs[3][...] if resumed else jnp.zeros_like(sum_ref)

    def step(gate_ref, up_ref, down_ref, hidden):
        x, dy = both[:, :features], both[:, features:]
        w_gate, w_up = gate_ref[...], up_ref[...]
        if joined:
            w_both = jnp.concatenate([w_gate, w_up], axis=1)
            gate_up = jnp.dot(x, w_both, preferred_element_type=F32)
            gate, up = gate_up[:, :tile], gate_up[:, tile:]
        else:
            gate = jnp.dot(x, w_gate, preferred_element_type=F32)
            up = jnp.dot(x, w_up, preferred_element_type=F32)
        d_hidden = by_rows(dy, down_ref[...])
        sig = 1.0 / (1.0 + jnp.exp(-gate))
        hidden[...] = (gate * sig * up).astype(BF16)
        d_gate = (d_hidden * up * sig * (1.0 + gate * (1.0 - sig))).astype(BF16)
        d_up = (d_hidden * gate * sig).astype(BF16)
        if joined:
            sum_ref[...] += by_rows(jnp.concatenate([d_gate, d_up], axis=1), w_both)
        else:
            sum_ref[...] += by_rows(d_gate, w_gate) + by_rows(d_up, w_up)

    deep = pl.Buffered(min(BUFFERS, count + 1))
    across = pl.BlockSpec((features, tile), lambda i: (0, first + i), pipeline_mode=deep)
    pltpu.emit_pipeline(
        step,
        grid=(count,),
        in_specs=[
            across,
            across,
            pl.BlockSpec((tile, features), lambda i: (first + i, 0), pipeline_mode=deep),
        ],
        out_specs=[pl.BlockSpec((rows, tile), lambda i: (0, i))],
    )(*weights, hidden_ref)


def layer(both, w_gate, w_up, w_down, partial_sum, after, tile, first, count):
    rows = both.shape[0]
    features = w_gate.shape[0]
    resumed = partial_sum is not None
    return pl.pallas_call(
        functools.partial(layer_body, resumed=resumed, tile=tile, first=first, count=count),
        in_specs=[WHOLE] + [ANY] * 3 + [WHOLE] * resumed + [ANY] * len(after),
        out_specs=[ANY, WHOLE],
        out_shape=[
            jax.ShapeDtypeStruct((rows, count * tile), BF16),
            jax.ShapeDtypeStruct((rows, features), F32),
        ],
        compiler_params=PARAMS,
        cost_estimate=cost(
            10 * rows * features * count * tile,
            3 * features * count * tile * 2,
            rows * count * tile,
        ),
        name="layer",
    )(both, w_gate, w_up, w_down, *([partial_sum] if resumed else []), *after)


def halve_body(bit, *refs, arrived, final):
    value = refs[0][...]
    if arrived:
        value = value + refs[1][...]
    if final:
        refs[-1][...] = value.astype(BF16)
        return
    kept, sent = refs[-2:]
    half = value.shape[0] // 2
    low, high = value[:half], value[half:]
    upper = bit[0] == 1
    kept[...] = jnp.where(upper, high, low)
    sent[...] = jnp.where(upper, low, high)


def halve(bit, value, arrived, after, final):
    rows, features = value.shape
    if final:
        out_shape = jax.ShapeDtypeStruct((rows, features), BF16)
    else:
        out_shape = [jax.ShapeDtypeStruct((rows // 2, features), F32)] * 2
    return pl.pallas_call(
        functools.partial(halve_body, arrived=bool(arrived), final=final),
        in_specs=[SMEM] + [WHOLE] * (1 + len(arrived)) + [ANY] * len(after),
        out_specs=WHOLE if final else [WHOLE, WHOLE],
        out_shape=out_shape,
        compiler_params=PARAMS,
        cost_estimate=cost(0, 3 * rows * features * 4),
        name="halve",
    )(bit, value, *arrived, *after)


class ScatteredSum:
    def __init__(self, value, axes):
        sizes = [lax.axis_size(axis) for axis in axes]
        self.value, self.arrived, self.levels = value, (), []
        self.done = any(size & (size - 1) for size in sizes)
        if self.done:
            summed = lax.psum_scatter(value, axes, scatter_dimension=0, tiled=True)
            self.value = summed.astype(BF16)
            return
        for axis, size in zip(axes, sizes):
            apart = size // 2
            while apart:
                self.levels.append((axis, size, apart))
                apart //= 2

    def advance(self, after):
        if self.done:
            return ()
        if self.levels:
            axis, size, apart = self.levels.pop(0)
            bit = ((lax.axis_index(axis) // apart) % 2).astype(jnp.int32)[None]
            self.value, sent = halve(bit, self.value, self.arrived, after, False)
            route = [(i, i ^ apart) for i in range(size)]
            self.arrived = (lax.ppermute(sent, axis, route),)
        else:
            bit = jnp.zeros((1,), jnp.int32)
            self.value = halve(bit, self.value, self.arrived, after, True)
            self.done = True
        return (self.value,)


def collect_body(failed, both, *refs, n, places, parts_count, size, pieces):
    roles = Roles(failed, n)
    parts = refs[:parts_count]
    blocks = refs[parts_count : parts_count + len(places)]
    hidden_t, outs, held, sem = refs[-4:]
    tokens, features = both.shape[0], both.shape[1] // 2
    width = outs.shape[1]

    def fetch(j, part):
        rows = pl.ds(size, pieces * tokens) if part == 0 else pl.ds(places[j], tokens)
        here = pl.ds(0, pieces * tokens) if part == 0 else pl.ds(pieces * tokens, tokens)
        return pltpu.make_async_copy(
            blocks[j].at[rows], held.at[j + 1, here], sem.at[j, part]
        )

    for j in range(len(places)):
        for part in range(2):
            fetch(j, part).start()
    for part, begin, piece, to, run in column_pieces([p.shape[1] for p in parts], width):
        units = parts[part][:, begin : begin + run]
        held[0, pl.ds(piece * tokens, tokens), pl.ds(to, run)] = jnp.where(
            roles.lost, jnp.zeros_like(units), units
        )
    slab = pl.ds(pl.multiple_of(features + roles.me * width, 128), width)
    held[0, pl.ds(pieces * tokens, tokens)] = both[:, slab]
    for j in range(len(places)):
        for part in range(2):
            fetch(j, part).wait()

    count = len(places) + 1
    for j in range(count):
        outs[pl.ds(j * tokens, tokens)] = held[j, pl.ds(pieces * tokens, tokens)]
    for piece in range(pieces):
        run = min(width, hidden_t.shape[0] - piece * width)
        rows = pl.ds(piece * tokens, tokens)
        hidden = jnp.concatenate([held[j, rows, :run] for j in range(count)], axis=0)
        hidden_t[pl.ds(piece * width, run)] = hidden.astype(F32).T.astype(BF16)


def collect(failed, n, both, parts, blocks, places, size, width, after):
    tokens = both.shape[0]
    units = sum(part.shape[1] for part in parts)
    pieces = -(-units // width)
    depth = tokens * (len(blocks) + 1)
    return pl.pallas_call(
        functools.partial(
            collect_body,
            n=n,
            places=places,
            parts_count=len(parts),
            size=size,
            pieces=pieces,
        ),
        in_specs=[SMEM]
        + [WHOLE] * (1 + len(parts))
        + [ANY] * (len(blocks) + len(after)),
        out_specs=[WHOLE, WHOLE],
        out_shape=[
            jax.ShapeDtypeStruct((units, depth), BF16),
            jax.ShapeDtypeStruct((depth, width), BF16),
        ],
        scratch_shapes=[
            pltpu.VMEM((len(blocks) + 1, (pieces + 1) * tokens, width), BF16),
            pltpu.SemaphoreType.DMA((len(blocks), 2)),
        ],
        compiler_params=PARAMS,
        cost_estimate=cost(0, 4 * depth * (units + width)),
        name="collect",
    )(failed, both, *parts, *blocks, *after)


def update_body(failed, hid_ref, out_ref, *refs, n, block, first, count, unread):
    state, news = refs[:3], refs[3 + unread : 6 + unread]
    total = refs[6 + unread]
    width = out_ref.shape[1]
    group = row_group(block)

    def step(hid, m_ref, a_ref, b_ref, m_new, a_new, b_new):
        total[...] = jnp.dot(hid[...], out_ref[...], preferred_element_type=F32)

        @pl.loop(0, block // group)
        def _(i):
            here = pl.ds(pl.multiple_of(i * group, group), group)
            m_new[here], a_new[here], b_new[here] = updated(
                m_ref[0, here], a_ref[0, here], b_ref[0, here], total[here], n - 1.0
            )

    deep = pl.Buffered(min(BUFFERS, count + 1))
    old = pl.BlockSpec(
        (1, block, width), lambda i: (0, first + i, 0), pipeline_mode=deep
    )
    new = pl.BlockSpec((block, width), lambda i: (first + i, 0))

    @pl.when(jnp.logical_not(Roles(failed, n).lost))
    def _():
        pltpu.emit_pipeline(
            step,
            grid=(count,),
            in_specs=[
                pl.BlockSpec((block, hid_ref.shape[1]), lambda i: (first + i, 0)),
                old,
                old,
                old,
            ],
            out_specs=[new] * 3,
        )(hid_ref, *state, *news)


def update(failed, n, hidden_t, outs, state, news, after, block, first, count):
    _, rows, width = state[0].shape
    depth = hidden_t.shape[1]
    shape = jax.ShapeDtypeStruct((rows, width), F32)
    unread = len(news) + len(after)
    return pl.pallas_call(
        functools.partial(
            update_body,
            n=n,
            block=block,
            first=first,
            count=count,
            unread=unread,
        ),
        in_specs=[SMEM, ANY, WHOLE] + [ANY] * (3 + unread),
        out_specs=[ANY] * 3,
        out_shape=[shape] * 3,
        scratch_shapes=[pltpu.VMEM((block, width), F32)],
        input_output_aliases={6 + k: k for k in range(len(news))},
        compiler_params=PARAMS,
        cost_estimate=cost(
            2 * count * block * width * depth,
            6 * count * block * width * 4,
            2 * count * block * width,
        ),
        name="update",
    )(failed, hidden_t, outs, *state, *news, *after)


def patch_body(failed, hid_ref, out_ref, *refs, arrivals, chunks, n, count_after):
    count = len(arrivals)
    got = refs[:count]
    rest = refs[count + 3 + count_after :]
    news = rest[:3]
    held, made, total, in_sem, out_sem = rest[3:]
    chunk = made.shape[2]
    group = row_group(chunk)
    roles = Roles(failed, n)
    ahead = roles.ahead()
    lag_of = {True: LAG * (ahead - 1), False: LAG * (n - ahead - 1)}

    def fetch(j):
        rows = got[j].at[pl.ds(0, 3 * chunk)]
        return pltpu.make_async_copy(rows, held.at[j % FETCHED], in_sem.at[j % FETCHED])

    def first_row(j):
        step, forward = arrivals[j]
        place = step - lag_of[forward]
        if not forward:
            place = chunks - 1 - place
        return pl.multiple_of(jnp.clip(place, 0, chunks - 1) * chunk, TILE)

    def store(j, k):
        return pltpu.make_async_copy(
            made.at[j % BUFFERS, k],
            news[k].at[pl.ds(first_row(j), chunk)],
            out_sem.at[j % BUFFERS, k],
        )

    def valid(j):
        step, forward = arrivals[j]
        return step >= lag_of[forward]

    def finish(j):
        @pl.when(valid(j))
        def _():
            for k in range(3):
                store(j, k).wait()

    @pl.when(roles.lost)
    def _():
        for j in range(min(FETCHED - 1, count)):
            fetch(j).start()
        for j in range(count):
            if j + FETCHED - 1 < count:
                fetch(j + FETCHED - 1).start()
            fetch(j).wait()
            if j >= BUFFERS:
                finish(j - BUFFERS)

            @pl.when(valid(j))
            def _(j=j, slot=j % FETCHED, out_slot=j % BUFFERS):
                first = first_row(j)

                units = hid_ref[pl.ds(first, chunk)]
                total[...] = jnp.dot(units, out_ref[...], preferred_element_type=F32)

                @pl.loop(0, chunk // group)
                def _(i):
                    base = pl.multiple_of(i * group, group)
                    old = [
                        held[slot, pl.ds(k * chunk + base, group)].astype(F32)
                        for k in range(3)
                    ]
                    new = updated(*old, total[pl.ds(base, group)], n - 1.0)
                    for k in range(3):
                        made[out_slot, k, pl.ds(base, group)] = new[k]

                for k in range(3):
                    store(j, k).start()

        for j in range(max(count - BUFFERS, 0), count):
            finish(j)


def patch(failed, n, hidden_t, outs, got, arrivals, news, after, chunks):
    rows, width = news[0].shape
    chunk = rows // chunks
    count = len(got)
    shape = jax.ShapeDtypeStruct((rows, width), F32)
    return pl.pallas_call(
        functools.partial(
            patch_body, arrivals=arrivals, chunks=chunks, n=n, count_after=len(after)
        ),
        in_specs=[SMEM, WHOLE, WHOLE] + [ANY] * (count + 3 + len(after)),
        out_specs=[ANY] * 3,
        out_shape=[shape] * 3,
        scratch_shapes=[
            pltpu.VMEM((FETCHED, 3 * chunk, width), BF16),
            pltpu.VMEM((BUFFERS, 3, chunk, width), F32),
            pltpu.VMEM((chunk, width), F32),
            pltpu.SemaphoreType.DMA((FETCHED,)),
            pltpu.SemaphoreType.DMA((BUFFERS, 3)),
        ],
        input_output_aliases={3 + count + k: k for k in range(3)},
        compiler_params=PARAMS,
        cost_estimate=cost(
            2 * count * chunk * width * hidden_t.shape[1],
            count * 3 * chunk * width * 6,
            2 * count * chunk * width,
        ),
        name="patch",
    )(failed, hidden_t, outs, *got, *news, *after)


def per_device(tokens, d_out, w_gate, w_up, w_down, failed, master, moment1, moment2):
    n = lax.axis_size("replica")
    _, rows, width = master.shape
    features, units = w_gate.shape

    order = ring_order(n)

    state = (master, moment1, moment2)
    chunks = largest(
        (c for c in range(2, MOST_CHUNKS + 1, 2) if rows % (TILE * c) == 0), 2
    )
    chunk = rows // chunks
    steps = (chunks + LAG * (n - 2)) // 2
    reach = (n // 2, (n - 1) // 2)
    forward = [(order[p], order[(p + 1) % n]) for p in range(n)]
    backward = [(b, a) for a, b in forward]
    sends, got = [], []
    parcel_from = None

    def send(*after, parcel=()):
        nonlocal parcel_from
        step = len(got)
        seen = got[step - LAG] if step >= LAG else ()
        here = min(step, chunks - 1)
        slabs, passed = (0, 0), (0, 0)
        if parcel:
            parcel_from, slabs = step, reach
        elif parcel_from is not None and (step - parcel_from) % LAG == 0:
            hop = (step - parcel_from) // LAG
            passed = tuple(
                seen[way].shape[0] - 3 * chunk - both.shape[0]
                if hop < reach[way]
                else 0
                for way in range(2)
            )
        sends.append(
            pack(
                failed,
                n,
                state,
                seen,
                parcel,
                after,
                (here, chunks - 1 - here),
                chunk,
                slabs,
                passed,
            )
        )
        got.append(
            (
                lax.ppermute(sends[-1][0], "replica", forward),
                lax.ppermute(sends[-1][1], "replica", backward),
            )
        )
        return (sends[-1][0],)

    sent = send()
    both = beside(tokens[0], d_out[0], sent)
    sent = send(both)
    exchanges = []
    for axis in ("tensor", "fsdp"):
        size = lax.axis_size(axis)
        exchanges += [(axis, size, 1 << k) for k in range((size - 1).bit_length())]
    if all(size & (size - 1) == 0 for _, size, _ in exchanges):
        after = sent
        for level, (axis, size, apart) in enumerate(exchanges):
            other = lax.ppermute(both, axis, [(i, i ^ apart) for i in range(size)])
            last = level == len(exchanges) - 1
            both = join(both, other, after, axis, apart, last)
            after = ()
    else:
        both = lax.all_gather(both[0], ("fsdp", "tensor"), axis=0, tiled=True)
    sent = send(both)

    tile = 128 if units % 128 == 0 else units
    hidden, d_rows = [], None
    pieces = shares(units // tile, PIECES)
    for first, count in pieces:
        part, d_rows = layer(both, w_gate, w_up, w_down, d_rows, sent, tile, first, count)
        hidden.append(part)
        last = len(hidden) == len(pieces)
        sent = send(d_rows, parcel=(both, *hidden) if last else ())
    cotangents = ScatteredSum(d_rows, ("fsdp", "tensor"))

    news = ()
    patched = 0
    hidden_t = outs = None

    def gathered(after):
        blocks, places = [], []
        for way in range(2):
            for hop in range(reach[way]):
                blocks.append(got[parcel_from + LAG * hop][way])
                places.append(blocks[-1].shape[0] - both.shape[0])
        return collect(
            failed, n, both, hidden, blocks, places, 3 * chunk, width, after
        )

    def update_part(first, count, after):
        return update(
            failed, n, hidden_t, outs, state, news, after, block, first, count
        )

    def patch_to(step, after):
        nonlocal patched
        arrivals = [(s, way) for s in range(patched, step) for way in (True, False)]
        if not arrivals:
            return news
        blocks = [b for s in range(patched, step) for b in got[s]]
        patched = step
        return patch(failed, n, hidden_t, outs, blocks, arrivals, news, after, chunks)

    block = largest((b for b in range(TILE, 193, TILE) if rows % b == 0), rows)
    blocks = rows // block
    early = blocks // 2
    ready = parcel_from + LAG * reach[0] + 1
    while len(got) < steps:
        ready_sum = len(got) > parcel_from + SUM_AFTER
        sent = send(*(cotangents.advance(sent) if ready_sum else ()), *news[:1])
        if len(got) == ready and early and len(got) < steps:
            hidden_t, outs = gathered(sent)
            news = update_part(0, early, (hidden_t,))
            news = patch_to(len(got) // 2, ())
    if hidden_t is None:
        hidden_t, outs = gathered(sent)
        early = 0
    news = update_part(early, blocks - early, sent)
    for step in (steps - 1, steps):
        news = patch_to(step, ())
    while not cotangents.done:
        cotangents.advance(sent)
    return (cotangents.value[None], *news)


def solution(mesh):
    placed = (
        P("replica", ("fsdp", "tensor"), None),
        P("replica", ("fsdp", "tensor"), None),
        P(None, ("fsdp", "tensor")),
        P(None, ("fsdp", "tensor")),
        P(("fsdp", "tensor"), None),
        P(("fsdp", "tensor")),
        P(None, ("fsdp", "tensor"), "replica"),
        P(None, ("fsdp", "tensor"), "replica"),
        P(None, ("fsdp", "tensor"), "replica"),
    )
    return jax.shard_map(
        per_device,
        mesh=mesh,
        in_specs=placed,
        out_specs=(
            P("replica", ("fsdp", "tensor"), None),
            P(("fsdp", "tensor"), "replica"),
            P(("fsdp", "tensor"), "replica"),
            P(("fsdp", "tensor"), "replica"),
        ),
        check_vma=False,
    )
```

```python
import functools

import jax
import jax.numpy as jnp
from jax import lax
from jax.experimental import pallas as pl
from jax.experimental.pallas import tpu as pltpu
from jax.sharding import PartitionSpec as P

BF16, F32 = jnp.bfloat16, jnp.float32
SUM_AFTER = 1
LAG = 2
MOST_CHUNKS = 24
TILE = 16
BUFFERS = 3
PIECES = 6
FETCHED = 4
VMEM = 50 << 20

ANY = pl.BlockSpec(memory_space=pl.ANY)
SMEM = pl.BlockSpec(memory_space=pltpu.SMEM)
WHOLE = pl.BlockSpec(memory_space=pltpu.VMEM)
PARAMS = pltpu.CompilerParams(vmem_limit_bytes=VMEM)


def ring_order(n):
    return [0, 1, 3, 2] if n == 4 else list(range(n))


def entry(table, index):
    found = jnp.int32(0)
    for at, value in enumerate(table):
        found = jnp.where(index == at, jnp.int32(value), found)
    return found


class Roles:
    def __init__(self, failed, n):
        self.n = n
        self.order = ring_order(n)
        self.spots = [self.order.index(i) for i in range(n)]
        self.me = lax.axis_index("replica").astype(jnp.int32)
        self.failed = failed[0]
        self.source = lax.rem(self.failed + 1, n)
        self.lost = self.me == self.failed

    def ahead(self):
        apart = entry(self.spots, self.failed) - entry(self.spots, self.source)
        return lax.rem(apart + self.n, self.n)

    def neighbour(self, hops):
        spot = lax.rem(entry(self.spots, self.me) + hops, self.n)
        return entry(self.order, spot)


def largest(options, default):
    options = list(options)
    return max(options) if options else default


def shares(total, parts):
    parts = min(parts, total)
    edges = [total * i // parts for i in range(parts + 1)]
    return [(a, b - a) for a, b in zip(edges, edges[1:])]


def row_group(rows):
    return largest((g for g in (16, 32) if rows % g == 0), rows)


def cost(flops, bytes_accessed, transcendentals=0):
    return pl.CostEstimate(
        flops=flops, bytes_accessed=bytes_accessed, transcendentals=transcendentals
    )


def updated(master_old, first_old, second_old, total, healthy):
    first_new = 0.9 * first_old + (0.1 / healthy) * total
    second_new = 0.95 * second_old + (0.05 / healthy**2) * (total * total)
    root = second_new * lax.rsqrt(second_new)
    step = first_new * pl.reciprocal(root + 1e-08)
    return master_old - 0.01 * step, first_new, second_new


def column_pieces(lengths, width):
    moves, column = [], 0
    for part, length in enumerate(lengths):
        begin = 0
        while begin < length:
            piece, to = divmod(column, width)
            run = min(length - begin, width - to)
            moves.append((part, begin, piece, to, run))
            begin, column = begin + run, column + run
    return moves


def pack_body(*refs, n, places, chunk, slabs, passed, counts):
    count_seen, count_parts, count_after = counts
    if count_seen:
        roles, refs = Roles(refs[0], n), refs[1:]
    state = refs[0:3]
    seen = refs[3 : 3 + count_seen]
    rest = refs[3 + count_seen :]
    if count_parts:
        both, parts, rest = rest[0], rest[1 : 1 + count_parts], rest[1 + count_parts :]
    sends = rest[count_after : count_after + 2]
    held, made, sem, out_sem, below_sem = rest[count_after + 2 :]
    width = held.shape[2]
    size = 3 * chunk

    def rows_of(j):
        way, k = divmod(j, 3)
        return way, pl.ds(k * chunk, chunk)

    def fetch(j):
        way, k = divmod(j, 3)
        rows = pl.ds(places[way] * chunk, chunk)
        return pltpu.make_async_copy(state[k].at[1, rows], held.at[j], sem.at[j])

    def take(j):
        way, rows = rows_of(j)
        return pltpu.make_async_copy(seen[way].at[rows], made.at[way, rows], sem.at[j])

    def store(j):
        way, rows = rows_of(j)
        return pltpu.make_async_copy(
            made.at[way, rows], sends[way].at[rows], out_sem.at[j]
        )

    def convert():
        for j in range(6):
            fetch(j).start()
        for j in range(6):
            way, rows = rows_of(j)
            fetch(j).wait()
            made[way, rows] = held[j].astype(BF16)
            store(j).start()
        for j in range(6):
            store(j).wait()

    def relay():
        for j in range(6):
            take(j).start()
        for j in range(6):
            take(j).wait()
            store(j).start()
        for j in range(6):
            store(j).wait()

    def below(way, inward):
        rows = pl.ds(size, passed[way] or sends[way].shape[0] - size)
        here = made.at[way, rows]
        if inward:
            return pltpu.make_async_copy(seen[way].at[rows], here, below_sem.at[way])
        return pltpu.make_async_copy(here, sends[way].at[rows], below_sem.at[way])

    for way in range(2):
        if passed[way]:
            below(way, True).start()
        if slabs[way]:
            tokens, features = both.shape[0], both.shape[1] // 2
            moves = column_pieces([part.shape[1] for part in parts], width)
            for part, begin, piece, to, run in moves:
                units = parts[part][:, begin : begin + run]
                made[way, pl.ds(size + piece * tokens, tokens), pl.ds(to, run)] = (
                    jnp.where(roles.lost, jnp.zeros_like(units), units)
                )
            row = size + (1 + moves[-1][2]) * tokens
            for far in range(slabs[way], 0, -1):
                target = roles.neighbour(far if way == 0 else n - far)
                slab = pl.ds(pl.multiple_of(features + target * width, 128), width)
                made[way, pl.ds(row, tokens)] = both[:, slab]
                row += tokens
            below(way, False).start()

    for way in range(2):
        if passed[way]:
            below(way, True).wait()
            below(way, False).start()

    if seen:
        pl.when(roles.me == roles.source)(convert)
        pl.when(roles.me != roles.source)(relay)
    else:
        convert()

    for way in range(2):
        if slabs[way] or passed[way]:
            below(way, False).wait()


def pack(failed, n, state, seen, parcel, after, places, chunk, slabs, passed):
    width = state[0].shape[2]
    extra = list(passed)
    if parcel:
        tokens = parcel[0].shape[0]
        pieces = -(-sum(part.shape[1] for part in parcel[1:]) // width)
        extra = [tokens * (pieces + count) if count else 0 for count in slabs]
    counts = (len(seen), max(len(parcel) - 1, 0), len(after))
    return pl.pallas_call(
        functools.partial(
            pack_body,
            n=n,
            places=places,
            chunk=chunk,
            slabs=slabs,
            passed=passed,
            counts=counts,
        ),
        in_specs=[SMEM] * bool(seen)
        + [ANY] * (3 + len(seen))
        + [WHOLE] * len(parcel)
        + [ANY] * len(after),
        out_specs=[ANY, ANY],
        out_shape=[
            jax.ShapeDtypeStruct((3 * chunk + more, width), BF16) for more in extra
        ],
        scratch_shapes=[
            pltpu.VMEM((6, chunk, width), F32),
            pltpu.VMEM((2, 3 * chunk + max(extra), width), BF16),
            pltpu.SemaphoreType.DMA((6,)),
            pltpu.SemaphoreType.DMA((6,)),
            pltpu.SemaphoreType.DMA((2,)),
        ],
        compiler_params=PARAMS,
        cost_estimate=cost(0, 2 * 3 * chunk * width * 6),
        name="pack",
    )(*([failed] if seen else []), *state, *seen, *parcel, *after)


def beside_body(*refs):
    tokens, d_out, out = refs[0], refs[1], refs[-1]
    width = tokens.shape[1]
    out[0, :, :width] = tokens[...]
    out[0, :, width:] = d_out[...]


def beside(tokens, d_out, after):
    rows, width = tokens.shape
    return pl.pallas_call(
        beside_body,
        in_specs=[WHOLE, WHOLE] + [ANY] * len(after),
        out_specs=WHOLE,
        out_shape=jax.ShapeDtypeStruct((1, rows, 2 * width), tokens.dtype),
        compiler_params=PARAMS,
        cost_estimate=cost(0, 4 * rows * width * 2),
        name="beside",
    )(tokens, d_out, *after)


def join_body(own, other, *refs, axis, apart, last):
    out = refs[-1]
    count, rows = own.shape[:2]
    second = lax.rem(lax.div(lax.axis_index(axis).astype(jnp.int32), apart), 2)
    if not last:
        out[pl.ds(second * count, count)] = own[...]
        out[pl.ds((1 - second) * count, count)] = other[...]
        return
    for i in range(2 * count):
        here, there = (own, other) if i < count else (other, own)
        value = jnp.where(second == 1, there[i % count], here[i % count])
        out[pl.ds(i * rows, rows)] = value


def join(own, other, after, axis, apart, last):
    count, rows, width = own.shape
    shape = (2 * count * rows, width) if last else (2 * count, rows, width)
    return pl.pallas_call(
        functools.partial(join_body, axis=axis, apart=apart, last=last),
        in_specs=[WHOLE, WHOLE] + [ANY] * len(after),
        out_specs=WHOLE,
        out_shape=jax.ShapeDtypeStruct(shape, own.dtype),
        compiler_params=PARAMS,
        cost_estimate=cost(0, 8 * count * rows * width),
        name="join",
    )(own, other, *after)


def by_rows(a, b):
    return lax.dot_general(a, b, (((1,), (1,)), ((), ())), preferred_element_type=F32)


def layer_body(both, *refs, resumed, tile, first, count):
    weights = refs[:3]
    hidden_ref, sum_ref = refs[-2:]
    features = weights[0].shape[0]
    rows = both.shape[0]
    joined = tile % 128 == 0
    sum_ref[...] = refs[3][...] if resumed else jnp.zeros_like(sum_ref)

    def step(gate_ref, up_ref, down_ref, hidden):
        x, dy = both[:, :features], both[:, features:]
        w_gate, w_up = gate_ref[...], up_ref[...]
        if joined:
            w_both = jnp.concatenate([w_gate, w_up], axis=1)
            gate_up = jnp.dot(x, w_both, preferred_element_type=F32)
            gate, up = gate_up[:, :tile], gate_up[:, tile:]
        else:
            gate = jnp.dot(x, w_gate, preferred_element_type=F32)
            up = jnp.dot(x, w_up, preferred_element_type=F32)
        d_hidden = by_rows(dy, down_ref[...])
        sig = 1.0 / (1.0 + jnp.exp(-gate))
        hidden[...] = (gate * sig * up).astype(BF16)
        d_gate = (d_hidden * up * sig * (1.0 + gate * (1.0 - sig))).astype(BF16)
        d_up = (d_hidden * gate * sig).astype(BF16)
        if joined:
            sum_ref[...] += by_rows(jnp.concatenate([d_gate, d_up], axis=1), w_both)
        else:
            sum_ref[...] += by_rows(d_gate, w_gate) + by_rows(d_up, w_up)

    deep = pl.Buffered(min(BUFFERS, count + 1))
    across = pl.BlockSpec((features, tile), lambda i: (0, first + i), pipeline_mode=deep)
    pltpu.emit_pipeline(
        step,
        grid=(count,),
        in_specs=[
            across,
            across,
            pl.BlockSpec((tile, features), lambda i: (first + i, 0), pipeline_mode=deep),
        ],
        out_specs=[pl.BlockSpec((rows, tile), lambda i: (0, i))],
    )(*weights, hidden_ref)


def layer(both, w_gate, w_up, w_down, partial_sum, after, tile, first, count):
    rows = both.shape[0]
    features = w_gate.shape[0]
    resumed = partial_sum is not None
    return pl.pallas_call(
        functools.partial(layer_body, resumed=resumed, tile=tile, first=first, count=count),
        in_specs=[WHOLE] + [ANY] * 3 + [WHOLE] * resumed + [ANY] * len(after),
        out_specs=[ANY, WHOLE],
        out_shape=[
            jax.ShapeDtypeStruct((rows, count * tile), BF16),
            jax.ShapeDtypeStruct((rows, features), F32),
        ],
        compiler_params=PARAMS,
        cost_estimate=cost(
            10 * rows * features * count * tile,
            3 * features * count * tile * 2,
            rows * count * tile,
        ),
        name="layer",
    )(both, w_gate, w_up, w_down, *([partial_sum] if resumed else []), *after)


def halve_body(bit, *refs, arrived, final):
    value = refs[0][...]
    if arrived:
        value = value + refs[1][...]
    if final:
        refs[-1][...] = value.astype(BF16)
        return
    kept, sent = refs[-2:]
    half = value.shape[0] // 2
    low, high = value[:half], value[half:]
    upper = bit[0] == 1
    kept[...] = jnp.where(upper, high, low)
    sent[...] = jnp.where(upper, low, high)


def halve(bit, value, arrived, after, final):
    rows, features = value.shape
    if final:
        out_shape = jax.ShapeDtypeStruct((rows, features), BF16)
    else:
        out_shape = [jax.ShapeDtypeStruct((rows // 2, features), F32)] * 2
    return pl.pallas_call(
        functools.partial(halve_body, arrived=bool(arrived), final=final),
        in_specs=[SMEM] + [WHOLE] * (1 + len(arrived)) + [ANY] * len(after),
        out_specs=WHOLE if final else [WHOLE, WHOLE],
        out_shape=out_shape,
        compiler_params=PARAMS,
        cost_estimate=cost(0, 3 * rows * features * 4),
        name="halve",
    )(bit, value, *arrived, *after)


class ScatteredSum:
    def __init__(self, value, axes):
        sizes = [lax.axis_size(axis) for axis in axes]
        self.value, self.arrived, self.levels = value, (), []
        self.done = any(size & (size - 1) for size in sizes)
        if self.done:
            summed = lax.psum_scatter(value, axes, scatter_dimension=0, tiled=True)
            self.value = summed.astype(BF16)
            return
        for axis, size in zip(axes, sizes):
            apart = size // 2
            while apart:
                self.levels.append((axis, size, apart))
                apart //= 2

    def advance(self, after):
        if self.done:
            return ()
        if self.levels:
            axis, size, apart = self.levels.pop(0)
            bit = ((lax.axis_index(axis) // apart) % 2).astype(jnp.int32)[None]
            self.value, sent = halve(bit, self.value, self.arrived, after, False)
            route = [(i, i ^ apart) for i in range(size)]
            self.arrived = (lax.ppermute(sent, axis, route),)
        else:
            bit = jnp.zeros((1,), jnp.int32)
            self.value = halve(bit, self.value, self.arrived, after, True)
            self.done = True
        return (self.value,)


def collect_body(failed, both, *refs, n, places, parts_count, size, pieces):
    roles = Roles(failed, n)
    parts = refs[:parts_count]
    blocks = refs[parts_count : parts_count + len(places)]
    hidden_t, outs, held, sem = refs[-4:]
    tokens, features = both.shape[0], both.shape[1] // 2
    width = outs.shape[1]

    def fetch(j, part):
        rows = pl.ds(size, pieces * tokens) if part == 0 else pl.ds(places[j], tokens)
        here = pl.ds(0, pieces * tokens) if part == 0 else pl.ds(pieces * tokens, tokens)
        return pltpu.make_async_copy(
            blocks[j].at[rows], held.at[j + 1, here], sem.at[j, part]
        )

    for j in range(len(places)):
        for part in range(2):
            fetch(j, part).start()
    for part, begin, piece, to, run in column_pieces([p.shape[1] for p in parts], width):
        units = parts[part][:, begin : begin + run]
        held[0, pl.ds(piece * tokens, tokens), pl.ds(to, run)] = jnp.where(
            roles.lost, jnp.zeros_like(units), units
        )
    slab = pl.ds(pl.multiple_of(features + roles.me * width, 128), width)
    held[0, pl.ds(pieces * tokens, tokens)] = both[:, slab]
    for j in range(len(places)):
        for part in range(2):
            fetch(j, part).wait()

    count = len(places) + 1
    for j in range(count):
        outs[pl.ds(j * tokens, tokens)] = held[j, pl.ds(pieces * tokens, tokens)]
    for piece in range(pieces):
        run = min(width, hidden_t.shape[0] - piece * width)
        rows = pl.ds(piece * tokens, tokens)
        hidden = jnp.concatenate([held[j, rows, :run] for j in range(count)], axis=0)
        hidden_t[pl.ds(piece * width, run)] = hidden.astype(F32).T.astype(BF16)


def collect(failed, n, both, parts, blocks, places, size, width, after):
    tokens = both.shape[0]
    units = sum(part.shape[1] for part in parts)
    pieces = -(-units // width)
    depth = tokens * (len(blocks) + 1)
    return pl.pallas_call(
        functools.partial(
            collect_body,
            n=n,
            places=places,
            parts_count=len(parts),
            size=size,
            pieces=pieces,
        ),
        in_specs=[SMEM]
        + [WHOLE] * (1 + len(parts))
        + [ANY] * (len(blocks) + len(after)),
        out_specs=[WHOLE, WHOLE],
        out_shape=[
            jax.ShapeDtypeStruct((units, depth), BF16),
            jax.ShapeDtypeStruct((depth, width), BF16),
        ],
        scratch_shapes=[
            pltpu.VMEM((len(blocks) + 1, (pieces + 1) * tokens, width), BF16),
            pltpu.SemaphoreType.DMA((len(blocks), 2)),
        ],
        compiler_params=PARAMS,
        cost_estimate=cost(0, 4 * depth * (units + width)),
        name="collect",
    )(failed, both, *parts, *blocks, *after)


def update_body(failed, hid_ref, out_ref, *refs, n, block, first, count, unread):
    state, news = refs[:3], refs[3 + unread : 6 + unread]
    total = refs[6 + unread]
    width = out_ref.shape[1]
    group = row_group(block)

    def step(hid, m_ref, a_ref, b_ref, m_new, a_new, b_new):
        total[...] = jnp.dot(hid[...], out_ref[...], preferred_element_type=F32)

        @pl.loop(0, block // group)
        def _(i):
            here = pl.ds(pl.multiple_of(i * group, group), group)
            m_new[here], a_new[here], b_new[here] = updated(
                m_ref[0, here], a_ref[0, here], b_ref[0, here], total[here], n - 1.0
            )

    deep = pl.Buffered(min(BUFFERS, count + 1))
    old = pl.BlockSpec(
        (1, block, width), lambda i: (0, first + i, 0), pipeline_mode=deep
    )
    new = pl.BlockSpec((block, width), lambda i: (first + i, 0))

    @pl.when(jnp.logical_not(Roles(failed, n).lost))
    def _():
        pltpu.emit_pipeline(
            step,
            grid=(count,),
            in_specs=[
                pl.BlockSpec((block, hid_ref.shape[1]), lambda i: (first + i, 0)),
                old,
                old,
                old,
            ],
            out_specs=[new] * 3,
        )(hid_ref, *state, *news)


def update(failed, n, hidden_t, outs, state, news, after, block, first, count):
    _, rows, width = state[0].shape
    depth = hidden_t.shape[1]
    shape = jax.ShapeDtypeStruct((rows, width), F32)
    unread = len(news) + len(after)
    return pl.pallas_call(
        functools.partial(
            update_body,
            n=n,
            block=block,
            first=first,
            count=count,
            unread=unread,
        ),
        in_specs=[SMEM, ANY, WHOLE] + [ANY] * (3 + unread),
        out_specs=[ANY] * 3,
        out_shape=[shape] * 3,
        scratch_shapes=[pltpu.VMEM((block, width), F32)],
        input_output_aliases={6 + k: k for k in range(len(news))},
        compiler_params=PARAMS,
        cost_estimate=cost(
            2 * count * block * width * depth,
            6 * count * block * width * 4,
            2 * count * block * width,
        ),
        name="update",
    )(failed, hidden_t, outs, *state, *news, *after)


def patch_body(failed, hid_ref, out_ref, *refs, arrivals, chunks, n, count_after):
    count = len(arrivals)
    got = refs[:count]
    rest = refs[count + 3 + count_after :]
    news = rest[:3]
    held, made, total, in_sem, out_sem = rest[3:]
    chunk = made.shape[2]
    group = row_group(chunk)
    roles = Roles(failed, n)
    ahead = roles.ahead()
    lag_of = {True: LAG * (ahead - 1), False: LAG * (n - ahead - 1)}

    def fetch(j):
        rows = got[j].at[pl.ds(0, 3 * chunk)]
        return pltpu.make_async_copy(rows, held.at[j % FETCHED], in_sem.at[j % FETCHED])

    def first_row(j):
        step, forward = arrivals[j]
        place = step - lag_of[forward]
        if not forward:
            place = chunks - 1 - place
        return pl.multiple_of(jnp.clip(place, 0, chunks - 1) * chunk, TILE)

    def store(j, k):
        return pltpu.make_async_copy(
            made.at[j % BUFFERS, k],
            news[k].at[pl.ds(first_row(j), chunk)],
            out_sem.at[j % BUFFERS, k],
        )

    def valid(j):
        step, forward = arrivals[j]
        return step >= lag_of[forward]

    def finish(j):
        @pl.when(valid(j))
        def _():
            for k in range(3):
                store(j, k).wait()

    @pl.when(roles.lost)
    def _():
        for j in range(min(FETCHED - 1, count)):
            fetch(j).start()
        for j in range(count):
            if j + FETCHED - 1 < count:
                fetch(j + FETCHED - 1).start()
            fetch(j).wait()
            if j >= BUFFERS:
                finish(j - BUFFERS)

            @pl.when(valid(j))
            def _(j=j, slot=j % FETCHED, out_slot=j % BUFFERS):
                first = first_row(j)

                units = hid_ref[pl.ds(first, chunk)]
                total[...] = jnp.dot(units, out_ref[...], preferred_element_type=F32)

                @pl.loop(0, chunk // group)
                def _(i):
                    base = pl.multiple_of(i * group, group)
                    old = [
                        held[slot, pl.ds(k * chunk + base, group)].astype(F32)
                        for k in range(3)
                    ]
                    new = updated(*old, total[pl.ds(base, group)], n - 1.0)
                    for k in range(3):
                        made[out_slot, k, pl.ds(base, group)] = new[k]

                for k in range(3):
                    store(j, k).start()

        for j in range(max(count - BUFFERS, 0), count):
            finish(j)


def patch(failed, n, hidden_t, outs, got, arrivals, news, after, chunks):
    rows, width = news[0].shape
    chunk = rows // chunks
    count = len(got)
    shape = jax.ShapeDtypeStruct((rows, width), F32)
    return pl.pallas_call(
        functools.partial(
            patch_body, arrivals=arrivals, chunks=chunks, n=n, count_after=len(after)
        ),
        in_specs=[SMEM, WHOLE, WHOLE] + [ANY] * (count + 3 + len(after)),
        out_specs=[ANY] * 3,
        out_shape=[shape] * 3,
        scratch_shapes=[
            pltpu.VMEM((FETCHED, 3 * chunk, width), BF16),
            pltpu.VMEM((BUFFERS, 3, chunk, width), F32),
            pltpu.VMEM((chunk, width), F32),
            pltpu.SemaphoreType.DMA((FETCHED,)),
            pltpu.SemaphoreType.DMA((BUFFERS, 3)),
        ],
        input_output_aliases={3 + count + k: k for k in range(3)},
        compiler_params=PARAMS,
        cost_estimate=cost(
            2 * count * chunk * width * hidden_t.shape[1],
            count * 3 * chunk * width * 6,
            2 * count * chunk * width,
        ),
        name="patch",
    )(failed, hidden_t, outs, *got, *news, *after)


def per_device(tokens, d_out, w_gate, w_up, w_down, failed, master, moment1, moment2):
    n = lax.axis_size("replica")
    _, rows, width = master.shape
    features, units = w_gate.shape

    order = ring_order(n)

    state = (master, moment1, moment2)
    chunks = largest(
        (c for c in range(2, MOST_CHUNKS + 1, 2) if rows % (TILE * c) == 0), 2
    )
    chunk = rows // chunks
    steps = (chunks + LAG * (n - 2)) // 2
    reach = (n // 2, (n - 1) // 2)
    forward = [(order[p], order[(p + 1) % n]) for p in range(n)]
    backward = [(b, a) for a, b in forward]
    sends, got = [], []
    parcel_from = None

    def send(*after, parcel=()):
        nonlocal parcel_from
        step = len(got)
        seen = got[step - LAG] if step >= LAG else ()
        here = min(step, chunks - 1)
        slabs, passed = (0, 0), (0, 0)
        if parcel:
            parcel_from, slabs = step, reach
        elif parcel_from is not None and (step - parcel_from) % LAG == 0:
            hop = (step - parcel_from) // LAG
            passed = tuple(
                seen[way].shape[0] - 3 * chunk - both.shape[0]
                if hop < reach[way]
                else 0
                for way in range(2)
            )
        sends.append(
            pack(
                failed,
                n,
                state,
                seen,
                parcel,
                after,
                (here, chunks - 1 - here),
                chunk,
                slabs,
                passed,
            )
        )
        got.append(
            (
                lax.ppermute(sends[-1][0], "replica", forward),
                lax.ppermute(sends[-1][1], "replica", backward),
            )
        )
        return (sends[-1][0],)

    sent = send()
    both = beside(tokens[0], d_out[0], sent)
    sent = send(both)
    exchanges = []
    for axis in ("tensor", "fsdp"):
        size = lax.axis_size(axis)
        exchanges += [(axis, size, 1 << k) for k in range((size - 1).bit_length())]
    if all(size & (size - 1) == 0 for _, size, _ in exchanges):
        after = sent
        for level, (axis, size, apart) in enumerate(exchanges):
            other = lax.ppermute(both, axis, [(i, i ^ apart) for i in range(size)])
            last = level == len(exchanges) - 1
            both = join(both, other, after, axis, apart, last)
            after = ()
    else:
        both = lax.all_gather(both[0], ("fsdp", "tensor"), axis=0, tiled=True)
    sent = send(both)

    tile = 128 if units % 128 == 0 else units
    hidden, d_rows = [], None
    pieces = shares(units // tile, PIECES)
    for first, count in pieces:
        part, d_rows = layer(both, w_gate, w_up, w_down, d_rows, sent, tile, first, count)
        hidden.append(part)
        last = len(hidden) == len(pieces)
        sent = send(d_rows, parcel=(both, *hidden) if last else ())
    cotangents = ScatteredSum(d_rows, ("fsdp", "tensor"))

    news = ()
    patched = 0
    hidden_t = outs = None

    def gathered(after):
        blocks, places = [], []
        for way in range(2):
            for hop in range(reach[way]):
                blocks.append(got[parcel_from + LAG * hop][way])
                places.append(blocks[-1].shape[0] - both.shape[0])
        return collect(
            failed, n, both, hidden, blocks, places, 3 * chunk, width, after
        )

    def update_part(first, count, after):
        return update(
            failed, n, hidden_t, outs, state, news, after, block, first, count
        )

    def patch_to(step, after):
        nonlocal patched
        arrivals = [(s, way) for s in range(patched, step) for way in (True, False)]
        if not arrivals:
            return news
        blocks = [b for s in range(patched, step) for b in got[s]]
        patched = step
        return patch(failed, n, hidden_t, outs, blocks, arrivals, news, after, chunks)

    block = largest((b for b in range(TILE, 193, TILE) if rows % b == 0), rows)
    blocks = rows // block
    early = 5 * blocks // 12
    ready = parcel_from + LAG * reach[0] + 1
    while len(got) < steps:
        ready_sum = len(got) > parcel_from + SUM_AFTER
        sent = send(*(cotangents.advance(sent) if ready_sum else ()), *news[:1])
        if len(got) == ready and early and len(got) < steps:
            hidden_t, outs = gathered(sent)
            news = update_part(0, early, (hidden_t,))
            news = patch_to(len(got) // 2 + 1, ())
    if hidden_t is None:
        hidden_t, outs = gathered(sent)
        early = 0
    news = update_part(early, blocks - early, sent)
    for step in (steps - 1, steps):
        news = patch_to(step, ())
    while not cotangents.done:
        cotangents.advance(sent)
    return (cotangents.value[None], *news)


def solution(mesh):
    placed = (
        P("replica", ("fsdp", "tensor"), None),
        P("replica", ("fsdp", "tensor"), None),
        P(None, ("fsdp", "tensor")),
        P(None, ("fsdp", "tensor")),
        P(("fsdp", "tensor"), None),
        P(("fsdp", "tensor")),
        P(None, ("fsdp", "tensor"), "replica"),
        P(None, ("fsdp", "tensor"), "replica"),
        P(None, ("fsdp", "tensor"), "replica"),
    )
    return jax.shard_map(
        per_device,
        mesh=mesh,
        in_specs=placed,
        out_specs=(
            P("replica", ("fsdp", "tensor"), None),
            P(("fsdp", "tensor"), "replica"),
            P(("fsdp", "tensor"), "replica"),
            P(("fsdp", "tensor"), "replica"),
        ),
        check_vma=False,
    )
```
